32 devices in a mesh: dp: 8 (over z, x), fsdp: 4 (over y, core).
Axes of the slice: x: 2, y: 2, z: 4, core: 2. Of those that a mesh axis runs over, the one named last changes fastest.
Arguments:
- block_in: bfloat16 [160, 185, 768], P(('dp', 'fsdp')), may hold values from -6 to 6
- out_grad: bfloat16 [160, 185, 768], P(('dp', 'fsdp')), may hold values from -8 to 8
- caption_len: int32 [160], P(('dp', 'fsdp')), may hold values from 4 to 40, as said below
- mask_marks: int32 [160, 40], P(('dp', 'fsdp')), may hold values 0 or 1
- qkv_weight: float32 [768, 2304], P('fsdp'), may hold values from -0.21875 to 0.21875
- out_weight: float32 [768, 768], P(None, 'fsdp'), may hold values from -1.75 to 1.75
- up_weight: float32 [768, 3072], P('fsdp'), may hold values from -0.21875 to 0.21875
- down_weight: float32 [3072, 768], P(None, 'fsdp'), may hold values from -0.109375 to 0.109375
- vector_params: float32 [13, 768], P(None, 'fsdp'), may hold values from -6 to 6
- qkv_first: float32 [768, 2304], P('fsdp'), may hold values from -688.18604 to 688.18604
- qkv_second: float32 [768, 2304], P('fsdp'), may hold values from 24272 to 97680
- out_first: float32 [768, 768], P(None, 'fsdp'), may hold values from -123.87348 to 123.87348
- out_second: float32 [768, 768], P(None, 'fsdp'), may hold values from 799.2 to 3167.2
- up_first: float32 [768, 3072], P('fsdp'), may hold values from -240.86511 to 240.86511
- up_second: float32 [768, 3072], P('fsdp'), may hold values from 2960 to 11840
- down_first: float32 [3072, 768], P(None, 'fsdp'), may hold values from -481.73022 to 481.73022
- down_second: float32 [3072, 768], P(None, 'fsdp'), may hold values from 11840 to 47360
- vector_first: float32 [13, 768], P(None, 'fsdp'), may hold values from -1204.32554 to 1204.32554
- vector_second: float32 [13, 768], P(None, 'fsdp'), may hold values from 888 to 296000
Outputs:
- block_out: bfloat16 [160, 185, 768], P(('dp', 'fsdp'))
- input_grad: float32 [160, 185, 768], P(('dp', 'fsdp'))
- qkv_new: float32 [768, 2304], P('fsdp')
- out_new: float32 [768, 768], P(None, 'fsdp')
- up_new: float32 [768, 3072], P('fsdp')
- down_new: float32 [3072, 768], P(None, 'fsdp')
- vector_new: float32 [13, 768], P(None, 'fsdp')
- qkv_first_new: float32 [768, 2304], P('fsdp')
- qkv_second_new: float32 [768, 2304], P('fsdp')
- out_first_new: float32 [768, 768], P(None, 'fsdp')
- out_second_new: float32 [768, 768], P(None, 'fsdp')
- up_first_new: float32 [768, 3072], P('fsdp')
- up_second_new: float32 [768, 3072], P('fsdp')
- down_first_new: float32 [3072, 768], P(None, 'fsdp')
- down_second_new: float32 [3072, 768], P(None, 'fsdp')
- vector_first_new: float32 [13, 768], P(None, 'fsdp')
- vector_second_new: float32 [13, 768], P(None, 'fsdp')
- matrix_norms: float32 [2, 4], replicated
The draws below stay inside these ranges and needn't reach their ends.
Inputs may be any that keep to these rules, and one draw needn't show every extreme that they name: `caption_len`: caption positions from an item's length on are padding; on every device of dp+fsdp one of its 5 items has the full 40.
All inputs are finite; a program needn't handle non-finite values. No bound on the sum of `mask_marks` on one device may be relied on, other than what follows from the above.
Results may differ from the reference program's by a relative error of at most 0.018.
The reference program's roundings to bfloat16 on the way count: a program that leaves them out, or rounds other values in their place, can miss the bound.
Values may be sent and summed in bfloat16 or wider, within the bound.
No kernel may reach another device: no remote copies, remote signals or barrier semaphores. Data moves between devices by JAX's collectives and lax.ppermute only.
A program may use at most 192 MiB of HBM per device.

```python
import math
import jax
import jax.numpy as jnp
from jax import lax

D = 768
FF = 3072
HEAD = 64
TXT = 40
PATCH = 145
STEP = 7
ITEMS_DEV = 5
ITEMS = 160
TOKENS = 29600
N_FSDP = 4


row_scales = [1.7, 1.7, 1.0, 1.0, 1.5, 0.6, 0.6, 1.2, 0.3, 0.3, 0.3, 0.3, 0.2]


def rising(lowest, factor):
    places = jnp.arange(D, dtype=jnp.float32) / (D - 1)
    return lowest * jnp.exp(places * math.log(factor))


def vector_scale():
    return jnp.array(row_scales, dtype=jnp.float32)[:, None] * TOKENS ** 0.5


def draw_out_grad(key, part):
    key = jax.random.fold_in(key, 5)
    base = jnp.clip(jax.random.normal(key, (ITEMS, TXT + PATCH, D), jnp.float32), -4.0, 4.0)
    ramp = rising(0.6, 3.0)
    return jnp.clip(base * ramp, -8.0, 8.0).astype(jnp.bfloat16)


def draw_caption_len(key, part):
    key = jax.random.fold_in(key, 7)
    key_one, key_two, key_three = jax.random.split(key, 3)
    spread = TXT - 4
    first = jax.random.randint(key_one, (ITEMS,), 0, spread + 1)
    second = jax.random.randint(key_two, (ITEMS,), 0, spread + 1)
    lengths = 4 + first * second // spread
    full = jax.random.randint(key_three, (ITEMS // ITEMS_DEV, 1), 0, ITEMS_DEV)
    slots = jnp.arange(ITEMS_DEV, dtype=jnp.int32)[None, :]
    lengths = jnp.where((slots == full).reshape(ITEMS), TXT, lengths)
    return lengths.astype(jnp.int32)


def draw_vector_params(key, part):
    key = jax.random.fold_in(key, 11)
    key_one, key_two, key_three = jax.random.split(key, 3)
    ramp = rising(0.6, 3.0)
    rough = jax.random.uniform(key_one, (2, D), jnp.float32, 0.7, 1.3)
    gains = ramp[None, :] * rough
    shifts = 0.2 * jax.random.normal(key_two, (13, D), jnp.float32)
    embed = jax.random.normal(key_three, (D,), jnp.float32)
    rows = [gains[0], shifts[1], shifts[2], shifts[3], shifts[4], gains[1], shifts[6], shifts[7], shifts[8], shifts[9], shifts[10], shifts[11], embed]
    return jnp.clip(jnp.stack(rows), -6.0, 6.0)


def draw_vector_first(key, part):
    key = jax.random.fold_in(key, 13)
    base = jnp.clip(jax.random.normal(key, (13, D), jnp.float32), -4.0, 4.0)
    return base * vector_scale()


def draw_vector_second(key, part):
    key = jax.random.fold_in(key, 17)
    factor = jnp.exp(jax.random.uniform(key, (13, D), jnp.float32, 0.0, math.log(4.0)))
    scale = vector_scale()
    return 0.82 * scale * scale * factor


def touch_ends(values, rng, low, high):
    dims = values.shape
    place = [jax.random.randint(jax.random.fold_in(rng, axis), (), 0, dims[axis]) for axis in range(len(dims))]
    values = values.at[tuple(place)].set(low)
    longest = dims.index(max(dims))
    place[longest] = (place[longest] + 1) % dims[longest]
    return values.at[tuple(place)].set(high)


def steps_of(key, shape, cuts, least, high):
    factor_of = 1.0
    for position, blocks in cuts:
        steps = jax.random.uniform(jax.random.fold_in(jax.random.fold_in(key, 6), position), (blocks,), jnp.float32, least / len(cuts), high / len(cuts))
        factor_of = factor_of * jnp.repeat(jnp.exp(steps), shape[position] // blocks).reshape((-1,) + (1,) * (len(shape) - 1 - position))
    return factor_of


def scatter_about(rng, shape, scale, limit, cuts=(), held_as=jnp.bfloat16):
    values = scale * jax.random.normal(rng, shape, jnp.float32)
    if cuts:
        values = values * steps_of(rng, shape, cuts, -0.22, 0.18)
    return jnp.clip(values, -limit, limit).astype(held_as)


def setup_inputs(seed: int = 0) -> dict:
    seeds = jax.random.split(jax.random.key(seed), 20)
    return {
        "block_in": scatter_about(seeds[0], (ITEMS, TXT + PATCH, D), 1.0, 6.0, ((0, 32),)),
        "out_grad": draw_out_grad(jax.random.fold_in(seeds[19], 71), 0),
        "caption_len": draw_caption_len(jax.random.fold_in(seeds[19], 71), 0),
        "mask_marks": touch_ends((jax.random.randint(seeds[3], (ITEMS, TXT), 0, 20) < 3).astype(jnp.int32), jax.random.fold_in(seeds[3], 1), 0, 1),
        "qkv_weight": scatter_about(seeds[4], (D, 3 * D), D ** -0.5, 0.21875, ((0, 4),), jnp.float32),
        "out_weight": scatter_about(seeds[5], (D, D), (3 * D // (TXT + PATCH)) ** -0.5, 1.75, ((1, 4),), jnp.float32),
        "up_weight": scatter_about(seeds[6], (D, FF), D ** -0.5, 0.21875, ((0, 4),), jnp.float32),
        "down_weight": scatter_about(seeds[7], (FF, D), FF ** -0.5, 0.109375, ((1, 4),), jnp.float32),
        "vector_params": draw_vector_params(jax.random.fold_in(seeds[19], 71), 0),
        "qkv_first": scatter_about(seeds[9], (D, 3 * D), (TOKENS ** 0.5), 688.18604, ((0, 4),), jnp.float32),
        "qkv_second": jnp.clip(jnp.exp(math.log(97680.0) - 1.3923734 * jax.random.uniform(seeds[10], (D, 3 * D), jnp.float32) ** steps_of(seeds[10], (D, 3 * D), ((0, 4),), -0.2, 0.2)), 24272.0, 97680.0),
        "out_first": scatter_about(seeds[11], (D, D), (0.18 * TOKENS ** 0.5), 123.87348, ((1, 4),), jnp.float32),
        "out_second": jnp.clip(jnp.exp(math.log(3167.2) - 1.376992 * jax.random.uniform(seeds[12], (D, D), jnp.float32) ** steps_of(seeds[12], (D, D), ((1, 4),), -0.2, 0.2)), 799.2, 3167.2),
        "up_first": scatter_about(seeds[13], (D, FF), (0.35 * TOKENS ** 0.5), 240.86511, ((0, 4),), jnp.float32),
        "up_second": jnp.clip(jnp.exp(math.log(11840.0) - 1.3862944 * jax.random.uniform(seeds[14], (D, FF), jnp.float32) ** steps_of(seeds[14], (D, FF), ((0, 4),), -0.2, 0.2)), 2960.0, 11840.0),
        "down_first": scatter_about(seeds[15], (FF, D), (0.7 * TOKENS ** 0.5), 481.73022, ((1, 4),), jnp.float32),
        "down_second": jnp.clip(jnp.exp(math.log(47360.0) - 1.3862944 * jax.random.uniform(seeds[16], (FF, D), jnp.float32) ** steps_of(seeds[16], (FF, D), ((1, 4),), -0.2, 0.2)), 11840.0, 47360.0),
        "vector_first": draw_vector_first(jax.random.fold_in(seeds[19], 71), 0),
        "vector_second": draw_vector_second(jax.random.fold_in(seeds[19], 71), 0),
    }


ln_eps = 1e-06
beta_one = 0.5
beta_two = 0.55
adam_eps = 1e-06
decay_rate = 0.01
matrix_rate = 0.5
vector_rate = 0.3
highest = lax.Precision.HIGHEST

@jax.custom_vjp
def low(v):
    return lax.optimization_barrier(v.astype(jnp.bfloat16)).astype(jnp.float32)

@jax.custom_vjp
def low_back(v):
    return v

def low_keep(v):
    return (low(v), None)

def low_pass(kept, grad):
    return (grad,)

def back_keep(v):
    return (v, None)

def back_low(kept, grad):
    return (low(grad),)
low.defvjp(low_keep, low_pass)
low_back.defvjp(back_keep, back_low)

def masks_for(lengths, marks):
    places = jnp.arange(TXT + PATCH, dtype=jnp.int32)
    key_valid = (places[None, :] >= TXT) | (places[None, :] < lengths[:, None])
    text_places = jnp.arange(TXT, dtype=jnp.int32)
    live = (marks == 1) & (text_places[None, :] >= 1) & (text_places[None, :] < lengths[:, None])
    chosen = jnp.concatenate([live, jnp.zeros((lengths.shape[0], PATCH), dtype=bool)], axis=1)
    return (key_valid, chosen)

def norm_rows(rows, gain, shift):
    centred = rows - lax.optimization_barrier(jnp.mean(rows, axis=-1, keepdims=True))
    return centred * lax.rsqrt(lax.optimization_barrier(jnp.mean(centred * centred, axis=-1, keepdims=True)) + ln_eps) * gain + shift

def block(start, key_valid, params):
    qkv_weight, out_weight, up_weight, down_weight, vectors = params
    n_items, seq_len, width = start.shape
    heads = width // HEAD
    flat = start.reshape(n_items * seq_len, width)
    normed = low(norm_rows(flat, vectors[0], vectors[1]))
    bias = jnp.concatenate([vectors[2], jnp.zeros_like(vectors[2]), vectors[3]])
    mixed = (jnp.dot(normed, qkv_weight, precision=highest) + bias).reshape(n_items, seq_len, 3, heads, HEAD)
    queries = low(low_back(mixed[:, :, 0]))
    keys_all = low(low_back(mixed[:, :, 1]))
    values_all = low(low_back(mixed[:, :, 2]))
    scores = jnp.einsum('nqhe,nkhe->nhqk', queries, keys_all, precision=highest) * HEAD ** (-0.5)
    scores = low_back(jnp.where(key_valid[:, None, None, :], scores, -1000000000.0))
    shifted = scores - lax.optimization_barrier(jnp.max(scores, axis=-1, keepdims=True))
    expd = jnp.exp(shifted)
    probs = low(expd / lax.optimization_barrier(jnp.sum(expd, axis=-1, keepdims=True)))
    attended = low(low_back(jnp.einsum('nhqk,nkhe->nqhe', probs, values_all, precision=highest)))
    attended = attended.reshape(n_items * seq_len, width)
    middle = flat + low_back(jnp.dot(attended, out_weight, precision=highest) + vectors[4])
    normed_two = low(norm_rows(middle, vectors[5], vectors[6]))
    hidden = low_back(jnp.dot(normed_two, up_weight, precision=highest) + vectors[8:12].reshape(-1))
    activated = low(jax.nn.gelu(hidden, approximate=False))
    result = middle + low_back(jnp.dot(activated, down_weight, precision=highest) + vectors[7])
    return result.reshape(n_items, seq_len, width)

def adam_moments(grad, first, second):
    first_new = beta_one * first + (1.0 - beta_one) * grad
    second_new = beta_two * second + (1.0 - beta_two) * grad * grad
    direction = first_new / (1.0 - beta_one ** STEP) / (jnp.sqrt(second_new / (1.0 - beta_two ** STEP)) + adam_eps)
    return (first_new, second_new, direction)

def reference(block_in, out_grad, caption_len, mask_marks, qkv_weight, out_weight, up_weight, down_weight, vector_params, qkv_first, qkv_second, out_first, out_second, up_first, up_second, down_first, down_second, vector_first, vector_second):
    seq_len = TXT + PATCH
    group = ITEMS_DEV * N_FSDP
    group_count = ITEMS // group
    masters = (qkv_weight, out_weight, up_weight, down_weight, vector_params)
    pieces = (block_in.reshape(group_count, group, seq_len, D), out_grad.reshape(group_count, group, seq_len, D), caption_len.reshape(group_count, group), mask_marks.reshape(group_count, group, TXT))

    def one_group(totals, piece):
        inputs, grads_out, lengths, marks = piece
        key_valid, chosen = masks_for(lengths, marks)

        def run(start_raw, params):
            rounded = tuple((low(param) for param in params))
            start = jnp.where(chosen[:, :, None], rounded[4][12][None, None, :], start_raw)
            return block(start, key_valid, rounded)
        result, pullback = jax.vjp(run, inputs.astype(jnp.float32), masters)
        grad_start, param_grads = pullback(grads_out.astype(jnp.float32))
        totals = tuple((left + right for left, right in zip(totals, param_grads)))
        return (totals, (result.astype(jnp.bfloat16), grad_start))
    zeros_init = tuple((jnp.zeros_like(param) for param in masters))
    grads, (outputs, input_grads) = lax.scan(one_group, zeros_init, pieces)
    firsts = (qkv_first, out_first, up_first, down_first, vector_first)
    seconds = (qkv_second, out_second, up_second, down_second, vector_second)
    moved = [adam_moments(grads[index], firsts[index], seconds[index]) for index in range(5)]
    new_params = []
    weight_norms = []
    update_norms = []
    for index in range(4):
        update = moved[index][2] + decay_rate * masters[index]
        weight_sq = jnp.sum(masters[index] * masters[index])
        update_sq = jnp.sum(update * update)
        new_params.append(masters[index] - matrix_rate * jnp.sqrt(weight_sq) * lax.rsqrt(update_sq + adam_eps) * update)
        weight_norms.append(jnp.sqrt(weight_sq))
        update_norms.append(jnp.sqrt(update_sq))
    vector_new = vector_params - vector_rate * moved[4][2]
    matrix_norms = jnp.stack([jnp.stack(weight_norms), jnp.stack(update_norms)])
    return (outputs.reshape(ITEMS, seq_len, D), input_grads.reshape(ITEMS, seq_len, D), new_params[0], new_params[1], new_params[2], new_params[3], vector_new, moved[0][0], moved[0][1], moved[1][0], moved[1][1], moved[2][0], moved[2][1], moved[3][0], moved[3][1], moved[4][0], moved[4][1], matrix_norms)
```

```python
import functools

import jax
import jax.numpy as jnp
from jax import lax
from jax.experimental import pallas as pl
from jax.experimental.pallas import tpu as pltpu
from jax.sharding import PartitionSpec as P

HEAD = 64
TXT = 40
PATCH = 145
STEP = 7
SEQ = TXT + PATCH
PAD = 192
GROUP = 4
PARTS = 2
TILE = 256

ln_eps = 1e-06
beta_one = 0.5
beta_two = 0.55
adam_eps = 1e-06
decay_rate = 0.01
matrix_rate = 0.5
vector_rate = 0.3

f32 = jnp.float32
bf16 = jnp.bfloat16
ORDER = (0, 2, 1, 3)
NT = (((1,), (1,)), ((), ()))
TN = (((0,), (0,)), ((), ()))

VM = pl.BlockSpec(memory_space=pltpu.VMEM)
SM = pl.BlockSpec(memory_space=pltpu.SMEM)


def dot(left, right, dims=None):
    if dims is None:
        return jnp.dot(left, right, preferred_element_type=f32)
    return lax.dot_general(left, right, dims, preferred_element_type=f32)


def call(body, grid, ins, outs, scratch, limit, args, name, after=(), aliases=None, flops=10**12):
    count = len(ins)

    def run(*refs):
        body(*refs[:count], *refs[count + len(after) :])

    return pl.pallas_call(
        run,
        grid=grid or (),
        in_specs=list(ins) + [pl.BlockSpec(memory_space=pl.ANY)] * len(after),
        out_specs=[o[1] for o in outs],
        out_shape=[o[0] for o in outs],
        input_output_aliases=aliases or {},
        scratch_shapes=scratch,
        compiler_params=pltpu.CompilerParams(vmem_limit_bytes=limit << 20),
        cost_estimate=pl.CostEstimate(flops=flops, bytes_accessed=flops // 100, transcendentals=0),
        name=name,
    )(*args, *after)


def far_mem(shape, dtype):
    return pltpu.HBM(tuple(shape), dtype)


def tie(value, *deps):
    return pl.pallas_call(
        lambda *refs: None,
        in_specs=[pl.BlockSpec(memory_space=pl.ANY)] * (1 + len(deps)),
        out_specs=pl.BlockSpec(memory_space=pl.ANY),
        out_shape=jax.ShapeDtypeStruct(value.shape, value.dtype),
        input_output_aliases={0: 0},
        name="tie",
    )(value, *deps)


def whole(shape):
    return pl.BlockSpec(shape, lambda i: (0,) * len(shape), pipeline_mode=pl.Buffered(1))


def shard_specs(shards, wide, columns):
    specs = [pl.BlockSpec((v.shape[0], wide), lambda i, at=at: (0, at + columns(i))) for v, at in shards]
    return specs, [v for v, _ in shards]


def unit_rows(rows):
    centred = rows - jnp.mean(rows, axis=-1, keepdims=True)
    factor = lax.rsqrt(jnp.mean(centred * centred, axis=-1, keepdims=True) + ln_eps)
    return centred * factor, factor


def unit_back(grad_normed, unit, factor, gain):
    grad_unit = grad_normed * gain
    return factor * (
        grad_unit
        - jnp.mean(grad_unit, axis=-1, keepdims=True)
        - unit * jnp.mean(grad_unit * unit, axis=-1, keepdims=True)
    )


def put_turned(who_ref, value, scratch, out_ref):
    rows = out_ref.shape[0] // 4
    scratch[...] = value.T
    for place, other in enumerate(ORDER):
        start = pl.multiple_of((who_ref[0] ^ other) * rows, 64)
        out_ref[place * rows : (place + 1) * rows, :] = scratch[pl.ds(start, rows), :]


def gather_rows(who_ref, refs, out_ref):
    rows = refs[0].shape[0]
    half = rows // 2
    places = [(0, None), (1, None)]
    places += [(2, None), (3, None)] if len(refs) == 4 else [(2, 0), (2, 1), (3, 0), (3, 1)]
    for (other, part), ref in zip(places, refs):
        start = (who_ref[0] ^ other) * rows
        if part is not None:
            start += (who_ref[1] ^ part) * half
        out_ref[pl.ds(pl.multiple_of(start, 32), ref.shape[0]), :] = ref[...]


def cast_heads_body(w_ref, *outs):
    wide = GROUP * HEAD
    width = w_ref.shape[1] // 3
    for group, out in enumerate(outs):
        for kind in range(3):
            at = kind * width + group * wide
            out[:, kind * wide : (kind + 1) * wide] = w_ref[:, at : at + wide].astype(bf16)


def cast_heads(weight):
    rows, cols = weight.shape
    groups = cols // (3 * GROUP * HEAD)
    out = jax.ShapeDtypeStruct((rows, cols // groups), bf16)
    return call(cast_heads_body, None, [VM], [(out, VM)] * groups, [], 8, (weight,), "cast_heads")


def cast_rest_body(who, out_ref, up_ref, down_ref, o_ref, up_half, down_half, *parts):
    o_ref[...] = out_ref[...].astype(bf16)
    cols = parts[0].shape[1] // 2
    for part, ref in enumerate(parts):
        ref[:, :cols] = up_ref[:, part * cols : (part + 1) * cols].astype(bf16)
        ref[:, cols:] = down_ref[:, part * cols : (part + 1) * cols].astype(bf16)
    half = up_half.shape[0]
    rows = pl.ds(pl.multiple_of(who[1] * half, 32), half)
    up_half[...] = up_ref[rows, :cols].astype(bf16)
    down_half[...] = down_ref[rows, :cols].astype(bf16)


def cast_rest(who, out_t, up, down_t, after):
    rows, hidden = up.shape
    cols = hidden // PARTS
    shapes = [(rows, out_t.shape[1]), (rows // 2, cols), (rows // 2, cols)] + [(rows, 2 * cols)] * PARTS
    outs = [(jax.ShapeDtypeStruct(shape, bf16), VM) for shape in shapes]
    return call(cast_rest_body, None, [SM, VM, VM, VM], outs, [], 8, (who, out_t, up, down_t), "cast_rest", after)


def chosen_rows(mark_ref, length, item):
    marks = mark_ref[:, item : item + 1]
    places = lax.broadcasted_iota(jnp.int32, marks.shape, 0)
    return jnp.where((marks == 1) & (places >= 1) & (places < length), 1.0, 0.0)


def spread_rows(chosen, width):
    return jnp.broadcast_to(chosen, (chosen.shape[0], width)) > 0


def prep_body(who, len_ref, x_ref, g_ref, mark_ref, v0, v1, v2, v3, vec_ref, xb_ref, a_ref, at_ref, dm_ref, dmt_ref, bd_ref, scratch, scratch_two):
    items, _, width = x_ref.shape
    rows, cols = v0.shape
    vec_ref[...] = jnp.zeros_like(vec_ref)
    for block in range(4):
        value = v0[...].astype(f32)
        for other, ref in ((1, v1), (2, v2), (3, v3)):
            value = jnp.where((who[0] ^ other) == block, ref[...].astype(f32), value)
        vec_ref[:rows, block * cols : (block + 1) * cols] = value
    gain, shift, embed = vec_ref[0:1, :], vec_ref[1:2, :], vec_ref[12:13, :]
    tail = jnp.zeros((PAD - SEQ, width), f32)
    for item in range(items):
        rows = slice(item * PAD, (item + 1) * PAD)
        x = x_ref[item].astype(f32)
        marked = spread_rows(chosen_rows(mark_ref, len_ref[item], item), width)
        x = jnp.concatenate([jnp.where(marked, embed, x[:TXT]), x[TXT:], tail], axis=0)
        xb_ref[rows, :] = x.astype(bf16)
        unit, _ = unit_rows(x)
        a_ref[rows, :] = (unit * gain + shift).astype(bf16)
        dm_ref[rows, :] = jnp.concatenate([g_ref[item].astype(f32), tail], axis=0).astype(bf16)
    bd_ref[...] = jnp.sum(dm_ref[...].astype(f32), axis=0, keepdims=True)
    put_turned(who, a_ref[...], scratch, at_ref)
    put_turned(who, dm_ref[...], scratch_two, dmt_ref)


def prep(who, lengths, block_in, out_grad, marks_t, vec_shards):
    items, _, width = block_in.shape
    rows = items * PAD
    near = jax.ShapeDtypeStruct((rows, width), bf16)
    flat, turned = far_mem((rows, width), bf16), far_mem((width, rows), bf16)
    return call(
        prep_body,
        None,
        [SM, SM, VM, VM, VM, VM, VM, VM, VM],
        [
            (jax.ShapeDtypeStruct((16, width), f32), VM),
            (flat, VM),
            (near, VM),
            (turned, VM),
            (flat, VM),
            (turned, VM),
            (jax.ShapeDtypeStruct((1, width), f32), VM),
        ],
        [pltpu.VMEM((width, rows), bf16)] * 2,
        20,
        (who, lengths, block_in, out_grad, marks_t, *vec_shards),
        "prep",
    )


def key_mask(length):
    places = lax.broadcasted_iota(jnp.int32, (PAD, 1), 0)
    return ((places >= TXT) & (places < SEQ)) | (places < length)


def half_masks():
    lanes = lax.broadcasted_iota(jnp.int32, (1, 2 * HEAD), 1)
    low = jnp.where(lanes < HEAD, 1.0, 0.0)
    return low.astype(bf16), (1.0 - low).astype(bf16)


def attend_body(group, who, len_ref, a_ref, vec_ref, *rest):
    wide = GROUP * HEAD
    shards, (qkv_ref, o_ref, st_ref, w_ref) = rest[:-4], rest[-4:]
    gather_rows(who, shards, w_ref)
    cols = slice(group * wide, (group + 1) * wide)
    bias = jnp.concatenate([vec_ref[2:3, cols], jnp.zeros((1, wide), f32), vec_ref[3:4, cols]], axis=1)
    qkv_ref[...] = (dot(a_ref[...], w_ref[...]) + bias).astype(bf16)
    halves = half_masks()

    @pl.loop(0, len_ref.shape[0])
    def _(item):
        rows = pl.ds(pl.multiple_of(item * PAD, PAD), PAD)
        valid = key_mask(len_ref[item])
        for pair in range(GROUP // 2):
            at = pair * 2 * HEAD
            q = qkv_ref[rows, at : at + 2 * HEAD]
            k = qkv_ref[rows, wide + at : wide + at + 2 * HEAD]
            v = qkv_ref[rows, 2 * wide + at : 2 * wide + at + 2 * HEAD]
            out = None
            for half in range(2):
                s = dot(k * halves[half], q, NT) * HEAD ** (-0.5)
                s = jnp.where(valid, s, -1000000000.0)
                top = jnp.max(s, axis=0, keepdims=True)
                e = jnp.exp(s - top)
                scale = 1.0 / jnp.sum(e, axis=0, keepdims=True)
                p = (e * scale).astype(bf16)
                part = dot(p, v * halves[half], TN)
                out = part if out is None else out + part
                head = 2 * pair + half
                st_ref[item, head : head + 1, :] = top
                st_ref[item, GROUP + head : GROUP + head + 1, :] = scale
            o_ref[rows, at : at + 2 * HEAD] = out.astype(bf16)


def attend(who, lengths, a, weights, vecs, group, after):
    rows, width = a.shape
    wide = GROUP * HEAD
    items = lengths.shape[0]
    specs, arrays = shard_specs(weights, 3 * wide, lambda i: 0)
    return call(
        functools.partial(attend_body, group),
        (1,),
        [SM, SM, whole(a.shape), whole(vecs.shape)] + specs,
        [
            (far_mem((rows, 3 * wide), bf16), whole((rows, 3 * wide))),
            (jax.ShapeDtypeStruct((rows, wide), bf16), whole((rows, wide))),
            (far_mem((items, 2 * GROUP, PAD), f32), whole((items, 2 * GROUP, PAD))),
        ],
        [pltpu.VMEM((width, 3 * wide), bf16)],
        16,
        (who, lengths, a, vecs, *arrays),
        "attend",
        after,
    )


def mix_body(who, x_ref, o0, o1, o2, vec_ref, *rest):
    shards, (y_ref, c_ref, ct_ref, w_ref, scratch) = rest[:-5], rest[-5:]
    gather_rows(who, shards, w_ref)
    wide = GROUP * HEAD
    acc = x_ref[...].astype(f32) + vec_ref[4:5, :]
    for group, o in enumerate((o0, o1, o2)):
        acc += dot(o[...], w_ref[:, group * wide : (group + 1) * wide], NT)
    y_ref[...] = acc
    unit, _ = unit_rows(acc)
    c_ref[...] = (unit * vec_ref[5:6, :] + vec_ref[6:7, :]).astype(bf16)
    put_turned(who, c_ref[...], scratch, ct_ref)


def mix(who, xb, outs, weights, vecs, after):
    rows, width = xb.shape
    specs, arrays = shard_specs(weights, width, lambda i: 0)
    return call(
        mix_body,
        (1,),
        [SM, whole(xb.shape)] + [whole(o.shape) for o in outs] + [whole(vecs.shape)] + specs,
        [
            (far_mem((rows, width), f32), whole((rows, width))),
            (jax.ShapeDtypeStruct((rows, width), bf16), whole((rows, width))),
            (jax.ShapeDtypeStruct((width, rows), bf16), whole((width, rows))),
        ],
        [pltpu.VMEM((width, width), bf16), pltpu.VMEM((width, rows), bf16)],
        18,
        (who, xb, *outs, vecs, *arrays),
        "mix",
        after,
    )


def gelu_pair(h):
    bell = jnp.exp(-0.5 * h * h)
    t = 1.0 / (1.0 + (0.3275911 * 0.7071067811865476) * jnp.abs(h))
    poly = t * (0.127414796 + t * (-0.142248368 + t * (0.7107068705 + t * (-0.7265760135 + t * 0.5307027145))))
    tail = poly * bell
    return jnp.where(h < 0, tail, 1.0 - tail), bell


def ffn_body(first, counts, base, who, c_ref, dm_ref, ct_ref, dmt_ref, *rest):
    ups, downs, rest = rest[: counts[0]], rest[counts[0] : sum(counts)], rest[sum(counts) :]
    if first:
        bu_ref, gk_ref, gs_ref, gelu_ref, gbu_ref, dc_ref, up_w, down_w = rest
    else:
        bu_ref, dc_in, gk_ref, gs_ref, gelu_ref, gbu_ref, dc_ref, up_w, down_w = rest

    @pl.when(pl.program_id(0) == 0)
    def _():
        dc_ref[...] = jnp.zeros_like(dc_ref) if first else dc_in[...]

    gather_rows(who, ups, up_w)
    gather_rows(who, downs, down_w)
    row = (base + pl.program_id(0)) // (c_ref.shape[1] // TILE)
    h = dot(c_ref[...], up_w[...]) + bu_ref[pl.ds(row, 1), :]
    phi, bell = gelu_pair(h)
    gelu = (h * phi).astype(bf16)
    gelu_ref[...] = gelu
    slope = phi + h * bell * 0.3989422804014327
    dh = (dot(dm_ref[...], down_w[...]) * slope).astype(bf16)
    gbu_ref[...] = jnp.sum(dh.astype(f32), axis=0, keepdims=True)
    half = gk_ref.shape[1]
    grad = dot(ct_ref[...], dh).astype(bf16)
    gk_ref[0], gs_ref[0] = grad[:half], grad[half:]
    grad = dot(dmt_ref[...], gelu).astype(bf16)
    gk_ref[1], gs_ref[1] = grad[:half], grad[half:]
    dc_ref[...] += dot(dh, up_w[...], NT)


def ffn(who, c, dm, ct, dmt, ups, downs, vecs, dc, part, after):
    rows, width = c.shape
    cols = 4 * width // PARTS
    base, across = part * cols // TILE, width // TILE
    up_specs, up_arrays = shard_specs(ups, TILE, lambda i: i)
    down_specs, down_arrays = shard_specs(downs, TILE, lambda i: i)
    half = jax.ShapeDtypeStruct((2, width // 2, cols), bf16)
    hspec = pl.BlockSpec((2, width // 2, TILE), lambda i: (0, 0, i))
    return call(
        functools.partial(ffn_body, dc is None, (len(ups), len(downs)), base),
        (cols // TILE,),
        [SM, whole(c.shape), whole(dm.shape), whole(ct.shape), whole(dmt.shape)]
        + up_specs
        + down_specs
        + [pl.BlockSpec((8, TILE), lambda i: (1, (base + i) % across))]
        + ([] if dc is None else [whole(dc.shape)]),
        [
            (half, hspec),
            (half, hspec),
            (far_mem((rows, cols), bf16), pl.BlockSpec((rows, TILE), lambda i: (0, i))),
            (jax.ShapeDtypeStruct((1, cols), f32), pl.BlockSpec((1, TILE), lambda i: (0, i))),
            (jax.ShapeDtypeStruct((rows, width), f32), whole((rows, width))),
        ],
        [pltpu.VMEM((width, TILE), bf16), pltpu.VMEM((width, TILE), bf16)],
        30,
        (who, c, dm, ct, dmt, *up_arrays, *down_arrays, vecs) + (() if dc is None else (dc,)),
        "ffn",
        after,
    )


def turn_body(who, dc_ref, y_ref, dm_ref, o0, o1, o2, vec_ref, *rest):
    shards, rest = rest[:-10], rest[-10:]
    dy_ref, gk_ref, gs_ref, do0, do1, do2, gv_ref, w_ref, scratch, drt_ref = rest
    gather_rows(who, shards, w_ref)
    wide = GROUP * HEAD
    dc = dc_ref[...]
    unit, factor = unit_rows(y_ref[...])
    gv_ref[0:1, :] = jnp.sum(dc * unit, axis=0, keepdims=True)
    gv_ref[1:2, :] = jnp.sum(dc, axis=0, keepdims=True)
    dy = dm_ref[...].astype(f32) + unit_back(dc, unit, factor, vec_ref[5:6, :])
    dy_ref[...] = dy
    dr = dy.astype(bf16)
    gv_ref[2:3, :] = jnp.sum(dr.astype(f32), axis=0, keepdims=True)
    put_turned(who, dr, scratch, drt_ref)
    half = gk_ref.shape[0]
    for group, (o, do) in enumerate(((o0, do0), (o1, do1), (o2, do2))):
        cols = slice(group * wide, (group + 1) * wide)
        do[...] = dot(dr, w_ref[:, cols]).astype(bf16)
        grad = dot(drt_ref[...], o[...]).astype(bf16)
        gk_ref[:, cols] = grad[:half]
        gs_ref[:, cols] = grad[half:]


def turn(who, dc, y, dm, outs, weights, vecs, after):
    rows, width = y.shape
    half = jax.ShapeDtypeStruct((width // 2, width), bf16)
    do = jax.ShapeDtypeStruct((rows, GROUP * HEAD), bf16)
    specs, arrays = shard_specs(weights, width, lambda i: 0)
    results = [far_mem((rows, width), f32), half, half, do, do, do, jax.ShapeDtypeStruct((3, width), f32)]
    return call(
        turn_body,
        (1,),
        [SM, whole(dc.shape), whole(y.shape), whole(dm.shape)] + [whole(o.shape) for o in outs] + [whole(vecs.shape)] + specs,
        [(r, whole(r.shape)) for r in results],
        [pltpu.VMEM((width, width), bf16), pltpu.VMEM((width, rows), bf16), pltpu.VMEM((width, rows), bf16)],
        28,
        (who, dc, y, dm, *outs, vecs, *arrays),
        "turn",
        after,
    )


def attend_back_body(len_ref, qkv_ref, do_ref, st_ref, at_ref, d_ref, gk_ref, gs_ref, gb_ref):
    wide = GROUP * HEAD
    halves = half_masks()

    @pl.loop(0, len_ref.shape[0])
    def _(item):
        rows = pl.ds(pl.multiple_of(item * PAD, PAD), PAD)
        valid = key_mask(len_ref[item])
        for pair in range(GROUP // 2):
            at = pair * 2 * HEAD
            q = qkv_ref[rows, at : at + 2 * HEAD]
            k = qkv_ref[rows, wide + at : wide + at + 2 * HEAD]
            v = qkv_ref[rows, 2 * wide + at : 2 * wide + at + 2 * HEAD]
            do = do_ref[rows, at : at + 2 * HEAD]
            dq = dk = dv = jnp.zeros((PAD, 2 * HEAD), f32)
            for half in range(2):
                head = 2 * pair + half
                km = k * halves[half]
                s = dot(km, q, NT) * HEAD ** (-0.5)
                s = jnp.where(valid, s, -1000000000.0)
                p = jnp.exp(s - st_ref[item, head : head + 1, :]) * st_ref[item, GROUP + head : GROUP + head + 1, :]
                dv += dot(p.astype(bf16), do * halves[half])
                dp = dot(v * halves[half], do, NT)
                delta = jnp.sum(dp * p, axis=0, keepdims=True)
                ds = (p * (dp - delta)).astype(bf16)
                dk += dot(ds, q * halves[half])
                dq += dot(ds, km, TN)
            d_ref[rows, at : at + 2 * HEAD] = (dq * HEAD ** (-0.5)).astype(bf16)
            d_ref[rows, wide + at : wide + at + 2 * HEAD] = (dk * HEAD ** (-0.5)).astype(bf16)
            d_ref[rows, 2 * wide + at : 2 * wide + at + 2 * HEAD] = dv.astype(bf16)

    half = gk_ref.shape[0]
    grad = dot(at_ref[...], d_ref[...]).astype(bf16)
    gk_ref[...] = grad[:half]
    gs_ref[...] = grad[half:]
    gb_ref[...] = jnp.sum(d_ref[...].astype(f32), axis=0, keepdims=True)


def attend_back(lengths, qkv, do, stats, at, after):
    rows, wide3 = qkv.shape
    width = at.shape[0]
    half = jax.ShapeDtypeStruct((width // 2, wide3), bf16)
    return call(
        attend_back_body,
        None,
        [SM, VM, VM, VM, VM],
        [
            (jax.ShapeDtypeStruct((rows, wide3), bf16), VM),
            (half, VM),
            (half, VM),
            (jax.ShapeDtypeStruct((1, wide3), f32), VM),
        ],
        [],
        16,
        (lengths, qkv, do, stats, at),
        "attend_back",
        after,
    )


def start_back_body(counts, who, len_ref, d0, d1, d2, xb_ref, dy_ref, mark_ref, vec_ref, gb0, gb1, gb2, mid_ref, bd_ref, bu0, bu1, *rest):
    shards, (out_ref, gv_ref, w_ref, da_ref) = rest[:-4], rest[-4:]
    at = 0
    wide3 = d0.shape[1]
    acc = None
    for group, d in enumerate((d0, d1, d2)):
        gather_rows(who, shards[at : at + counts[group]], w_ref.at[group])
        at += counts[group]
        part = dot(d[...], w_ref[group], NT)
        acc = part if acc is None else acc + part
    da_ref[...] = acc
    gain_grad = shift_grad = embed_grad = jnp.zeros((1, xb_ref.shape[1]), f32)
    for item in range(out_ref.shape[0]):
        rows = slice(item * PAD, (item + 1) * PAD)
        da = da_ref[rows, :]
        unit, factor = unit_rows(xb_ref[rows, :].astype(f32))
        gain_grad += jnp.sum(da * unit, axis=0, keepdims=True)
        shift_grad += jnp.sum(da, axis=0, keepdims=True)
        dx = dy_ref[rows, :] + unit_back(da, unit, factor, vec_ref[0:1, :])
        marked = spread_rows(chosen_rows(mark_ref, len_ref[item], item), dx.shape[1])
        text = dx[:TXT]
        embed_grad += jnp.sum(jnp.where(marked, text, 0.0), axis=0, keepdims=True)
        out_ref[item] = jnp.concatenate([jnp.where(marked, 0.0, text), dx[TXT:SEQ]], axis=0)
    wide, width = GROUP * HEAD, gv_ref.shape[1]
    gv_ref[...] = jnp.zeros_like(gv_ref)
    gv_ref[0:1, :] = gain_grad
    gv_ref[1:2, :] = shift_grad
    for group, gb in enumerate((gb0, gb1, gb2)):
        gv_ref[2:3, group * wide : (group + 1) * wide] = gb[:, :wide]
        gv_ref[3:4, group * wide : (group + 1) * wide] = gb[:, 2 * wide :]
    gv_ref[4:5, :] = mid_ref[2:3, :]
    gv_ref[5:7, :] = mid_ref[0:2, :]
    gv_ref[7:8, :] = bd_ref[...]
    for row, (ref, place) in enumerate(((bu0, 0), (bu0, 1), (bu1, 0), (bu1, 1))):
        gv_ref[8 + row : 9 + row, :] = ref[:, place * width : (place + 1) * width]
    gv_ref[12:13, :] = embed_grad


def start_back(who, lengths, grads, weights, xb, dy, marks_t, vecs, sums, after):
    rows, width = xb.shape
    wide3 = grads[0].shape[1]
    specs, arrays = shard_specs([w for ws in weights for w in ws], wide3, lambda i: 0)
    out = jax.ShapeDtypeStruct((rows // PAD, SEQ, width), f32)
    small = jax.ShapeDtypeStruct((16, width), f32)
    return call(
        functools.partial(start_back_body, [len(ws) for ws in weights]),
        (1,),
        [SM, SM] + [whole(v.shape) for v in (*grads, xb, dy, marks_t, vecs, *sums)] + specs,
        [(out, whole(out.shape)), (small, whole(small.shape))],
        [pltpu.VMEM((len(weights), width, wide3), bf16), pltpu.VMEM((rows, width), f32)],
        28,
        (who, lengths, *grads, xb, dy, marks_t, vecs, *sums, *arrays),
        "start_back",
        after,
    )


def finish_body(who, y_ref, g_ref, *rest):
    weights, (vec_ref, acc_ref, w_ref) = rest[:-3], rest[-3:]

    @pl.when(pl.program_id(0) == 0)
    def _():
        acc_ref[...] = y_ref[...] + vec_ref[7:8, :]

    gather_rows(who, weights, w_ref)
    acc_ref[...] += dot(g_ref[...], w_ref[...], NT)


def finish_last_body(who, y_ref, g_ref, *rest):
    weights, (out_ref, acc_ref, w_ref) = rest[:-3], rest[-3:]

    @pl.when(pl.program_id(0) == 0)
    def _():
        acc_ref[...] = y_ref[...]

    gather_rows(who, weights, w_ref)
    acc_ref[...] += dot(g_ref[...], w_ref[...], NT)

    @pl.when(pl.program_id(0) == pl.num_programs(0) - 1)
    def _():
        for item in range(out_ref.shape[0]):
            out_ref[item] = acc_ref[item * PAD : (item + 1) * PAD, :].astype(bf16)[:SEQ]


def finish(who, y, gelu, downs, vecs, after):
    rows, width = y.shape
    step = 768
    last = vecs is None
    out = jax.ShapeDtypeStruct((rows // PAD, SEQ, width) if last else y.shape, bf16 if last else f32)
    specs, arrays = shard_specs([(v, at * TILE // step) for v, at in downs], step, lambda i: i)
    return call(
        finish_last_body if last else finish_body,
        (gelu.shape[1] // step,),
        [SM, whole(y.shape), pl.BlockSpec((rows, step), lambda i: (0, i))]
        + specs
        + ([] if last else [whole(vecs.shape)]),
        [(out, whole(out.shape))],
        ([pltpu.VMEM((rows, width), f32)] if last else []) + [pltpu.VMEM((width, step), bf16)],
        24,
        (who, y, gelu, *arrays) + (() if last else (vecs,)),
        "finish",
        after,
    )[0]


def swap(value, axis, bit):
    size = lax.axis_size(axis)
    return lax.ppermute(value, axis, [(i, i ^ (1 << bit)) for i in range(size)])


def half_of(value, which, dim):
    size = value.shape[dim] // 2
    return lax.dynamic_slice_in_dim(value, which * size, size, dim)


def plus(*arrays):
    return functools.reduce(lambda a, b: a + b, (v.astype(f32) for v in arrays))


def step_call(body, who, ins, shapes, name, after):
    outs = [(jax.ShapeDtypeStruct(shape, dtype), VM) for shape, dtype in shapes]
    return call(body, None, [SM] + [VM] * len(ins), outs, [], 8, (who, *ins), name, after, flops=10**9)


def far_body(who, *refs):
    out, pairs = refs[-1], refs[:-1]
    at = 0
    for keep, got in zip(pairs[0::2], pairs[1::2]):
        for one in range(keep.shape[0]):
            out[at] = plus(keep[one, 1], got[one, 1]).astype(bf16)
            at += 1


def near_body(who, *refs):
    far, send, mine = refs[-3:]
    half = send.shape[1]
    go = pl.ds(pl.multiple_of((1 - who[1]) * half, 32), half)
    stay = pl.ds(pl.multiple_of(who[1] * half, 32), half)
    at = 0
    for keep, got in zip(refs[:-3:2], refs[1:-3:2]):
        for one in range(keep.shape[0]):
            send[at] = plus(keep[one, 0, go], got[one, 0, go], far[at, go]).astype(bf16)
            mine[at] = plus(keep[one, 0, stay], got[one, 0, stay], far[at, stay])
            at += 1


def mid_body(who, keep, got, send, mine):
    half = send.shape[1]
    go = pl.ds(pl.multiple_of((1 - who[2]) * half, 16), half)
    stay = pl.ds(pl.multiple_of(who[2] * half, 16), half)
    send[...] = plus(keep[:, go], got[:, go]).astype(bf16)
    mine[...] = plus(keep[:, stay], got[:, stay])


def add_body(who, one, two, out):
    out[...] = plus(one[...], two[...]).astype(bf16)


def join_body(who, mine, got, out):
    half = mine.shape[1]
    out[:, pl.ds(pl.multiple_of(who[2] * half, 16), half)] = mine[...]
    out[:, pl.ds(pl.multiple_of((1 - who[2]) * half, 16), half)] = got[...]


class Chunk:
    def __init__(self, who, keeps, sends):
        split = lambda v: v.reshape(-1, 2, v.shape[-2] // 2, v.shape[-1])
        self.who = who
        self.pairs = [w for k, s in zip(keeps, sends) for w in (split(k), swap(split(s), "fsdp", 0))]
        self.count = sum(k.shape[0] for k in self.pairs[::2])
        self.rows, self.cols = self.pairs[0].shape[2:]

    def far(self, *after):
        self.out = step_call(far_body, self.who, self.pairs, [((self.count, self.rows, self.cols), bf16)], "far", after)[0]
        return self.out

    def near(self, *after):
        shape = (self.count, self.rows // 2, self.cols)
        got = swap(self.out, "fsdp", 1)
        self.out, self.mine = step_call(near_body, self.who, [*self.pairs, got], [(shape, bf16), (shape, f32)], "near", after)
        return self.out

    def mid(self, *after):
        shape = (self.count, self.rows // 4, self.cols)
        got = swap(self.out, "dp", 0)
        self.out, self.mine = step_call(mid_body, self.who, [self.mine, got], [(shape, bf16), (shape, f32)], "mid", after)
        return self.out

    def rest(self, *after):
        got = swap(self.out, "dp", 1)
        self.out = step_call(add_body, self.who, [self.mine, got], [(got.shape, bf16)], "rest", after)[0]
        return self.out

    def part(self, *after):
        for bit in range(2, lax.axis_size("dp").bit_length() - 1):
            got = swap(self.out, "dp", bit)
            self.out = step_call(add_body, self.who, [self.out, got], [(got.shape, bf16)], "part", after)[0]
        return self.out

    def half(self, *after):
        got = swap(self.out, "dp", 1)
        shape = (self.count, self.rows // 2, self.cols)
        self.out = step_call(join_body, self.who, [self.out, got], [(shape, bf16)], "join", after)[0]
        return self.out

    def halves(self):
        return self.out, swap(self.out, "dp", 0)


def adam_body(chained, who, mine, got, first, second, weight, *rest):
    first_new, second_new, update, sums = rest[-4:]
    low = who[1] == 0
    a, b = mine[0].astype(f32), got[0].astype(f32)
    grad = jnp.concatenate([jnp.where(low, a, b), jnp.where(low, b, a)], axis=0)
    moved = adam_moments(grad, first[...], second[...])
    master = weight[...]
    first_new[...], second_new[...] = moved[0], moved[1]
    change = moved[2] + decay_rate * master
    update[...] = change

    @pl.when(pl.program_id(0) == 0)
    def _():
        sums[...] = jnp.zeros_like(sums)

    sums[0:1, :] += jnp.sum(master * master, axis=0, keepdims=True)
    sums[1:2, :] += jnp.sum(change * change, axis=0, keepdims=True)


def adam(who, halves, first, second, weight, wide, steps, grad_at, column_at, made, after):
    rows = weight.shape[0]
    grad = pl.BlockSpec((1, rows // 2, wide), lambda i: (grad_at(i)[0], 0, grad_at(i)[1]))
    block = pl.BlockSpec((rows, wide), lambda i: (0, column_at(i)))
    full = jax.ShapeDtypeStruct(weight.shape, f32)
    sums = jax.ShapeDtypeStruct((2, wide), f32)
    made = list(made or [])
    return call(
        functools.partial(adam_body, len(made)),
        (steps,),
        [SM, grad, grad, block, block, block] + [pl.BlockSpec(memory_space=pl.ANY)] * len(made),
        [(full, block), (full, block), (full, block), (sums, whole(sums.shape))],
        [],
        14,
        (who, *halves, first, second, weight, *made),
        "adam",
        after,
        {6 + k: k for k in range(len(made))},
    )


def total_body(*refs):
    *parts, out = refs
    for row, group in enumerate(parts_of(parts)):
        for kind in range(2):
            value = sum(jnp.sum(ref[kind : kind + 1, :]) for ref in group)
            out[4 * kind + row : 4 * kind + row + 1, :] = jnp.full((1, out.shape[1]), value, f32)


def parts_of(parts):
    return parts[0:2], parts[2:3], parts[3:5], parts[5:7]


def totals(sums):
    out = jax.ShapeDtypeStruct((8, 128), f32)
    return call(total_body, None, [VM] * len(sums), [(out, VM)], [], 8, tuple(sums), "totals")[0]


def apply_body(one, two, w0, w1, w2, w3, u0, u1, u2, u3, n0, n1, n2, n3, norms):
    total = one[...] + two[...]
    norms[...] = jnp.sqrt(total)
    for row, (w, u, n) in enumerate(((w0, u0, n0), (w1, u1, n1), (w2, u2, n2), (w3, u3, n3))):
        ratio = jnp.sqrt(total[row : row + 1, :1]) * lax.rsqrt(total[4 + row : 5 + row, :1] + adam_eps)
        n[...] = w[...] - (matrix_rate * ratio) * u[...]


def apply(one, two, weights, updates):
    steps = 3
    blocks = [pl.BlockSpec((w.shape[0], w.shape[1] // steps), lambda i: (0, i)) for w in weights]
    norms = jax.ShapeDtypeStruct(one.shape, f32)
    return call(
        apply_body,
        (steps,),
        [whole(one.shape)] * 2 + blocks + blocks,
        [(jax.ShapeDtypeStruct(w.shape, f32), b) for w, b in zip(weights, blocks)] + [(norms, whole(one.shape))],
        [],
        24,
        (one, two, *weights, *updates),
        "apply",
    )


def vector_body(who, one, two, first, second, params, new, first_new, second_new):
    rows, cols = params.shape
    total = one[...] + two[...]
    grad = total[:rows, :cols]
    for block in range(1, 4):
        grad = jnp.where(who[0] == block, total[:rows, block * cols : (block + 1) * cols], grad)
    moved = adam_moments(grad, first[...], second[...])
    first_new[...], second_new[...] = moved[0], moved[1]
    new[...] = params[...] - vector_rate * moved[2]


def vector_step(who, one, two, first, second, params):
    out = jax.ShapeDtypeStruct(params.shape, f32)
    args = (who, one, two, first, second, params)
    return call(vector_body, None, [SM] + [VM] * 5, [(out, VM)] * 3, [], 8, args, "vector_step")


def adam_moments(grad, first, second):
    first_new = beta_one * first + (1.0 - beta_one) * grad
    second_new = beta_two * second + (1.0 - beta_two) * grad * grad
    direction = (
        first_new
        / (1.0 - beta_one**STEP)
        / (jnp.sqrt(second_new / (1.0 - beta_two**STEP)) + adam_eps)
    )
    return (first_new, second_new, direction)


def local(
    block_in,
    out_grad,
    caption_len,
    mask_marks,
    qkv_weight,
    out_weight,
    up_weight,
    down_weight,
    vector_params,
    qkv_first,
    qkv_second,
    out_first,
    out_second,
    up_first,
    up_second,
    down_first,
    down_second,
    vector_first,
    vector_second,
):
    width = block_in.shape[2]
    hidden = up_weight.shape[1]
    groups = width // (GROUP * HEAD)
    shard = lax.axis_index("fsdp")
    replica = lax.axis_index("dp")
    who = jnp.stack([shard, replica & 1, (replica >> 1) & 1]).astype(jnp.int32)
    cols = hidden // PARTS
    core = lambda v: swap(v, "fsdp", 0)
    far = lambda v: swap(v, "fsdp", 1)
    turned = lambda v: v.T

    own_heads = cast_heads(qkv_weight)
    vec_own = vector_params.astype(bf16)
    far_heads = [far(own_heads[0])]
    vec_far = far(vec_own)
    far_heads += [far(v) for v in own_heads[1:]]
    own_out, half_up, half_down, *own_parts = cast_rest(
        who, out_weight.T, up_weight, down_weight.T, [own_heads[0]]
    )
    far_out, far_up, far_down, far_part = (far(v) for v in (own_out, half_up, half_down, own_parts[1]))
    vec_shards = [vec_own, core(vec_own), vec_far, core(vec_far)]
    core_parts = [core(v) for v in own_parts]
    first_block = lambda *arrays: [(v, 0) for v in arrays]
    heads_full = [first_block(own, core(own), other, core(other)) for own, other in zip(own_heads, far_heads)]
    out_full = first_block(own_out, core(own_out), far_out, core(far_out))

    marks_t = mask_marks.T
    vecs, xb, a, at, dm, dmt, grad_bd = prep(who, caption_len, block_in, out_grad, marks_t, vec_shards)
    heads = []
    for g in range(groups):
        waits = [h[1] for h in heads[-1:]]
        if g == 2:
            mine_up = tie(far_up, *waits)
            waits.append(mine_up)
        heads.append(attend(who, caption_len, a, heads_full[g], vecs, g, waits))
    mine_down = tie(far_down, heads[-1][1])
    outs = [h[1] for h in heads]
    y, c, ct = mix(who, xb, outs, out_full, vecs, [mine_down])
    tile = cols // TILE
    sides = lambda mine: (mine, swap(mine, "dp", 0))
    pair = lambda own, at: [(own, at), (core(own), at)]
    up_far, down_far = sides(mine_up), sides(mine_down)
    part0 = [(own_parts[0], 0), (core_parts[0], 0)]
    part0_down = [(own_parts[0], tile), (core_parts[0], tile)]
    ups = part0 + first_block(*up_far, *(core(v) for v in up_far))
    downs = part0_down + first_block(*down_far, *(core(v) for v in down_far))
    ffn0 = ffn(who, c, dm, ct, dmt, ups, downs, vecs, None, 0, [])
    chunk_a = Chunk(who, [ffn0[0]], [ffn0[1]])
    result = finish(who, y, ffn0[2], downs, vecs, [])
    far_part = tie(far_part, result)
    shards1 = (own_parts[1], core_parts[1], far_part, core(far_part))
    ups1 = [(v, 0) for v in shards1]
    downs1 = [(v, tile) for v in shards1]
    ffn1 = ffn(who, c, dm, ct, dmt, ups1, downs1, vecs, ffn0[4], 1, [chunk_a.far(result)])
    chunk_b = Chunk(who, [ffn1[0]], [ffn1[1]])
    block_out = finish(who, result, ffn1[2], downs1, None, [])
    sent_b = chunk_b.far(block_out)
    sent_a = chunk_a.near(sent_b)
    dy, out_keep, out_send, *dos, grad_mid = turn(who, ffn1[4], y, dm, outs, out_full, vecs, [sent_b, sent_a])
    back0 = attend_back(caption_len, heads[0][0], dos[0], heads[0][2], at, [])
    chunk_c = Chunk(who, [out_keep, back0[1]], [out_send, back0[2]])
    sent_a = chunk_a.mid(back0[0])
    sent_c = chunk_c.far(sent_a)
    back1 = attend_back(caption_len, heads[1][0], dos[1], heads[1][2], at, [sent_a, sent_c])
    sent_a = chunk_a.rest(back1[0])
    back2 = attend_back(caption_len, heads[2][0], dos[2], heads[2][2], at, [sent_a])
    backs = [back0, back1, back2]
    chunk_d = Chunk(who, [back1[1], back2[1]], [back1[2], back2[2]])
    sent_b = chunk_b.near(back2[0])
    sent_a = chunk_a.part(sent_b)
    sent_d = chunk_d.far(sent_a)
    sent_c = chunk_c.near(sent_d)
    sums = [b[3] for b in backs] + [grad_mid, grad_bd, ffn0[3], ffn1[3]]
    input_grad, vector_grads = start_back(
        who,
        caption_len,
        [b[0] for b in backs],
        heads_full,
        xb,
        dy,
        marks_t,
        vecs,
        sums,
        [sent_a, sent_b, sent_c, sent_d],
    )
    sent_a = chunk_a.half(input_grad)
    sent_b = chunk_b.mid(sent_a)
    vector_one = vector_grads + core(vector_grads)
    sent_d = chunk_d.near(sent_b)
    sent_c = chunk_c.mid(sent_d)
    vector_one = vector_one + far(vector_one)

    qkv = (qkv_first, qkv_second, qkv_weight)
    out = tuple(turned(v) for v in (out_first, out_second, out_weight))
    up = (up_first, up_second, up_weight)
    down = tuple(turned(v) for v in (down_first, down_second, down_weight))
    wide = 2 * TILE
    per = cols // wide

    sent_b = chunk_b.rest(sent_c)
    sent_d = chunk_d.mid(sent_b)
    sent_c = chunk_c.rest(sent_d)
    halves_a = chunk_a.halves()
    up_made = adam(who, halves_a, *up, wide, per, lambda i: (0, i), lambda i: i, None, [sent_c])
    sent_b = chunk_b.part(up_made[3])
    sent_d = chunk_d.rest(sent_b)
    sent_c = chunk_c.part(sent_d)
    down_made = adam(who, halves_a, *down, wide, per, lambda i: (1, i), lambda i: i, None, [sent_c])
    sent_b = chunk_b.half(down_made[3])
    sent_d = chunk_d.part(sent_b)
    sent_c = chunk_c.half(sent_d)
    sent_d = chunk_d.half(sent_c)
    for bit in range(lax.axis_size("dp").bit_length() - 1):
        got = swap(vector_one, "dp", bit)
        if bit < lax.axis_size("dp").bit_length() - 2:
            vector_one = vector_one + got
    halves_c = chunk_c.halves()
    out_made = adam(who, halves_c, *out, TILE, width // TILE, lambda i: (0, i), lambda i: i, None, [sent_d])
    qkv_made = adam(who, halves_c, *qkv, TILE, 3, lambda i: (1, i), lambda i: groups * i, None, [out_made[3]])
    halves_b = chunk_b.halves()
    up_last = adam(who, halves_b, *up, wide, per, lambda i: (0, i), lambda i: per + i, up_made[:3], [qkv_made[3]])
    down_last = adam(who, halves_b, *down, wide, per, lambda i: (1, i), lambda i: per + i, down_made[:3], [up_last[3]])
    qkv_last = adam(
        who,
        chunk_d.halves(),
        *qkv,
        TILE,
        3 * (groups - 1),
        lambda i: (i // 3, i % 3),
        lambda i: groups * (i % 3) + 1 + i // 3,
        qkv_made[:3],
        [down_last[3]],
    )
    vector_new, vector_first_new, vector_second_new = vector_step(
        who, vector_one, got, vector_first, vector_second, vector_params
    )
    squares = totals([qkv_made[3], qkv_last[3], out_made[3], up_made[3], up_last[3], down_made[3], down_last[3]])
    squares = squares + core(squares)
    weights = (qkv_weight, out[2], up_weight, down[2])
    made = (qkv_last, out_made, up_last, down_last)
    *new_weights, norms = apply(squares, far(squares), weights, [m[2] for m in made])
    back = (lambda v: v, turned, lambda v: v, turned)
    moments = [f(m[k]) for f, m in zip(back, made) for k in range(2)]
    return (
        block_out,
        input_grad,
        *(f(w) for f, w in zip(back, new_weights)),
        vector_new,
        *moments,
        vector_first_new,
        vector_second_new,
        norms[:, 0].reshape(2, 4),
    )


def solution(mesh):
    placed = (
        P(("dp", "fsdp"), None, None),
        P(("dp", "fsdp"), None, None),
        P(("dp", "fsdp")),
        P(("dp", "fsdp"), None),
        P("fsdp", None),
        P(None, "fsdp"),
        P("fsdp", None),
        P(None, "fsdp"),
        P(None, "fsdp"),
        P("fsdp", None),
        P("fsdp", None),
        P(None, "fsdp"),
        P(None, "fsdp"),
        P("fsdp", None),
        P("fsdp", None),
        P(None, "fsdp"),
        P(None, "fsdp"),
        P(None, "fsdp"),
        P(None, "fsdp"),
    )
    return jax.shard_map(
        local,
        mesh=mesh,
        in_specs=placed,
        out_specs=(
            P(("dp", "fsdp"), None, None),
            P(("dp", "fsdp"), None, None),
            P("fsdp", None),
            P(None, "fsdp"),
            P("fsdp", None),
            P(None, "fsdp"),
            P(None, "fsdp"),
            P("fsdp", None),
            P("fsdp", None),
            P(None, "fsdp"),
            P(None, "fsdp"),
            P("fsdp", None),
            P("fsdp", None),
            P(None, "fsdp"),
            P(None, "fsdp"),
            P(None, "fsdp"),
            P(None, "fsdp"),
            P(),
        ),
        check_vma=False,
    )
```

```python
import functools

import jax
import jax.numpy as jnp
from jax import lax
from jax.experimental import pallas as pl
from jax.experimental.pallas import tpu as pltpu
from jax.sharding import PartitionSpec as P

HEAD = 64
TXT = 40
PATCH = 145
STEP = 7
SEQ = TXT + PATCH
PAD = 192
GROUP = 4
PARTS = 2
EXTRA = 16
LIGHT = 10**4
TILE = 256

ln_eps = 1e-06
beta_one = 0.5
beta_two = 0.55
adam_eps = 1e-06
decay_rate = 0.01
matrix_rate = 0.5
vector_rate = 0.3

f32 = jnp.float32
bf16 = jnp.bfloat16
ORDER = (0, 2, 1, 3)
NT = (((1,), (1,)), ((), ()))
TN = (((0,), (0,)), ((), ()))

VM = pl.BlockSpec(memory_space=pltpu.VMEM)
SM = pl.BlockSpec(memory_space=pltpu.SMEM)


def dot(left, right, dims=None):
    if dims is None:
        return jnp.dot(left, right, preferred_element_type=f32)
    return lax.dot_general(left, right, dims, preferred_element_type=f32)


def call(body, grid, ins, outs, scratch, limit, args, name, after=(), aliases=None, flops=8 * 10**9):
    count = len(ins)
    after = [afar(v) if v.size > 65536 else v for v in after]

    def run(*refs):
        body(*refs[:count], *refs[count + len(after) :])

    return pl.pallas_call(
        run,
        grid=grid or (),
        in_specs=list(ins) + [pl.BlockSpec(memory_space=pl.ANY)] * len(after),
        out_specs=[o[1] for o in outs],
        out_shape=[o[0] for o in outs],
        input_output_aliases=aliases or {},
        scratch_shapes=scratch,
        compiler_params=pltpu.CompilerParams(vmem_limit_bytes=limit << 20),
        cost_estimate=pl.CostEstimate(flops=flops, bytes_accessed=flops // 200, transcendentals=0),
        name=name,
    )(*args, *after)


def far_mem(shape, dtype):
    return pltpu.HBM(tuple(shape), dtype)


def near_mem(shape, dtype):
    return pltpu.VMEM(tuple(shape), dtype)


def near(value):
    return pltpu.with_memory_space_constraint(value, pltpu.VMEM)


def afar(value):
    return pltpu.with_memory_space_constraint(value, pltpu.HBM)


def tie(value, *deps):
    return pl.pallas_call(
        lambda *refs: None,
        in_specs=[pl.BlockSpec(memory_space=pl.ANY)] * (1 + len(deps)),
        out_specs=pl.BlockSpec(memory_space=pl.ANY),
        out_shape=jax.ShapeDtypeStruct(value.shape, value.dtype),
        input_output_aliases={0: 0},
        cost_estimate=pl.CostEstimate(flops=LIGHT, bytes_accessed=LIGHT, transcendentals=0),
        name="tie",
    )(value, *[afar(v) if v.size > 65536 else v for v in deps])


def whole(shape):
    return pl.BlockSpec(shape, lambda i: (0,) * len(shape), pipeline_mode=pl.Buffered(1))


def wholes(*arrays):
    return [whole(v.shape) for v in arrays]


def shard_specs(shards, wide, columns):
    rows = lambda v: v.shape[0] - v.shape[0] % 96
    specs = [pl.BlockSpec((rows(v), wide), lambda i, at=at: (0, at + columns(i))) for v, at in shards]
    return specs, [afar(v) for v, _ in shards]


def unit_rows(rows):
    centred = rows - jnp.mean(rows, axis=-1, keepdims=True)
    factor = lax.rsqrt(jnp.mean(centred * centred, axis=-1, keepdims=True) + ln_eps)
    return centred * factor, factor


def unit_back(grad_normed, unit, factor, gain):
    grad_unit = grad_normed * gain
    return factor * (
        grad_unit
        - jnp.mean(grad_unit, axis=-1, keepdims=True)
        - unit * jnp.mean(grad_unit * unit, axis=-1, keepdims=True)
    )


def put_turned(who_ref, value, scratch, out_ref):
    part = out_ref.shape[0] // 16
    scratch[...] = value.T
    for place in range(16):
        core, one, two, three = (place >> 3) & 1, (place >> 2) & 1, (place >> 1) & 1, place & 1
        odd = (who_ref[0] & 1) ^ core
        pair = jnp.where(odd == 0, one, two)
        low = jnp.where(odd == 0, two, one)
        start = 4 * (who_ref[0] ^ (2 * pair + core)) + 2 * (who_ref[1] ^ low) + (who_ref[2] ^ three)
        out_ref[place * part : (place + 1) * part, :] = scratch[pl.ds(pl.multiple_of(start * part, 16), part), :]


def gather_rows(who_ref, refs, out_ref):
    rows = refs[0].shape[0]
    half = rows // 2
    places = [(0, None), (1, None)]
    places += [(2, None), (3, None)] if len(refs) == 4 else [(2, 0), (2, 1), (3, 0), (3, 1)]
    for (other, part), ref in zip(places, refs):
        start = (who_ref[0] ^ other) * rows
        if part is not None:
            start += (who_ref[1] ^ part) * half
        out_ref[pl.ds(pl.multiple_of(start, 32), ref.shape[0]), :] = ref[...]


def cast_heads_body(q_ref, k_ref, v_ref, vec_ref, one_ref, rest_ref):
    wide = GROUP * HEAD
    rows = q_ref.shape[0]
    step = pl.program_id(0)

    @pl.when(step == 0)
    def _():
        for kind, ref in enumerate((q_ref, k_ref, v_ref)):
            one_ref[:rows, kind * wide : (kind + 1) * wide] = ref[...].astype(bf16)
        count, cols = vec_ref.shape
        one_ref[rows:, :] = jnp.zeros_like(one_ref[rows:, :])
        one_ref[rows : rows + count, :cols] = vec_ref[...].astype(bf16)

    @pl.when(step > 0)
    def _():
        for kind, ref in enumerate((q_ref, k_ref, v_ref)):
            at = pl.multiple_of(((step - 1) * 3 + kind) * wide, wide)
            rest_ref[:, pl.ds(at, wide)] = ref[...].astype(bf16)


def cast_heads(weight, vectors):
    rows, cols = weight.shape
    wide = GROUP * HEAD
    groups = cols // (3 * wide)
    blocks = [pl.BlockSpec((rows, wide), lambda i, kind=kind: (0, kind * groups + i)) for kind in range(3)]
    shapes = [(rows + EXTRA, 3 * wide), (rows, 3 * wide * (groups - 1))]
    outs = [(far_mem(shape, bf16), whole(shape)) for shape in shapes]
    args = (*[afar(weight)] * 3, vectors)
    return call(cast_heads_body, (groups,), blocks + wholes(vectors), outs, [], 12, args, "cast_heads")


def cast_rest_body(who, out_ref, up_ref, down_ref, o_ref, up_half, down_half, *parts):
    half = up_half.shape[0]
    rows = pl.ds(pl.multiple_of(who[1] * half, 32), half)
    step = pl.program_id(0)
    per = pl.num_programs(0) // PARTS

    @pl.when(step == 0)
    def _():
        o_ref[...] = out_ref[...].astype(bf16)

    @pl.when(step < per)
    def _():
        up_half[...] = up_ref[rows, :].astype(bf16)
        down_half[...] = down_ref[rows, :].astype(bf16)

    @pl.when(step < per)
    def _():
        parts[0][...] = up_ref[...].astype(bf16)
        parts[1][...] = down_ref[...].astype(bf16)

    wide = up_ref.shape[1]
    for place in range(per):

        @pl.when(step == per + place)
        def _(place=place):
            parts[2][:, place * wide : (place + 1) * wide] = up_ref[...].astype(bf16)
            parts[2][:, (per + place) * wide : (per + place + 1) * wide] = down_ref[...].astype(bf16)


def cast_rest(who, out_t, up, down_t, after):
    rows, hidden = up.shape
    cols, wide = hidden // PARTS, 768
    per = cols // wide
    block = pl.BlockSpec((rows, wide), lambda i: (0, i))
    at = lambda part: lambda i: (0, jnp.clip(i - part * per, 0, per - 1))
    out = lambda n, part: (far_mem((n, cols), bf16), pl.BlockSpec((n, wide), at(part)))
    outs = [(far_mem(out_t.shape, bf16), whole(out_t.shape)), out(rows // 2, 0), out(rows // 2, 0)]
    both = (rows, 2 * cols)
    outs += [out(rows, 0), out(rows, 0), (far_mem(both, bf16), whole(both))]
    ins = [SM] + wholes(out_t) + [block, block]
    args = (who, out_t, afar(up), afar(down_t))
    return call(cast_rest_body, (hidden // wide,), ins, outs, [], 16, args, "cast_rest", after)


def chosen_rows(marks, length):
    places = lax.broadcasted_iota(jnp.int32, marks.shape, 0)
    return jnp.where((marks == 1) & (places >= 1) & (places < length), 1.0, 0.0)


def spread_rows(chosen, width):
    return jnp.broadcast_to(chosen, (chosen.shape[0], width)) > 0


def prep_grad_body(who, g_ref, dm_ref, dmt_ref, bd_ref, all_ref, scratch):
    step = pl.program_id(0)
    tail = jnp.zeros((PAD - SEQ, g_ref.shape[2]), f32)
    dm = jnp.concatenate([g_ref[0].astype(f32), tail], axis=0)
    dm_ref[...] = dm.astype(bf16)
    all_ref[pl.ds(pl.multiple_of(step * PAD, PAD), PAD), :] = dm.astype(bf16)

    @pl.when(step == 0)
    def _():
        bd_ref[...] = jnp.zeros_like(bd_ref)

    bd_ref[...] += jnp.sum(dm, axis=0, keepdims=True)

    @pl.when(step == pl.num_programs(0) - 1)
    def _():
        put_turned(who, all_ref[...], scratch, dmt_ref)


def prep_grad(who, out_grad, after):
    items, seq, width = out_grad.shape
    rows = items * PAD
    item = pl.BlockSpec((1, seq, width), lambda i: (i, 0, 0))
    return call(
        prep_grad_body,
        (items,),
        [SM, item],
        [
            (far_mem((rows, width), bf16), pl.BlockSpec((PAD, width), lambda i: (i, 0))),
            (far_mem((width, rows), bf16), whole((width, rows))),
            (jax.ShapeDtypeStruct((1, width), f32), whole((1, width))),
        ],
        [pltpu.VMEM((rows, width), bf16), pltpu.VMEM((width, rows), bf16)],
        20,
        (who, afar(out_grad)),
        "prep_grad",
        after,
        flops=LIGHT,
    )


def prep_body(who, len_ref, x_ref, mark_ref, v0, v1, v2, v3, vec_ref, xb_ref, a_ref):
    step = pl.program_id(0)
    width = x_ref.shape[2]

    @pl.when(step == 0)
    def _():
        cols = width // 4
        for block in range(4):
            value = v0[:, :cols].astype(f32)
            for other, ref in ((1, v1), (2, v2), (3, v3)):
                value = jnp.where((who[0] ^ other) == block, ref[:, :cols].astype(f32), value)
            vec_ref[:, block * cols : (block + 1) * cols] = value

    gain, shift, embed = vec_ref[0:1, :], vec_ref[1:2, :], vec_ref[12:13, :]
    x = x_ref[0].astype(f32)
    marked = spread_rows(chosen_rows(mark_ref[0], len_ref[step]), width)
    tail = jnp.zeros((PAD - SEQ, width), f32)
    x = jnp.concatenate([jnp.where(marked, embed, x[:TXT]), x[TXT:], tail], axis=0)
    xb_ref[...] = x.astype(bf16)
    unit, _ = unit_rows(x)
    a_ref[...] = (unit * gain + shift).astype(bf16)


def turn_rows_body(who, a_ref, at_ref, scratch):
    put_turned(who, a_ref[...], scratch, at_ref)


def turn_rows(who, a, after):
    rows, width = a.shape
    out = (far_mem((width, rows), bf16), whole((width, rows)))
    scratch = [pltpu.VMEM((width, rows), bf16)]
    return call(turn_rows_body, (1,), [SM] + wholes(a), [out], scratch, 16, (who, afar(a)), "turn_rows", after)[0]


def prep(who, lengths, block_in, marks, vec_shards, after):
    items, seq, width = block_in.shape
    rows = items * PAD
    item = lambda *shape: pl.BlockSpec((1, *shape), lambda i: (i, 0, 0))
    flat = pl.BlockSpec((PAD, width), lambda i: (i, 0))
    extra = pl.BlockSpec((EXTRA, width), lambda i: (vec_shards[0].shape[0] // EXTRA - 1, 0))
    return call(
        prep_body,
        (items,),
        [SM, SM, item(seq, width), item(*marks.shape[1:])] + [extra] * 4,
        [
            (near_mem((16, width), f32), whole((16, width))),
            (far_mem((rows, width), bf16), flat),
            (far_mem((rows, width), bf16), flat),
        ],
        [],
        16,
        (who, lengths, afar(block_in), marks, *[afar(v) for v in vec_shards]),
        "prep",
        after,
        flops=LIGHT,
    )


def key_mask(length):
    places = lax.broadcasted_iota(jnp.int32, (PAD, 1), 0)
    return ((places >= TXT) & (places < SEQ)) | (places < length)


def half_masks():
    lanes = lax.broadcasted_iota(jnp.int32, (1, 2 * HEAD), 1)
    low = jnp.where(lanes < HEAD, 1.0, 0.0)
    return low.astype(bf16), (1.0 - low).astype(bf16)


def attend_body(group, who, len_ref, a_ref, vec_ref, *rest):
    wide = GROUP * HEAD
    shards, (qkv_ref, o_ref, st_ref, w_ref) = rest[:-4], rest[-4:]
    gather_rows(who, shards, w_ref)
    cols = slice(group * wide, (group + 1) * wide)
    bias = jnp.concatenate([vec_ref[2:3, cols], jnp.zeros((1, wide), f32), vec_ref[3:4, cols]], axis=1)
    qkv_ref[...] = (dot(a_ref[...], w_ref[...]) + bias).astype(bf16)
    halves = half_masks()

    @pl.loop(0, len_ref.shape[0])
    def _(item):
        rows = pl.ds(pl.multiple_of(item * PAD, PAD), PAD)
        valid = key_mask(len_ref[item])
        for pair in range(GROUP // 2):
            at = pair * 2 * HEAD
            q = qkv_ref[rows, at : at + 2 * HEAD]
            k = qkv_ref[rows, wide + at : wide + at + 2 * HEAD]
            v = qkv_ref[rows, 2 * wide + at : 2 * wide + at + 2 * HEAD]
            out = None
            for half in range(2):
                s = dot(k * halves[half], q, NT) * HEAD ** (-0.5)
                s = jnp.where(valid, s, -1000000000.0)
                top = jnp.max(s, axis=0, keepdims=True)
                e = jnp.exp(s - top)
                scale = 1.0 / jnp.sum(e, axis=0, keepdims=True)
                p = (e * scale).astype(bf16)
                part = dot(p, v * halves[half], TN)
                out = part if out is None else out + part
                head = 2 * pair + half
                st_ref[item, head : head + 1, :] = top
                st_ref[item, GROUP + head : GROUP + head + 1, :] = scale
            o_ref[rows, at : at + 2 * HEAD] = out.astype(bf16)


def attend(who, lengths, a, weights, vecs, group, after):
    rows, width = a.shape
    wide = GROUP * HEAD
    items = lengths.shape[0]
    specs, arrays = shard_specs(weights, 3 * wide, lambda i: 0)
    return call(
        functools.partial(attend_body, group),
        (1,),
        [SM, SM, whole(a.shape), whole(vecs.shape)] + specs,
        [
            (far_mem((rows, 3 * wide), bf16), whole((rows, 3 * wide))),
            (far_mem((rows, wide), bf16), whole((rows, wide))),
            (far_mem((items, 2 * GROUP, PAD), f32), whole((items, 2 * GROUP, PAD))),
        ],
        [pltpu.VMEM((width, 3 * wide), bf16)],
        16,
        (who, lengths, afar(a), vecs, *arrays),
        "attend",
        after,
    )


def mix_body(who, x_ref, o0, o1, o2, vec_ref, *rest):
    shards, (y_ref, c_ref, ct_ref, w_ref, scratch) = rest[:-5], rest[-5:]
    gather_rows(who, shards, w_ref)
    wide = GROUP * HEAD
    acc = x_ref[...].astype(f32) + vec_ref[4:5, :]
    for group, o in enumerate((o0, o1, o2)):
        acc += dot(o[...], w_ref[:, group * wide : (group + 1) * wide], NT)
    y_ref[...] = acc
    unit, _ = unit_rows(acc)
    c_ref[...] = (unit * vec_ref[5:6, :] + vec_ref[6:7, :]).astype(bf16)
    put_turned(who, c_ref[...], scratch, ct_ref)


def mix(who, xb, outs, weights, vecs, after):
    rows, width = xb.shape
    specs, arrays = shard_specs(weights, width, lambda i: 0)
    return call(
        mix_body,
        (1,),
        [SM, whole(xb.shape)] + [whole(o.shape) for o in outs] + [whole(vecs.shape)] + specs,
        [
            (far_mem((rows, width), f32), whole((rows, width))),
            (near_mem((rows, width), bf16), whole((rows, width))),
            (near_mem((width, rows), bf16), whole((width, rows))),
        ],
        [pltpu.VMEM((width, width), bf16), pltpu.VMEM((width, rows), bf16)],
        18,
        (who, afar(xb), *[afar(o) for o in outs], vecs, *arrays),
        "mix",
        after,
    )


def gelu_pair(h):
    bell = jnp.exp(-0.5 * h * h)
    t = 1.0 / (1.0 + (0.3275911 * 0.7071067811865476) * jnp.abs(h))
    poly = t * (0.127414796 + t * (-0.142248368 + t * (0.7107068705 + t * (-0.7265760135 + t * 0.5307027145))))
    tail = poly * bell
    return jnp.where(h < 0, tail, 1.0 - tail), bell


def ffn_body(first, counts, base, who, c_ref, dm_ref, ct_ref, dmt_ref, *rest):
    ups, downs, rest = rest[: counts[0]], rest[counts[0] : sum(counts)], rest[sum(counts) :]
    if first:
        bu_ref, uk_ref, us_ref, dk_ref, ds_ref, gelu_ref, gbu_ref, dc_ref, up_w, down_w = rest
    else:
        bu_ref, dc_in, uk_ref, us_ref, dk_ref, ds_ref, gelu_ref, gbu_ref, dc_ref, up_w, down_w = rest

    @pl.when(pl.program_id(0) == 0)
    def _():
        dc_ref[...] = jnp.zeros_like(dc_ref) if first else dc_in[...]

    gather_rows(who, ups, up_w)
    gather_rows(who, downs, down_w)
    row = (base + pl.program_id(0)) // (c_ref.shape[1] // TILE)
    h = dot(c_ref[...], up_w[...]) + bu_ref[pl.ds(row, 1), :]
    phi, bell = gelu_pair(h)
    gelu = (h * phi).astype(bf16)
    gelu_ref[...] = gelu
    slope = phi + h * bell * 0.3989422804014327
    dh = (dot(dm_ref[...], down_w[...]) * slope).astype(bf16)
    gbu_ref[...] = jnp.sum(dh.astype(f32), axis=0, keepdims=True)
    half = uk_ref.shape[0]
    grad = dot(ct_ref[...], dh).astype(bf16)
    uk_ref[...], us_ref[...] = grad[:half], grad[half:]
    grad = dot(dmt_ref[...], gelu).astype(bf16)
    dk_ref[...], ds_ref[...] = grad[:half], grad[half:]
    dc_ref[...] += dot(dh, up_w[...], NT)


def ffn(who, c, dm, ct, dmt, ups, downs, vecs, dc, part, after):
    rows, width = c.shape
    cols = 4 * width // PARTS
    base, across = part * cols // TILE, width // TILE
    up_specs, up_arrays = shard_specs(ups, TILE, lambda i: i)
    down_specs, down_arrays = shard_specs(downs, TILE, lambda i: i)
    half = near_mem((width // 2, cols), bf16)
    hspec = pl.BlockSpec((width // 2, TILE), lambda i: (0, i))
    return call(
        functools.partial(ffn_body, dc is None, (len(ups), len(downs)), base),
        (cols // TILE,),
        [SM, whole(c.shape), whole(dm.shape), whole(ct.shape), whole(dmt.shape)]
        + up_specs
        + down_specs
        + [pl.BlockSpec((8, TILE), lambda i: (1, (base + i) % across))]
        + ([] if dc is None else [whole(dc.shape)]),
        [
            (half, hspec),
            (half, hspec),
            (half, hspec),
            (half, hspec),
            (near_mem((rows, cols), bf16), pl.BlockSpec((rows, TILE), lambda i: (0, i))),
            (jax.ShapeDtypeStruct((1, cols), f32), pl.BlockSpec((1, TILE), lambda i: (0, i))),
            (jax.ShapeDtypeStruct((rows, width), f32), whole((rows, width))),
        ],
        [pltpu.VMEM((width, TILE), bf16), pltpu.VMEM((width, TILE), bf16)],
        30,
        (who, c, dm, ct, dmt, *up_arrays, *down_arrays, vecs) + (() if dc is None else (dc,)),
        "ffn",
        after,
    )


def turn_body(who, dc_ref, y_ref, dm_ref, o0, o1, o2, vec_ref, *rest):
    shards, rest = rest[:-10], rest[-10:]
    dy_ref, gk_ref, gs_ref, do0, do1, do2, gv_ref, w_ref, scratch, drt_ref = rest
    gather_rows(who, shards, w_ref)
    wide = GROUP * HEAD
    dc = dc_ref[...]
    unit, factor = unit_rows(y_ref[...])
    gv_ref[0:1, :] = jnp.sum(dc * unit, axis=0, keepdims=True)
    gv_ref[1:2, :] = jnp.sum(dc, axis=0, keepdims=True)
    dy = dm_ref[...].astype(f32) + unit_back(dc, unit, factor, vec_ref[5:6, :])
    dy_ref[...] = dy
    dr = dy.astype(bf16)
    gv_ref[2:3, :] = jnp.sum(dr.astype(f32), axis=0, keepdims=True)
    put_turned(who, dr, scratch, drt_ref)
    half = gk_ref.shape[0]
    for group, (o, do) in enumerate(((o0, do0), (o1, do1), (o2, do2))):
        cols = slice(group * wide, (group + 1) * wide)
        do[...] = dot(dr, w_ref[:, cols]).astype(bf16)
        grad = dot(drt_ref[...], o[...]).astype(bf16)
        gk_ref[:, cols] = grad[:half]
        gs_ref[:, cols] = grad[half:]


def turn(who, dc, y, dm, outs, weights, vecs, after):
    rows, width = y.shape
    half = jax.ShapeDtypeStruct((width // 2, width), bf16)
    do = jax.ShapeDtypeStruct((rows, GROUP * HEAD), bf16)
    specs, arrays = shard_specs(weights, width, lambda i: 0)
    results = [far_mem((rows, width), f32), half, half, do, do, do, jax.ShapeDtypeStruct((3, width), f32)]
    return call(
        turn_body,
        (1,),
        [SM, whole(dc.shape), whole(y.shape), whole(dm.shape)] + [whole(o.shape) for o in outs] + [whole(vecs.shape)] + specs,
        [(r, whole(r.shape)) for r in results],
        [pltpu.VMEM((width, width), bf16), pltpu.VMEM((width, rows), bf16), pltpu.VMEM((width, rows), bf16)],
        28,
        (who, dc, afar(y), afar(dm), *[afar(o) for o in outs], vecs, *arrays),
        "turn",
        after,
    )


def attend_back_body(len_ref, qkv_ref, do_ref, st_ref, at_ref, d_ref, gk_ref, gb_ref, *gs_refs):
    wide = GROUP * HEAD
    halves = half_masks()

    @pl.loop(0, len_ref.shape[0])
    def _(item):
        rows = pl.ds(pl.multiple_of(item * PAD, PAD), PAD)
        valid = key_mask(len_ref[item])
        for pair in range(GROUP // 2):
            at = pair * 2 * HEAD
            q = qkv_ref[rows, at : at + 2 * HEAD]
            k = qkv_ref[rows, wide + at : wide + at + 2 * HEAD]
            v = qkv_ref[rows, 2 * wide + at : 2 * wide + at + 2 * HEAD]
            do = do_ref[rows, at : at + 2 * HEAD]
            dq = dk = dv = jnp.zeros((PAD, 2 * HEAD), f32)
            for half in range(2):
                head = 2 * pair + half
                km = k * halves[half]
                s = dot(km, q, NT) * HEAD ** (-0.5)
                s = jnp.where(valid, s, -1000000000.0)
                p = jnp.exp(s - st_ref[item, head : head + 1, :]) * st_ref[item, GROUP + head : GROUP + head + 1, :]
                dv += dot(p.astype(bf16), do * halves[half])
                dp = dot(v * halves[half], do, NT)
                delta = jnp.sum(dp * p, axis=0, keepdims=True)
                ds = (p * (dp - delta)).astype(bf16)
                dk += dot(ds, q * halves[half])
                dq += dot(ds, km, TN)
            d_ref[rows, at : at + 2 * HEAD] = (dq * HEAD ** (-0.5)).astype(bf16)
            d_ref[rows, wide + at : wide + at + 2 * HEAD] = (dk * HEAD ** (-0.5)).astype(bf16)
            d_ref[rows, 2 * wide + at : 2 * wide + at + 2 * HEAD] = dv.astype(bf16)

    half = gk_ref.shape[0]
    grad = dot(at_ref[...], d_ref[...]).astype(bf16)
    gk_ref[...] = grad[:half]
    for ref in gs_refs:
        ref[...] = grad[half : half + ref.shape[0]]
        half += ref.shape[0]
    gb_ref[...] = jnp.sum(d_ref[...].astype(f32), axis=0, keepdims=True)


def attend_back(lengths, qkv, do, stats, at, pieces, after):
    rows, wide3 = qkv.shape
    width = at.shape[0]
    half = jax.ShapeDtypeStruct((width // 2, wide3), bf16)
    piece = jax.ShapeDtypeStruct((width // 2 // pieces, wide3), bf16)
    return call(
        attend_back_body,
        None,
        [SM, VM, VM, VM, VM],
        [
            (jax.ShapeDtypeStruct((rows, wide3), bf16), VM),
            (half, VM),
            (jax.ShapeDtypeStruct((1, wide3), f32), VM),
        ]
        + [(piece, VM)] * pieces,
        [],
        16,
        (lengths, qkv, do, stats, at),
        "attend_back",
        after,
    )


def start_back_body(counts, who, len_ref, d0, d1, d2, xb_ref, dy_ref, mark_ref, vec_ref, gb0, gb1, gb2, mid_ref, bd_ref, bu0, bu1, *rest):
    shards, (out_ref, gv_ref, w_ref, da_ref) = rest[:-4], rest[-4:]
    at = 0
    wide3 = d0.shape[1]
    acc = None
    for group, d in enumerate((d0, d1, d2)):
        gather_rows(who, shards[at : at + counts[group]], w_ref.at[group])
        at += counts[group]
        part = dot(d[...], w_ref[group], NT)
        acc = part if acc is None else acc + part
    da_ref[...] = acc
    gain_grad = shift_grad = embed_grad = jnp.zeros((1, xb_ref.shape[1]), f32)
    for item in range(out_ref.shape[0]):
        rows = slice(item * PAD, (item + 1) * PAD)
        da = da_ref[rows, :]
        unit, factor = unit_rows(xb_ref[rows, :].astype(f32))
        gain_grad += jnp.sum(da * unit, axis=0, keepdims=True)
        shift_grad += jnp.sum(da, axis=0, keepdims=True)
        dx = dy_ref[rows, :] + unit_back(da, unit, factor, vec_ref[0:1, :])
        marked = spread_rows(chosen_rows(mark_ref[item], len_ref[item]), dx.shape[1])
        text = dx[:TXT]
        embed_grad += jnp.sum(jnp.where(marked, text, 0.0), axis=0, keepdims=True)
        out_ref[item] = jnp.concatenate([jnp.where(marked, 0.0, text), dx[TXT:SEQ]], axis=0)
    wide, width = GROUP * HEAD, gv_ref.shape[1]
    gv_ref[...] = jnp.zeros_like(gv_ref)
    gv_ref[0:1, :] = gain_grad
    gv_ref[1:2, :] = shift_grad
    for group, gb in enumerate((gb0, gb1, gb2)):
        gv_ref[2:3, group * wide : (group + 1) * wide] = gb[:, :wide]
        gv_ref[3:4, group * wide : (group + 1) * wide] = gb[:, 2 * wide :]
    gv_ref[4:5, :] = mid_ref[2:3, :]
    gv_ref[5:7, :] = mid_ref[0:2, :]
    gv_ref[7:8, :] = bd_ref[...]
    for row, (ref, place) in enumerate(((bu0, 0), (bu0, 1), (bu1, 0), (bu1, 1))):
        gv_ref[8 + row : 9 + row, :] = ref[:, place * width : (place + 1) * width]
    gv_ref[12:13, :] = embed_grad


def start_back(who, lengths, grads, weights, xb, dy, marks, vecs, sums, after):
    rows, width = xb.shape
    wide3 = grads[0].shape[1]
    specs, arrays = shard_specs([w for ws in weights for w in ws], wide3, lambda i: 0)
    out = far_mem((rows // PAD, SEQ, width), f32)
    small = jax.ShapeDtypeStruct((16, width), f32)
    return call(
        functools.partial(start_back_body, [len(ws) for ws in weights]),
        (1,),
        [SM, SM] + [whole(v.shape) for v in (*grads, xb, dy, marks, vecs, *sums)] + specs,
        [(out, whole(out.shape)), (small, whole(small.shape))],
        [pltpu.VMEM((len(weights), width, wide3), bf16), pltpu.VMEM((rows, width), f32)],
        28,
        (who, lengths, *grads, afar(xb), afar(dy), marks, vecs, *sums, *arrays),
        "start_back",
        after,
    )


def finish_body(counts, who, y_ref, vec_ref, *rest):
    parts = len(counts)
    gelus, rest = rest[:parts], rest[parts:]
    shards, (out_ref, token, acc_ref, *w_refs) = rest[: sum(counts)], rest[sum(counts) :]
    token[...] = jnp.zeros(TOKEN, f32)
    step = pl.program_id(0)

    @pl.when(step == 0)
    def _():
        acc_ref[...] = y_ref[...] + vec_ref[7:8, :]

    at = 0
    total = acc_ref[...]
    for gelu, count, w_ref in zip(gelus, counts, w_refs):
        gather_rows(who, shards[at : at + count], w_ref)
        total += dot(gelu[...], w_ref[...], NT)
        at += count
    acc_ref[...] = total

    @pl.when(step == pl.num_programs(0) - 1)
    def _():
        for item in range(out_ref.shape[0]):
            out_ref[item] = acc_ref[item * PAD : (item + 1) * PAD, :].astype(bf16)[:SEQ]


def finish(who, y, gelus, downs, vecs, after):
    rows, width = y.shape
    step = 768
    out = far_mem((rows // PAD, SEQ, width), bf16)
    views = [shard_specs([(v, at * TILE // step) for v, at in down], step, lambda i: i) for down in downs]
    return call(
        functools.partial(finish_body, [len(down) for down in downs]),
        (gelus[0].shape[1] // step,),
        [SM] + wholes(y, vecs)
        + [pl.BlockSpec((rows, step), lambda i: (0, i)) for _ in gelus]
        + [spec for specs, _ in views for spec in specs],
        [(out, whole(out.shape)), (jax.ShapeDtypeStruct(TOKEN, f32), whole(TOKEN))],
        [pltpu.VMEM((rows, width), f32)] + [pltpu.VMEM((width, step), bf16)] * len(gelus),
        32,
        (who, afar(y), vecs, *gelus, *[v for _, arrays in views for v in arrays]),
        "finish",
        after,
    )


def swap(value, axis, bit):
    size = lax.axis_size(axis)
    return lax.ppermute(value, axis, [(i, i ^ (1 << bit)) for i in range(size)])


def half_of(value, which, dim):
    size = value.shape[dim] // 2
    return lax.dynamic_slice_in_dim(value, which * size, size, dim)


def plus(*arrays):
    return functools.reduce(lambda a, b: a + b, (v.astype(f32) for v in arrays))


TOKEN = (8, 128)


def step_call(body, ins, shapes, name, after):
    outs = [(near_mem(shape, dtype), VM) for shape, dtype in shapes]
    outs.append((near_mem(TOKEN, f32), VM))
    return call(body, None, [VM] * len(ins), outs, [], 8, [near(v) for v in ins], name, after, flops=10**4)


def paired(counts, refs):
    at = 0
    for count in counts:
        got = [ref[...] for ref in refs[at + 1 : at + 1 + count]]
        yield refs[at], got[0] if count == 1 else jnp.concatenate(got, axis=0)
        at += 1 + count


def first_body(counts, *refs):
    out = refs[-1]
    half = out.shape[1]
    for one, (keep, got) in enumerate(paired(counts, refs[:-1])):
        out[one] = plus(keep[half:], got[half:]).astype(bf16)


def second_body(counts, *refs):
    back, send, mine = refs[-3:]
    half = send.shape[1]
    for one, (keep, got) in enumerate(paired(counts, refs[:-3])):
        mine[one] = plus(keep[:half], got[:half], back[one, :half])
        send[one] = plus(keep[half : 2 * half], got[half : 2 * half], back[one, half:]).astype(bf16)


def third_body(keep, got, send, mine):
    half = send.shape[1]
    mine[...] = plus(keep[:, :half], got[:, :half])
    send[...] = plus(keep[:, half:], got[:, half:]).astype(bf16)


def add_body(one, two, out):
    out[...] = plus(one[...], two[...]).astype(out.dtype)


def join_body(mine, got, out):
    half = mine.shape[1]
    out[:, :half] = mine[...]
    out[:, half:] = got[...]


def cross(value, swapped):
    size, shards = lax.axis_size("dp") * lax.axis_size("fsdp"), lax.axis_size("fsdp")
    flip = lambda i: 2 if (i & 1) == swapped else shards
    return lax.ppermute(value, ("dp", "fsdp"), [(i, i ^ flip(i)) for i in range(size)])


def slot(tasks, *after):
    counts = [(len(ins), len(shapes)) for _, _, ins, shapes in tasks]

    def body(*refs):
        at, to = 0, sum(n for n, _ in counts)
        for (_, step, _, _), (n, m) in zip(tasks, counts):
            step(*refs[at : at + n], *refs[to : to + m])
            at, to = at + n, to + m
        refs[-1][...] = jnp.zeros(TOKEN, f32)

    ins = [v for task in tasks for v in task[2]]
    shapes = [v for task in tasks for v in task[3]]
    *results, token = step_call(body, ins, shapes, "slot", after)
    done = [token]
    for (owner, _, _, _), (_, m) in zip(tasks, counts):
        owner.out, *rest = results[:m]
        owner.mine = rest[0] if rest else owner.out
        results = results[m:]
    return done


class Chunk:
    def __init__(self, keeps, sends):
        self.counts = [len(s) for s in sends]
        self.pairs = [w for k, s in zip(keeps, sends) for w in (k, *[swap(v, "fsdp", 0) for v in s])]
        self.shape = (len(keeps), keeps[0].shape[0], keeps[0].shape[1])

    def task(self, body, ins, outs):
        count, rows, cols = self.shape
        return self, body, ins, [((count, rows // parts, cols), dtype) for parts, dtype in outs]

    def first(self):
        return self.task(functools.partial(first_body, self.counts), self.pairs, [(2, bf16)])

    def second(self):
        return self.task(functools.partial(second_body, self.counts), [*self.pairs, cross(self.out, 0)], [(4, bf16), (4, f32)])

    def third(self):
        return self.task(third_body, [self.mine, cross(self.out, 1)], [(8, bf16), (8, f32)])

    def rest(self):
        return self.task(add_body, [self.mine, swap(self.out, "dp", 1)], [(8, bf16)])

    def part(self):
        last = lax.axis_size("dp").bit_length() - 2
        for bit in range(2, last):
            slot([self.task(add_body, [self.out, swap(self.out, "dp", bit)], [(8, bf16)])])
        return self.task(add_body, [self.out, swap(self.out, "dp", last)], [(8, bf16)])

    def half(self):
        return self.task(join_body, [self.out, swap(self.out, "dp", 1)], [(4, bf16)])

    def halves(self):
        return self.out, swap(self.out, "dp", 0)


class Rows:
    def __init__(self, value):
        self.out = value
        bits = lambda axis: range(lax.axis_size(axis).bit_length() - 1)
        self.left = [(axis, bit) for axis in ("fsdp", "dp") for bit in bits(axis)]

    def pair(self):
        axis, bit = self.left.pop(0)
        return [self.out, swap(self.out, axis, bit)]

    def step(self):
        return self, add_body, self.pair(), [(self.out.shape, f32)]

    def last(self):
        while len(self.left) > 1:
            slot([self.step()])
        return self.pair()


def adam_body(chained, who, mine, got, first, second, weight, *rest):
    first_new, second_new, update, sums = rest[-4:]
    half = mine.shape[1] // 2
    low, mid = who[1] == 0, who[2] == 0
    rows = []
    for ref in (mine, got):
        a, b = ref[0, :half].astype(f32), ref[0, half:].astype(f32)
        rows.append((jnp.where(mid, a, b), jnp.where(mid, b, a)))
    near_rows, other_rows = rows
    grad = [jnp.where(low, a, b) for a, b in zip(near_rows, other_rows)]
    grad += [jnp.where(low, b, a) for a, b in zip(near_rows, other_rows)]
    grad = jnp.concatenate(grad, axis=0)
    moved = adam_moments(grad, first[...], second[...])
    master = weight[...]
    first_new[...], second_new[...] = moved[0], moved[1]
    change = moved[2] + decay_rate * master
    update[...] = change

    @pl.when(pl.program_id(0) == 0)
    def _():
        sums[...] = jnp.zeros_like(sums)

    sums[0:1, :] += jnp.sum(master * master, axis=0, keepdims=True)
    sums[1:2, :] += jnp.sum(change * change, axis=0, keepdims=True)


def adam(who, halves, first, second, weight, wide, steps, grad_at, column_at, made, after):
    rows = weight.shape[0]
    grad = pl.BlockSpec((1, rows // 2, wide), lambda i: (grad_at(i)[0], 0, grad_at(i)[1]))
    block = pl.BlockSpec((rows, wide), lambda i: (0, column_at(i)))
    full = jax.ShapeDtypeStruct(weight.shape, f32)
    sums = jax.ShapeDtypeStruct((2, wide), f32)
    made = list(made or [])
    return call(
        functools.partial(adam_body, len(made)),
        (steps,),
        [SM, grad, grad, block, block, block] + [pl.BlockSpec(memory_space=pl.ANY)] * len(made),
        [(full, block), (full, block), (full, block), (sums, whole(sums.shape))],
        [],
        14,
        (who, *halves, first, second, weight, *made),
        "adam",
        after,
        {6 + k: k for k in range(len(made))},
    )


def total_body(*refs):
    *parts, out = refs
    for row, group in enumerate(parts_of(parts)):
        for kind in range(2):
            value = sum(jnp.sum(ref[kind : kind + 1, :]) for ref in group)
            out[4 * kind + row : 4 * kind + row + 1, :] = jnp.full((1, out.shape[1]), value, f32)


def parts_of(parts):
    return parts[0:2], parts[2:3], parts[3:5], parts[5:7]


def totals(sums):
    out = jax.ShapeDtypeStruct((8, 128), f32)
    return call(total_body, None, [VM] * len(sums), [(out, VM)], [], 8, tuple(sums), "totals")[0]


def apply_body(one, two, w0, w1, w2, w3, u0, u1, u2, u3, n0, n1, n2, n3, norms):
    total = one[...] + two[...]
    norms[...] = jnp.sqrt(total)
    for row, (w, u, n) in enumerate(((w0, u0, n0), (w1, u1, n1), (w2, u2, n2), (w3, u3, n3))):
        ratio = jnp.sqrt(total[row : row + 1, :1]) * lax.rsqrt(total[4 + row : 5 + row, :1] + adam_eps)
        n[...] = w[...] - (matrix_rate * ratio) * u[...]


def apply(one, two, weights, updates):
    steps = 3
    blocks = [pl.BlockSpec((w.shape[0], w.shape[1] // steps), lambda i: (0, i)) for w in weights]
    norms = jax.ShapeDtypeStruct(one.shape, f32)
    return call(
        apply_body,
        (steps,),
        [whole(one.shape)] * 2 + blocks + blocks,
        [(jax.ShapeDtypeStruct(w.shape, f32), b) for w, b in zip(weights, blocks)] + [(norms, whole(one.shape))],
        [],
        24,
        (one, two, *weights, *updates),
        "apply",
    )


def vector_body(who, one, two, first, second, params, new, first_new, second_new):
    rows, cols = params.shape
    total = one[...] + two[...]
    grad = total[:rows, :cols]
    for block in range(1, 4):
        grad = jnp.where(who[0] == block, total[:rows, block * cols : (block + 1) * cols], grad)
    moved = adam_moments(grad, first[...], second[...])
    first_new[...], second_new[...] = moved[0], moved[1]
    new[...] = params[...] - vector_rate * moved[2]


def vector_step(who, one, two, first, second, params):
    out = jax.ShapeDtypeStruct(params.shape, f32)
    args = (who, one, two, first, second, params)
    return call(vector_body, None, [SM] + [VM] * 5, [(out, VM)] * 3, [], 8, args, "vector_step")


def adam_moments(grad, first, second):
    first_new = beta_one * first + (1.0 - beta_one) * grad
    second_new = beta_two * second + (1.0 - beta_two) * grad * grad
    direction = (
        first_new
        / (1.0 - beta_one**STEP)
        / (jnp.sqrt(second_new / (1.0 - beta_two**STEP)) + adam_eps)
    )
    return (first_new, second_new, direction)


def local(
    block_in,
    out_grad,
    caption_len,
    mask_marks,
    qkv_weight,
    out_weight,
    up_weight,
    down_weight,
    vector_params,
    qkv_first,
    qkv_second,
    out_first,
    out_second,
    up_first,
    up_second,
    down_first,
    down_second,
    vector_first,
    vector_second,
):
    width = block_in.shape[2]
    hidden = up_weight.shape[1]
    groups = width // (GROUP * HEAD)
    shard = lax.axis_index("fsdp")
    replica = lax.axis_index("dp")
    who = jnp.stack([shard, replica & 1, (replica >> 1) & 1]).astype(jnp.int32)
    cols = hidden // PARTS
    core = lambda v: swap(v, "fsdp", 0)
    far = lambda v: swap(v, "fsdp", 1)
    turned = lambda v: v.T

    own_one, own_more = cast_heads(qkv_weight, vector_params)
    far_one, far_more = far(own_one), far(own_more)
    own_out, half_up, half_down, *own_parts = cast_rest(who, out_weight.T, up_weight, down_weight.T, [own_one])
    far_one = tie(far_one, own_out)
    far_out, far_up, far_down, far_part = (far(v) for v in (own_out, half_up, half_down, own_parts[2]))
    core_parts = [core(v) for v in own_parts]
    first_block = lambda *arrays: [(v, 0) for v in arrays]
    one_shards = (own_one, core(own_one), far_one, core(far_one))
    out_full = first_block(own_out, core(own_out), far_out, core(far_out))

    marks = mask_marks.reshape(*mask_marks.shape, 1)
    vecs, xb, a = prep(who, caption_len, block_in, marks, one_shards, [])
    dm, dmt, grad_bd = prep_grad(who, out_grad, [vecs])
    far_more = tie(far_more, grad_bd)
    more_shards = (own_more, core(own_more), far_more, core(far_more))
    heads_full = [first_block(*one_shards)] + [[(v, g) for v in more_shards] for g in range(groups - 1)]
    sides = lambda mine: (mine, swap(mine, "dp", 0))
    heads = [attend(who, caption_len, a, heads_full[0], vecs, 0, [far_more, grad_bd])]
    up_far = sides(tie(far_up, heads[0][2]))
    heads.append(attend(who, caption_len, a, heads_full[1], vecs, 1, [heads[0][2], up_far[0]]))
    down_far = sides(tie(far_down, heads[1][2]))
    heads.append(attend(who, caption_len, a, heads_full[2], vecs, 2, [heads[1][2], down_far[0], up_far[1]]))
    outs = [h[1] for h in heads]
    y, c, ct = mix(who, xb, outs, out_full, vecs, [down_far[1]])
    ups = first_block(own_parts[0], core_parts[0], *up_far, *(core(v) for v in up_far))
    downs = first_block(own_parts[1], core_parts[1], *down_far, *(core(v) for v in down_far))
    ffn0 = ffn(who, c, dm, ct, dmt, ups, downs, vecs, None, 0, [])
    chunk_a = Chunk([ffn0[0], ffn0[2]], [[ffn0[1]], [ffn0[3]]])
    at = turn_rows(who, a, [ffn0[5]])
    done = slot([chunk_a.first()], at)
    far_part = tie(far_part, ffn0[5])
    shards1 = (own_parts[2], core_parts[2], far_part, core(far_part))
    ups1 = first_block(*shards1)
    downs1 = [(v, cols // TILE) for v in shards1]
    ffn1 = ffn(who, c, dm, ct, dmt, ups1, downs1, vecs, ffn0[6], 1, done)
    chunk_b = Chunk([ffn1[0], ffn1[2]], [[ffn1[1]], [ffn1[3]]])
    done = slot([chunk_a.second()], ffn1[5])
    done = slot([chunk_b.first()], *done)
    dy, out_keep, out_send, *dos, grad_mid = turn(who, ffn1[6], y, dm, outs, out_full, vecs, done)
    done = slot([chunk_a.third()], grad_mid)
    back0 = attend_back(caption_len, heads[0][0], dos[0], heads[0][2], at, 1, done)
    chunk_c = Chunk([out_keep, back0[1]], [[out_send], back0[3:]])
    done = slot([chunk_b.second(), chunk_a.rest()], back0[2])
    back1 = attend_back(caption_len, heads[1][0], dos[1], heads[1][2], at, 1, done)
    done = slot([chunk_b.third(), chunk_c.first()], back1[2])
    back2 = attend_back(caption_len, heads[2][0], dos[2], heads[2][2], at, 3, done)
    backs = [back0, back1, back2]
    chunk_d = Chunk([back1[1], back2[1]], [back1[3:], back2[3:]])
    done = slot([chunk_b.rest(), chunk_a.part(), chunk_c.second()], back2[2])
    done = slot([chunk_d.first()], *done)
    sums = [b[2] for b in backs] + [grad_mid, grad_bd, ffn0[5], ffn1[5]]
    input_grad, vector_grads = start_back(
        who, caption_len, [b[0] for b in backs], heads_full, xb, dy, marks, vecs, sums, done
    )
    rows = Rows(vector_grads)
    done = slot([chunk_a.half(), chunk_c.third(), chunk_d.second()], vector_grads)
    block_out, token = finish(who, y, [ffn0[4], ffn1[4]], [downs, downs1], vecs, done)

    qkv = (qkv_first, qkv_second, qkv_weight)
    out = tuple(turned(v) for v in (out_first, out_second, out_weight))
    up = (up_first, up_second, up_weight)
    down = tuple(turned(v) for v in (down_first, down_second, down_weight))
    wide = 2 * TILE
    per = cols // wide
    done = slot([chunk_b.part(), chunk_c.rest(), chunk_d.third(), rows.step()], token)
    halves_a = chunk_a.halves()
    up_made = adam(who, halves_a, *up, wide, per, lambda i: (0, i), lambda i: i, None, done)
    done = slot([chunk_b.half(), chunk_d.rest(), rows.step()], up_made[3])
    down_made = adam(who, halves_a, *down, wide, per, lambda i: (1, i), lambda i: i, None, done)
    done = slot([chunk_c.part(), rows.step()], down_made[3])
    done = slot([chunk_c.half(), chunk_d.part(), rows.step()], *done)
    halves_b = chunk_b.halves()
    up_last = adam(who, halves_b, *up, wide, per, lambda i: (0, i), lambda i: per + i, up_made[:3], done)
    done = slot([chunk_d.half()], up_last[3])
    down_last = adam(who, halves_b, *down, wide, per, lambda i: (1, i), lambda i: per + i, down_made[:3], done)
    halves_c = chunk_c.halves()
    out_made = adam(who, halves_c, *out, TILE, width // TILE, lambda i: (0, i), lambda i: i, None, [down_last[3]])
    qkv_made = adam(who, halves_c, *qkv, TILE, 3, lambda i: (1, i), lambda i: groups * i, None, [out_made[3]])
    vector_one, got = rows.last()
    qkv_last = adam(
        who,
        chunk_d.halves(),
        *qkv,
        TILE,
        3 * (groups - 1),
        lambda i: (i // 3, i % 3),
        lambda i: groups * (i % 3) + 1 + i // 3,
        qkv_made[:3],
        [qkv_made[3]],
    )
    vector_new, vector_first_new, vector_second_new = vector_step(
        who, vector_one, got, vector_first, vector_second, vector_params
    )
    squares = totals([qkv_made[3], qkv_last[3], out_made[3], up_made[3], up_last[3], down_made[3], down_last[3]])
    squares = squares + core(squares)
    weights = (qkv_weight, out[2], up_weight, down[2])
    made = (qkv_last, out_made, up_last, down_last)
    *new_weights, norms = apply(squares, far(squares), weights, [m[2] for m in made])
    back = (lambda v: v, turned, lambda v: v, turned)
    moments = [f(m[k]) for f, m in zip(back, made) for k in range(2)]
    return (
        block_out,
        input_grad,
        *(f(w) for f, w in zip(back, new_weights)),
        vector_new,
        *moments,
        vector_first_new,
        vector_second_new,
        norms[:, 0].reshape(2, 4),
    )


def solution(mesh):
    placed = (
        P(("dp", "fsdp"), None, None),
        P(("dp", "fsdp"), None, None),
        P(("dp", "fsdp")),
        P(("dp", "fsdp"), None),
        P("fsdp", None),
        P(None, "fsdp"),
        P("fsdp", None),
        P(None, "fsdp"),
        P(None, "fsdp"),
        P("fsdp", None),
        P("fsdp", None),
        P(None, "fsdp"),
        P(None, "fsdp"),
        P("fsdp", None),
        P("fsdp", None),
        P(None, "fsdp"),
        P(None, "fsdp"),
        P(None, "fsdp"),
        P(None, "fsdp"),
    )
    return jax.shard_map(
        local,
        mesh=mesh,
        in_specs=placed,
        out_specs=(
            P(("dp", "fsdp"), None, None),
            P(("dp", "fsdp"), None, None),
            P("fsdp", None),
            P(None, "fsdp"),
            P("fsdp", None),
            P(None, "fsdp"),
            P(None, "fsdp"),
            P("fsdp", None),
            P("fsdp", None),
            P(None, "fsdp"),
            P(None, "fsdp"),
            P("fsdp", None),
            P("fsdp", None),
            P(None, "fsdp"),
            P(None, "fsdp"),
            P(None, "fsdp"),
            P(None, "fsdp"),
            P(),
        ),
        check_vma=False,
    )
```

```python
import functools

import jax
import jax.numpy as jnp
from jax import lax
from jax.experimental import pallas as pl
from jax.experimental.pallas import tpu as pltpu
from jax.sharding import PartitionSpec as P

HEAD = 64
TXT = 40
PATCH = 145
STEP = 7
SEQ = TXT + PATCH
PAD = 192
GROUP = 4
PARTS = 2
EXTRA = 16
LIGHT = 10**4
TILE = 256
BLOCK = 768

ln_eps = 1e-06
beta_one = 0.5
beta_two = 0.55
adam_eps = 1e-06
decay_rate = 0.01
matrix_rate = 0.5
vector_rate = 0.3

f32 = jnp.float32
bf16 = jnp.bfloat16
ORDER = (0, 2, 1, 3)
NT = (((1,), (1,)), ((), ()))
TN = (((0,), (0,)), ((), ()))

VM = pl.BlockSpec(memory_space=pltpu.VMEM)
SM = pl.BlockSpec(memory_space=pltpu.SMEM)


def dot(left, right, dims=None):
    if dims is None:
        return jnp.dot(left, right, preferred_element_type=f32)
    return lax.dot_general(left, right, dims, preferred_element_type=f32)


def call(body, grid, ins, outs, scratch, limit, args, name, after=(), aliases=None, flops=8 * 10**9):
    count = len(ins)
    after = [afar(v) if v.size > 65536 else v for v in after]

    def run(*refs):
        body(*refs[:count], *refs[count + len(after) :])

    return pl.pallas_call(
        run,
        grid=grid or (),
        in_specs=list(ins) + [pl.BlockSpec(memory_space=pl.ANY)] * len(after),
        out_specs=[o[1] for o in outs],
        out_shape=[o[0] for o in outs],
        input_output_aliases=aliases or {},
        scratch_shapes=scratch,
        compiler_params=pltpu.CompilerParams(vmem_limit_bytes=limit << 20),
        cost_estimate=pl.CostEstimate(flops=flops, bytes_accessed=flops // 200, transcendentals=0),
        name=name,
    )(*args, *after)


def far_mem(shape, dtype):
    return pltpu.HBM(tuple(shape), dtype)


def near_mem(shape, dtype):
    return pltpu.VMEM(tuple(shape), dtype)


def near(value):
    return pltpu.with_memory_space_constraint(value, pltpu.VMEM)


def afar(value):
    return pltpu.with_memory_space_constraint(value, pltpu.HBM)


def tie(value, *deps):
    return pl.pallas_call(
        lambda *refs: None,
        in_specs=[pl.BlockSpec(memory_space=pl.ANY)] * (1 + len(deps)),
        out_specs=pl.BlockSpec(memory_space=pl.ANY),
        out_shape=jax.ShapeDtypeStruct(value.shape, value.dtype),
        input_output_aliases={0: 0},
        cost_estimate=pl.CostEstimate(flops=LIGHT, bytes_accessed=LIGHT, transcendentals=0),
        name="tie",
    )(value, *[afar(v) if v.size > 65536 else v for v in deps])


def whole(shape):
    return pl.BlockSpec(shape, lambda i: (0,) * len(shape), pipeline_mode=pl.Buffered(1))


def wholes(*arrays):
    return [whole(v.shape) for v in arrays]


def shard_specs(shards, wide, columns):
    rows = lambda v: v.shape[0] - v.shape[0] % 96
    specs = [pl.BlockSpec((rows(v), wide), lambda i, at=at: (0, at + columns(i))) for v, at in shards]
    return specs, [afar(v) for v, _ in shards]


def unit_rows(rows):
    centred = rows - jnp.mean(rows, axis=-1, keepdims=True)
    factor = lax.rsqrt(jnp.mean(centred * centred, axis=-1, keepdims=True) + ln_eps)
    return centred * factor, factor


def unit_back(grad_normed, unit, factor, gain):
    grad_unit = grad_normed * gain
    return factor * (
        grad_unit
        - jnp.mean(grad_unit, axis=-1, keepdims=True)
        - unit * jnp.mean(grad_unit * unit, axis=-1, keepdims=True)
    )


def put_turned(who_ref, value, scratch, out_ref):
    part = out_ref.shape[0] // 16
    scratch[...] = value.T
    for place in range(16):
        core, one, two, three = (place >> 3) & 1, (place >> 2) & 1, (place >> 1) & 1, place & 1
        odd = (who_ref[0] & 1) ^ core
        pair = jnp.where(odd == 0, one, two)
        low = jnp.where(odd == 0, two, one)
        start = 4 * (who_ref[0] ^ (2 * pair + core)) + 2 * (who_ref[1] ^ low) + (who_ref[2] ^ three)
        out_ref[place * part : (place + 1) * part, :] = scratch[pl.ds(pl.multiple_of(start * part, 16), part), :]


def gather_rows(who_ref, refs, out_ref):
    rows = refs[0].shape[0]
    half = rows // 2
    places = [(0, None), (1, None)]
    places += [(2, None), (3, None)] if len(refs) == 4 else [(2, 0), (2, 1), (3, 0), (3, 1)]
    for (other, part), ref in zip(places, refs):
        start = (who_ref[0] ^ other) * rows
        if part is not None:
            start += (who_ref[1] ^ part) * half
        out_ref[pl.ds(pl.multiple_of(start, 32), ref.shape[0]), :] = ref[...]


def cast_heads_body(q_ref, k_ref, v_ref, vec_ref, one_ref, rest_ref):
    wide = GROUP * HEAD
    rows = q_ref.shape[0]
    step = pl.program_id(0)

    @pl.when(step == 0)
    def _():
        for kind, ref in enumerate((q_ref, k_ref, v_ref)):
            one_ref[:rows, kind * wide : (kind + 1) * wide] = ref[...].astype(bf16)
        count, cols = vec_ref.shape
        one_ref[rows:, :] = jnp.zeros_like(one_ref[rows:, :])
        one_ref[rows : rows + count, :cols] = vec_ref[...].astype(bf16)

    @pl.when(step > 0)
    def _():
        for kind, ref in enumerate((q_ref, k_ref, v_ref)):
            at = pl.multiple_of(((step - 1) * 3 + kind) * wide, wide)
            rest_ref[:, pl.ds(at, wide)] = ref[...].astype(bf16)


def cast_heads(weight, vectors):
    rows, cols = weight.shape
    wide = GROUP * HEAD
    groups = cols // (3 * wide)
    blocks = [pl.BlockSpec((rows, wide), lambda i, kind=kind: (0, kind * groups + i)) for kind in range(3)]
    shapes = [(rows + EXTRA, 3 * wide), (rows, 3 * wide * (groups - 1))]
    outs = [(far_mem(shape, bf16), whole(shape)) for shape in shapes]
    args = (*[afar(weight)] * 3, vectors)
    return call(cast_heads_body, (groups,), blocks + wholes(vectors), outs, [], 12, args, "cast_heads")


def cast_rest_body(who, out_ref, up_ref, down_ref, o_ref, up_half, down_half, *parts):
    half = up_half.shape[0]
    rows = pl.ds(pl.multiple_of(who[1] * half, 32), half)
    step = pl.program_id(0)
    per = pl.num_programs(0) // PARTS

    @pl.when(step == 0)
    def _():
        o_ref[...] = out_ref[...].astype(bf16)

    @pl.when(step < per)
    def _():
        up_half[...] = up_ref[rows, :].astype(bf16)
        down_half[...] = down_ref[rows, :].astype(bf16)

    @pl.when(step < per)
    def _():
        parts[0][...] = up_ref[...].astype(bf16)
        parts[1][...] = down_ref[...].astype(bf16)

    wide = up_ref.shape[1]
    for place in range(per):

        @pl.when(step == per + place)
        def _(place=place):
            parts[2][:, place * wide : (place + 1) * wide] = up_ref[...].astype(bf16)
            parts[2][:, (per + place) * wide : (per + place + 1) * wide] = down_ref[...].astype(bf16)


def cast_rest(who, out_t, up, down_t, after):
    rows, hidden = up.shape
    cols, wide = hidden // PARTS, 768
    per = cols // wide
    block = pl.BlockSpec((rows, wide), lambda i: (0, i))
    at = lambda part: lambda i: (0, jnp.clip(i - part * per, 0, per - 1))
    out = lambda n, part: (far_mem((n, cols), bf16), pl.BlockSpec((n, wide), at(part)))
    outs = [(far_mem(out_t.shape, bf16), whole(out_t.shape)), out(rows // 2, 0), out(rows // 2, 0)]
    both = (rows, 2 * cols)
    outs += [out(rows, 0), out(rows, 0), (far_mem(both, bf16), whole(both))]
    ins = [SM] + wholes(out_t) + [block, block]
    args = (who, out_t, afar(up), afar(down_t))
    return call(cast_rest_body, (hidden // wide,), ins, outs, [], 16, args, "cast_rest", after)


def chosen_rows(marks, length):
    places = lax.broadcasted_iota(jnp.int32, marks.shape, 0)
    return jnp.where((marks == 1) & (places >= 1) & (places < length), 1.0, 0.0)


def spread_rows(chosen, width):
    return jnp.broadcast_to(chosen, (chosen.shape[0], width)) > 0


def prep_grad_body(who, g_ref, dm_ref, dmt_ref, bd_ref, all_ref, scratch):
    step = pl.program_id(0)
    tail = jnp.zeros((PAD - SEQ, g_ref.shape[2]), f32)
    dm = jnp.concatenate([g_ref[0].astype(f32), tail], axis=0)
    dm_ref[...] = dm.astype(bf16)
    all_ref[pl.ds(pl.multiple_of(step * PAD, PAD), PAD), :] = dm.astype(bf16)

    @pl.when(step == 0)
    def _():
        bd_ref[...] = jnp.zeros_like(bd_ref)

    bd_ref[...] += jnp.sum(dm, axis=0, keepdims=True)

    @pl.when(step == pl.num_programs(0) - 1)
    def _():
        put_turned(who, all_ref[...], scratch, dmt_ref)


def prep_grad(who, out_grad, after):
    items, seq, width = out_grad.shape
    rows = items * PAD
    item = pl.BlockSpec((1, seq, width), lambda i: (i, 0, 0))
    return call(
        prep_grad_body,
        (items,),
        [SM, item],
        [
            (far_mem((rows, width), bf16), pl.BlockSpec((PAD, width), lambda i: (i, 0))),
            (far_mem((width, rows), bf16), whole((width, rows))),
            (jax.ShapeDtypeStruct((1, width), f32), whole((1, width))),
        ],
        [pltpu.VMEM((rows, width), bf16), pltpu.VMEM((width, rows), bf16)],
        20,
        (who, afar(out_grad)),
        "prep_grad",
        after,
        flops=LIGHT,
    )


def prep_body(who, len_ref, x_ref, mark_ref, v0, v1, v2, v3, vec_ref, xb_ref, a_ref):
    step = pl.program_id(0)
    width = x_ref.shape[2]

    @pl.when(step == 0)
    def _():
        cols = width // 4
        for block in range(4):
            value = v0[:, :cols].astype(f32)
            for other, ref in ((1, v1), (2, v2), (3, v3)):
                value = jnp.where((who[0] ^ other) == block, ref[:, :cols].astype(f32), value)
            vec_ref[:, block * cols : (block + 1) * cols] = value

    gain, shift, embed = vec_ref[0:1, :], vec_ref[1:2, :], vec_ref[12:13, :]
    x = x_ref[0].astype(f32)
    marked = spread_rows(chosen_rows(mark_ref[0], len_ref[step]), width)
    tail = jnp.zeros((PAD - SEQ, width), f32)
    x = jnp.concatenate([jnp.where(marked, embed, x[:TXT]), x[TXT:], tail], axis=0)
    xb_ref[...] = x.astype(bf16)
    unit, _ = unit_rows(x)
    a_ref[...] = (unit * gain + shift).astype(bf16)


def turn_rows_body(who, a_ref, at_ref, scratch):
    put_turned(who, a_ref[...], scratch, at_ref)


def turn_rows(who, a, after):
    rows, width = a.shape
    out = (far_mem((width, rows), bf16), whole((width, rows)))
    scratch = [pltpu.VMEM((width, rows), bf16)]
    return call(turn_rows_body, (1,), [SM] + wholes(a), [out], scratch, 16, (who, afar(a)), "turn_rows", after)[0]


def prep(who, lengths, block_in, marks, vec_shards, after):
    items, seq, width = block_in.shape
    rows = items * PAD
    item = lambda *shape: pl.BlockSpec((1, *shape), lambda i: (i, 0, 0))
    flat = pl.BlockSpec((PAD, width), lambda i: (i, 0))
    extra = pl.BlockSpec((EXTRA, width), lambda i: (vec_shards[0].shape[0] // EXTRA - 1, 0))
    return call(
        prep_body,
        (items,),
        [SM, SM, item(seq, width), item(*marks.shape[1:])] + [extra] * 4,
        [
            (near_mem((16, width), f32), whole((16, width))),
            (far_mem((rows, width), bf16), flat),
            (far_mem((rows, width), bf16), flat),
        ],
        [],
        16,
        (who, lengths, afar(block_in), marks, *[afar(v) for v in vec_shards]),
        "prep",
        after,
        flops=LIGHT,
    )


def key_mask(length):
    places = lax.broadcasted_iota(jnp.int32, (PAD, 1), 0)
    return ((places >= TXT) & (places < SEQ)) | (places < length)


def half_masks():
    lanes = lax.broadcasted_iota(jnp.int32, (1, 2 * HEAD), 1)
    low = jnp.where(lanes < HEAD, 1.0, 0.0)
    return low.astype(bf16), (1.0 - low).astype(bf16)


def scaled_masks():
    return [(mask.astype(f32) * HEAD ** (-0.5)).astype(bf16) for mask in half_masks()]


def attend_body(group, who, len_ref, a_ref, vec_ref, *rest):
    wide = GROUP * HEAD
    shards, (qkv_ref, o_ref, st_ref, w_ref) = rest[:-4], rest[-4:]
    gather_rows(who, shards, w_ref)
    cols = slice(group * wide, (group + 1) * wide)
    bias = jnp.concatenate([vec_ref[2:3, cols], jnp.zeros((1, wide), f32), vec_ref[3:4, cols]], axis=1)
    qkv_ref[...] = (dot(a_ref[...], w_ref[...]) + bias).astype(bf16)
    halves, scaled = half_masks(), scaled_masks()

    @pl.loop(0, len_ref.shape[0])
    def _(item):
        rows = pl.ds(pl.multiple_of(item * PAD, PAD), PAD)
        valid = key_mask(len_ref[item])
        for pair in range(GROUP // 2):
            at = pair * 2 * HEAD
            q = qkv_ref[rows, at : at + 2 * HEAD]
            k = qkv_ref[rows, wide + at : wide + at + 2 * HEAD]
            v = qkv_ref[rows, 2 * wide + at : 2 * wide + at + 2 * HEAD]
            out = None
            for half in range(2):
                s = dot(k * scaled[half], q, NT)
                s = jnp.where(valid, s, -1000000000.0)
                top = jnp.max(s, axis=0, keepdims=True)
                e = jnp.exp(s - top)
                scale = 1.0 / jnp.sum(e, axis=0, keepdims=True)
                p = (e * scale).astype(bf16)
                part = dot(p, v * halves[half], TN)
                out = part if out is None else out + part
                head = 2 * pair + half
                st_ref[item, head : head + 1, :] = top
                st_ref[item, GROUP + head : GROUP + head + 1, :] = scale
            o_ref[rows, at : at + 2 * HEAD] = out.astype(bf16)


def attend(who, lengths, a, weights, vecs, group, after):
    rows, width = a.shape
    wide = GROUP * HEAD
    items = lengths.shape[0]
    specs, arrays = shard_specs(weights, 3 * wide, lambda i: 0)
    return call(
        functools.partial(attend_body, group),
        (1,),
        [SM, SM, whole(a.shape), whole(vecs.shape)] + specs,
        [
            (far_mem((rows, 3 * wide), bf16), whole((rows, 3 * wide))),
            (far_mem((rows, wide), bf16), whole((rows, wide))),
            (far_mem((items, 2 * GROUP, PAD), f32), whole((items, 2 * GROUP, PAD))),
        ],
        [pltpu.VMEM((width, 3 * wide), bf16)],
        16,
        (who, lengths, afar(a), vecs, *arrays),
        "attend",
        after,
    )


def mix_body(who, x_ref, o0, o1, o2, vec_ref, *rest):
    shards, (y_ref, c_ref, ct_ref, w_ref, scratch) = rest[:-5], rest[-5:]
    gather_rows(who, shards, w_ref)
    wide = GROUP * HEAD
    acc = x_ref[...].astype(f32) + vec_ref[4:5, :]
    for group, o in enumerate((o0, o1, o2)):
        acc += dot(o[...], w_ref[:, group * wide : (group + 1) * wide], NT)
    y_ref[...] = acc
    unit, _ = unit_rows(acc)
    c_ref[...] = (unit * vec_ref[5:6, :] + vec_ref[6:7, :]).astype(bf16)
    put_turned(who, c_ref[...], scratch, ct_ref)


def mix(who, xb, outs, weights, vecs, after):
    rows, width = xb.shape
    specs, arrays = shard_specs(weights, width, lambda i: 0)
    return call(
        mix_body,
        (1,),
        [SM, whole(xb.shape)] + [whole(o.shape) for o in outs] + [whole(vecs.shape)] + specs,
        [
            (far_mem((rows, width), f32), whole((rows, width))),
            (near_mem((rows, width), bf16), whole((rows, width))),
            (near_mem((width, rows), bf16), whole((width, rows))),
        ],
        [pltpu.VMEM((width, width), bf16), pltpu.VMEM((width, rows), bf16)],
        18,
        (who, afar(xb), *[afar(o) for o in outs], vecs, *arrays),
        "mix",
        after,
    )


def item_rows(cols):
    return pl.BlockSpec((PAD, cols), lambda i: (i, 0))


def gelu_pair(h):
    bell = jnp.exp(-0.5 * h * h)
    t = 1.0 / (1.0 + (0.3275911 * 0.7071067811865476) * jnp.abs(h))
    poly = t * (0.127414796 + t * (-0.142248368 + t * (0.7107068705 + t * (-0.7265760135 + t * 0.5307027145))))
    tail = poly * bell
    return jnp.where(h < 0, tail, 1.0 - tail), bell


def ffn_body(counts, base, who, c_ref, dm_ref, ct_ref, dmt_ref, *rest):
    ups, downs, rest = rest[: counts[0]], rest[counts[0] : sum(counts)], rest[sum(counts) :]
    bu_ref, uk_ref, us_ref, dk_ref, ds_ref, gelu_ref, gbu_ref, dc_ref, up_w, down_w = rest

    @pl.when(pl.program_id(0) == 0)
    def _():
        dc_ref[...] = jnp.zeros_like(dc_ref)

    gather_rows(who, ups, up_w)
    gather_rows(who, downs, down_w)
    row = (base + pl.program_id(0)) // (c_ref.shape[1] // BLOCK)
    h = dot(c_ref[...], up_w[...]) + bu_ref[pl.ds(row, 1), :]
    phi, bell = gelu_pair(h)
    gelu = (h * phi).astype(bf16)
    gelu_ref[...] = gelu
    slope = phi + h * bell * 0.3989422804014327
    dh = (dot(dm_ref[...], down_w[...]) * slope).astype(bf16)
    gbu_ref[...] = jnp.sum(dh.astype(f32), axis=0, keepdims=True)
    half = uk_ref.shape[0]
    grad = dot(ct_ref[...], dh).astype(bf16)
    uk_ref[...], us_ref[...] = grad[:half], grad[half:]
    grad = dot(dmt_ref[...], gelu).astype(bf16)
    dk_ref[...], ds_ref[...] = grad[:half], grad[half:]
    dc_ref[...] += dot(dh, up_w[...], NT)


def ffn(who, c, dm, ct, dmt, ups, downs, vecs, part, after):
    rows, width = c.shape
    cols = 4 * width // PARTS
    base, across = part * cols // BLOCK, width // BLOCK
    up_specs, up_arrays = shard_specs(ups, BLOCK, lambda i: i)
    down_specs, down_arrays = shard_specs(downs, BLOCK, lambda i: i)
    half = near_mem((width // 2, cols), bf16)
    hspec = pl.BlockSpec((width // 2, BLOCK), lambda i: (0, i))
    return call(
        functools.partial(ffn_body, (len(ups), len(downs)), base),
        (cols // BLOCK,),
        [SM, whole(c.shape), whole(dm.shape), whole(ct.shape), whole(dmt.shape)]
        + up_specs
        + down_specs
        + [pl.BlockSpec((8, BLOCK), lambda i: (1, (base + i) % across))],
        [
            (half, hspec),
            (half, hspec),
            (half, hspec),
            (half, hspec),
            (far_mem((rows, cols), bf16), pl.BlockSpec((rows, BLOCK), lambda i: (0, i))),
            (jax.ShapeDtypeStruct((1, cols), f32), pl.BlockSpec((1, BLOCK), lambda i: (0, i))),
            (far_mem((rows, width), f32), whole((rows, width))),
        ],
        [pltpu.VMEM((width, BLOCK), bf16), pltpu.VMEM((width, BLOCK), bf16)],
        36,
        (who, c, dm, ct, dmt, *up_arrays, *down_arrays, vecs),
        "ffn",
        after,
    )


def turn_body(who, dc0_ref, dc1_ref, y_ref, dm_ref, o0, o1, o2, vec_ref, *rest):
    shards, rest = rest[:-11], rest[-11:]
    dy_ref, gk_ref, gs_ref, do0, do1, do2, gv_ref, w_ref, all_ref, scratch, drt_ref = rest
    step = pl.program_id(0)

    @pl.when(step == 0)
    def _():
        gather_rows(who, shards, w_ref)
        gv_ref[...] = jnp.zeros_like(gv_ref)

    wide = GROUP * HEAD
    here = pl.ds(pl.multiple_of(step * PAD, PAD), PAD)
    dc = dc0_ref[...] + dc1_ref[...]
    unit, factor = unit_rows(y_ref[...])
    gv_ref[0:1, :] += jnp.sum(dc * unit, axis=0, keepdims=True)
    gv_ref[1:2, :] += jnp.sum(dc, axis=0, keepdims=True)
    dy = dm_ref[...].astype(f32) + unit_back(dc, unit, factor, vec_ref[5:6, :])
    dy_ref[...] = dy
    dr = dy.astype(bf16)
    gv_ref[2:3, :] += jnp.sum(dr.astype(f32), axis=0, keepdims=True)
    all_ref[here, :] = dr

    @pl.when(step == pl.num_programs(0) - 1)
    def _():
        put_turned(who, all_ref[...], scratch, drt_ref)
        half = gk_ref.shape[0]
        for group, (o, do) in enumerate(((o0, do0), (o1, do1), (o2, do2))):
            cols = slice(group * wide, (group + 1) * wide)
            do[...] = dot(all_ref[...], w_ref[:, cols]).astype(bf16)
            grad = dot(drt_ref[...], o[...]).astype(bf16)
            gk_ref[:, cols] = grad[:half]
            gs_ref[:, cols] = grad[half:]


def turn(who, dcs, y, dm, outs, weights, vecs, after):
    rows, width = y.shape
    half = jax.ShapeDtypeStruct((width // 2, width), bf16)
    do = (jax.ShapeDtypeStruct((rows, GROUP * HEAD), bf16), whole((rows, GROUP * HEAD)))
    small = jax.ShapeDtypeStruct((3, width), f32)
    specs, arrays = shard_specs(weights, width, lambda i: 0)
    flat, across = pltpu.VMEM((rows, width), bf16), pltpu.VMEM((width, rows), bf16)
    return call(
        turn_body,
        (rows // PAD,),
        [SM] + [item_rows(width)] * 4 + wholes(*outs, vecs) + specs,
        [(far_mem((rows, width), f32), item_rows(width))]
        + [(half, whole(half.shape))] * 2
        + [do] * 3
        + [(small, whole(small.shape))],
        [pltpu.VMEM((width, width), bf16), flat, across, across],
        32,
        (who, *[afar(v) for v in dcs], afar(y), afar(dm), *[afar(o) for o in outs], vecs, *arrays),
        "turn",
        after,
    )


def attend_back_body(len_ref, qkv_ref, do_ref, st_ref, at_ref, d_ref, gk_ref, gb_ref, *gs_refs):
    wide = GROUP * HEAD
    halves, scaled = half_masks(), scaled_masks()

    @pl.loop(0, len_ref.shape[0])
    def _(item):
        rows = pl.ds(pl.multiple_of(item * PAD, PAD), PAD)
        valid = key_mask(len_ref[item])
        for pair in range(GROUP // 2):
            at = pair * 2 * HEAD
            q = qkv_ref[rows, at : at + 2 * HEAD]
            k = qkv_ref[rows, wide + at : wide + at + 2 * HEAD]
            v = qkv_ref[rows, 2 * wide + at : 2 * wide + at + 2 * HEAD]
            do = do_ref[rows, at : at + 2 * HEAD]
            dq = dk = dv = jnp.zeros((PAD, 2 * HEAD), f32)
            for half in range(2):
                head = 2 * pair + half
                km = k * scaled[half]
                s = dot(km, q, NT)
                s = jnp.where(valid, s, -1000000000.0)
                p = jnp.exp(s - st_ref[item, head : head + 1, :]) * st_ref[item, GROUP + head : GROUP + head + 1, :]
                dv += dot(p.astype(bf16), do * halves[half])
                dp = dot(v * halves[half], do, NT)
                delta = jnp.sum(dp * p, axis=0, keepdims=True)
                ds = (p * (dp - delta)).astype(bf16)
                dk += dot(ds, q * scaled[half])
                dq += dot(ds, km, TN)
            d_ref[rows, at : at + 2 * HEAD] = dq.astype(bf16)
            d_ref[rows, wide + at : wide + at + 2 * HEAD] = dk.astype(bf16)
            d_ref[rows, 2 * wide + at : 2 * wide + at + 2 * HEAD] = dv.astype(bf16)

    half = gk_ref.shape[0]
    grad = dot(at_ref[...], d_ref[...]).astype(bf16)
    gk_ref[...] = grad[:half]
    for ref in gs_refs:
        ref[...] = grad[half : half + ref.shape[0]]
        half += ref.shape[0]
    gb_ref[...] = jnp.sum(d_ref[...].astype(f32), axis=0, keepdims=True)


def attend_back(lengths, qkv, do, stats, at, pieces, after):
    rows, wide3 = qkv.shape
    width = at.shape[0]
    half = jax.ShapeDtypeStruct((width // 2, wide3), bf16)
    piece = jax.ShapeDtypeStruct((width // 2 // pieces, wide3), bf16)
    return call(
        attend_back_body,
        None,
        [SM, VM, VM, VM, VM],
        [
            (jax.ShapeDtypeStruct((rows, wide3), bf16), VM),
            (half, VM),
            (jax.ShapeDtypeStruct((1, wide3), f32), VM),
        ]
        + [(piece, VM)] * pieces,
        [],
        16,
        (lengths, qkv, do, stats, at),
        "attend_back",
        after,
    )


def start_back_body(counts, who, len_ref, d0, d1, d2, xb_ref, dy_ref, mark_ref, vec_ref, gb0, gb1, gb2, mid_ref, bd_ref, bu0, bu1, *rest):
    shards, (out_ref, gv_ref, w_ref, da_ref) = rest[:-4], rest[-4:]
    at = 0
    wide3 = d0.shape[1]
    acc = None
    for group, d in enumerate((d0, d1, d2)):
        gather_rows(who, shards[at : at + counts[group]], w_ref.at[group])
        at += counts[group]
        part = dot(d[...], w_ref[group], NT)
        acc = part if acc is None else acc + part
    da_ref[...] = acc
    gain_grad = shift_grad = embed_grad = jnp.zeros((1, xb_ref.shape[1]), f32)
    for item in range(out_ref.shape[0]):
        rows = slice(item * PAD, (item + 1) * PAD)
        da = da_ref[rows, :]
        unit, factor = unit_rows(xb_ref[rows, :].astype(f32))
        gain_grad += jnp.sum(da * unit, axis=0, keepdims=True)
        shift_grad += jnp.sum(da, axis=0, keepdims=True)
        dx = dy_ref[rows, :] + unit_back(da, unit, factor, vec_ref[0:1, :])
        marked = spread_rows(chosen_rows(mark_ref[item], len_ref[item]), dx.shape[1])
        text = dx[:TXT]
        embed_grad += jnp.sum(jnp.where(marked, text, 0.0), axis=0, keepdims=True)
        out_ref[item] = jnp.concatenate([jnp.where(marked, 0.0, text), dx[TXT:SEQ]], axis=0)
    wide, width = GROUP * HEAD, gv_ref.shape[1]
    gv_ref[...] = jnp.zeros_like(gv_ref)
    gv_ref[0:1, :] = gain_grad
    gv_ref[1:2, :] = shift_grad
    for group, gb in enumerate((gb0, gb1, gb2)):
        gv_ref[2:3, group * wide : (group + 1) * wide] = gb[:, :wide]
        gv_ref[3:4, group * wide : (group + 1) * wide] = gb[:, 2 * wide :]
    gv_ref[4:5, :] = mid_ref[2:3, :]
    gv_ref[5:7, :] = mid_ref[0:2, :]
    gv_ref[7:8, :] = bd_ref[...]
    for row, (ref, place) in enumerate(((bu0, 0), (bu0, 1), (bu1, 0), (bu1, 1))):
        gv_ref[8 + row : 9 + row, :] = ref[:, place * width : (place + 1) * width]
    gv_ref[12:13, :] = embed_grad


def start_back(who, lengths, grads, weights, xb, dy, marks, vecs, sums, after):
    rows, width = xb.shape
    wide3 = grads[0].shape[1]
    specs, arrays = shard_specs([w for ws in weights for w in ws], wide3, lambda i: 0)
    out = far_mem((rows // PAD, SEQ, width), f32)
    small = jax.ShapeDtypeStruct((16, width), f32)
    return call(
        functools.partial(start_back_body, [len(ws) for ws in weights]),
        (1,),
        [SM, SM] + [whole(v.shape) for v in (*grads, xb, dy, marks, vecs, *sums)] + specs,
        [(out, whole(out.shape)), (small, whole(small.shape))],
        [pltpu.VMEM((len(weights), width, wide3), bf16), pltpu.VMEM((rows, width), f32)],
        28,
        (who, lengths, *grads, afar(xb), afar(dy), marks, vecs, *sums, *arrays),
        "start_back",
        after,
    )


def finish_body(counts, who, y_ref, vec_ref, *rest):
    parts = len(counts)
    gelus, rest = rest[:parts], rest[parts:]
    shards, (out_ref, token, acc_ref, *w_refs) = rest[: sum(counts)], rest[sum(counts) :]
    token[...] = jnp.zeros(TOKEN, f32)
    step = pl.program_id(0)

    @pl.when(step == 0)
    def _():
        acc_ref[...] = y_ref[...] + vec_ref[7:8, :]

    at = 0
    total = acc_ref[...]
    for gelu, count, w_ref in zip(gelus, counts, w_refs):
        gather_rows(who, shards[at : at + count], w_ref)
        total += dot(gelu[...], w_ref[...], NT)
        at += count
    acc_ref[...] = total

    @pl.when(step == pl.num_programs(0) - 1)
    def _():
        for item in range(out_ref.shape[0]):
            out_ref[item] = acc_ref[item * PAD : (item + 1) * PAD, :].astype(bf16)[:SEQ]


def finish(who, y, gelus, downs, vecs, after):
    rows, width = y.shape
    step = BLOCK
    out = far_mem((rows // PAD, SEQ, width), bf16)
    views = [shard_specs([(v, at * BLOCK // step) for v, at in down], step, lambda i: i) for down in downs]
    return call(
        functools.partial(finish_body, [len(down) for down in downs]),
        (gelus[0].shape[1] // step,),
        [SM] + wholes(y, vecs)
        + [pl.BlockSpec((rows, step), lambda i: (0, i)) for _ in gelus]
        + [spec for specs, _ in views for spec in specs],
        [(out, whole(out.shape)), (jax.ShapeDtypeStruct(TOKEN, f32), whole(TOKEN))],
        [pltpu.VMEM((rows, width), f32)] + [pltpu.VMEM((width, step), bf16)] * len(gelus),
        32,
        (who, afar(y), vecs, *[afar(g) for g in gelus], *[v for _, arrays in views for v in arrays]),
        "finish",
        after,
    )


def swap(value, axis, bit):
    size = lax.axis_size(axis)
    return lax.ppermute(value, axis, [(i, i ^ (1 << bit)) for i in range(size)])


def half_of(value, which, dim):
    size = value.shape[dim] // 2
    return lax.dynamic_slice_in_dim(value, which * size, size, dim)


def plus(*arrays):
    return functools.reduce(lambda a, b: a + b, (v.astype(f32) for v in arrays))


TOKEN = (8, 128)


def step_call(body, ins, shapes, name, after):
    outs = [(near_mem(shape, dtype), VM) for shape, dtype in shapes]
    outs.append((near_mem(TOKEN, f32), VM))
    return call(body, None, [VM] * len(ins), outs, [], 8, [near(v) for v in ins], name, after, flops=10**4)


def paired(counts, refs):
    at = 0
    for count in counts:
        got = [ref[...] for ref in refs[at + 1 : at + 1 + count]]
        yield refs[at], got[0] if count == 1 else jnp.concatenate(got, axis=0)
        at += 1 + count


def first_body(counts, *refs):
    out = refs[-1]
    half = out.shape[1]
    for one, (keep, got) in enumerate(paired(counts, refs[:-1])):
        out[one] = plus(keep[half:], got[half:]).astype(bf16)


def second_body(counts, *refs):
    back, send, mine = refs[-3:]
    half = send.shape[1]
    for one, (keep, got) in enumerate(paired(counts, refs[:-3])):
        mine[one] = plus(keep[:half], got[:half], back[one, :half])
        send[one] = plus(keep[half : 2 * half], got[half : 2 * half], back[one, half:]).astype(bf16)


def third_body(keep, got, send, mine):
    half = send.shape[1]
    mine[...] = plus(keep[:, :half], got[:, :half])
    send[...] = plus(keep[:, half:], got[:, half:]).astype(bf16)


def add_body(one, two, out):
    out[...] = plus(one[...], two[...]).astype(out.dtype)


def join_body(mine, got, out):
    half = mine.shape[1]
    out[:, :half] = mine[...]
    out[:, half:] = got[...]


def cross(value, swapped):
    size, shards = lax.axis_size("dp") * lax.axis_size("fsdp"), lax.axis_size("fsdp")
    flip = lambda i: 2 if (i & 1) == swapped else shards
    return lax.ppermute(value, ("dp", "fsdp"), [(i, i ^ flip(i)) for i in range(size)])


def slot(tasks, *after):
    counts = [(len(ins), len(shapes)) for _, _, ins, shapes in tasks]

    def body(*refs):
        at, to = 0, sum(n for n, _ in counts)
        for (_, step, _, _), (n, m) in zip(tasks, counts):
            step(*refs[at : at + n], *refs[to : to + m])
            at, to = at + n, to + m
        refs[-1][...] = jnp.zeros(TOKEN, f32)

    ins = [v for task in tasks for v in task[2]]
    shapes = [v for task in tasks for v in task[3]]
    *results, token = step_call(body, ins, shapes, "slot", after)
    done = [token]
    for (owner, _, _, _), (_, m) in zip(tasks, counts):
        owner.out, *rest = results[:m]
        owner.mine = rest[0] if rest else owner.out
        results = results[m:]
    return done


class Chunk:
    def __init__(self, keeps, sends):
        self.counts = [len(s) for s in sends]
        self.pairs = [w for k, s in zip(keeps, sends) for w in (k, *[swap(v, "fsdp", 0) for v in s])]
        self.shape = (len(keeps), keeps[0].shape[0], keeps[0].shape[1])

    def task(self, body, ins, outs):
        count, rows, cols = self.shape
        return self, body, ins, [((count, rows // parts, cols), dtype) for parts, dtype in outs]

    def first(self):
        return self.task(functools.partial(first_body, self.counts), self.pairs, [(2, bf16)])

    def second(self):
        return self.task(functools.partial(second_body, self.counts), [*self.pairs, cross(self.out, 0)], [(4, bf16), (4, f32)])

    def third(self):
        return self.task(third_body, [self.mine, cross(self.out, 1)], [(8, bf16), (8, f32)])

    def rest(self):
        return self.task(add_body, [self.mine, swap(self.out, "dp", 1)], [(8, bf16)])

    def part(self):
        last = lax.axis_size("dp").bit_length() - 2
        for bit in range(2, last):
            slot([self.task(add_body, [self.out, swap(self.out, "dp", bit)], [(8, bf16)])])
        return self.task(add_body, [self.out, swap(self.out, "dp", last)], [(8, bf16)])

    def half(self):
        return self.task(join_body, [self.out, swap(self.out, "dp", 1)], [(4, bf16)])

    def halves(self):
        return self.out, swap(self.out, "dp", 0)


class Rows:
    def __init__(self, value):
        self.out = value
        bits = lambda axis: range(lax.axis_size(axis).bit_length() - 1)
        self.left = [(axis, bit) for axis in ("fsdp", "dp") for bit in bits(axis)]

    def pair(self):
        axis, bit = self.left.pop(0)
        return [self.out, swap(self.out, axis, bit)]

    def step(self):
        return self, add_body, self.pair(), [(self.out.shape, f32)]

    def last(self):
        while len(self.left) > 1:
            slot([self.step()])
        return self.pair()


def adam_body(count, who, mine, got, *rest):
    ins, outs = rest[: 3 * count], rest[-4 * count :]
    half = mine.shape[1] // 2
    low, mid = who[1] == 0, who[2] == 0
    for one in range(count):
        first, second, weight = ins[3 * one : 3 * one + 3]
        first_new, second_new, update, sums = outs[4 * one : 4 * one + 4]
        rows = []
        for ref in (mine, got):
            a, b = ref[one, :half].astype(f32), ref[one, half:].astype(f32)
            rows.append((jnp.where(mid, a, b), jnp.where(mid, b, a)))
        near_rows, other_rows = rows
        grad = [jnp.where(low, a, b) for a, b in zip(near_rows, other_rows)]
        grad += [jnp.where(low, b, a) for a, b in zip(near_rows, other_rows)]
        moved = adam_moments(jnp.concatenate(grad, axis=0), first[...], second[...])
        master = weight[...]
        first_new[...], second_new[...] = moved[0], moved[1]
        change = moved[2] + decay_rate * master
        update[...] = change

        @pl.when(pl.program_id(0) == 0)
        def _(sums=sums):
            sums[...] = jnp.zeros_like(sums)

        sums[0:1, :] += jnp.sum(master * master, axis=0, keepdims=True)
        sums[1:2, :] += jnp.sum(change * change, axis=0, keepdims=True)


def adam(who, halves, matrices, wide, steps, columns, made, after, grad_at=None):
    count, rows = len(matrices), halves[0].shape[1]
    grad = pl.BlockSpec((count, rows, wide), grad_at or (lambda i: (0, 0, i)))
    ins, outs, args, extra, aliases = [SM, grad, grad], [], [who, *halves], [], {}
    for one, matrix in enumerate(matrices):
        block = pl.BlockSpec((matrix[2].shape[0], wide), lambda i, at=columns[one]: (0, at(i)))
        full = (jax.ShapeDtypeStruct(matrix[2].shape, f32), block)
        ins += [block] * 3
        args += matrix
        outs += [full] * 3 + [(jax.ShapeDtypeStruct((2, wide), f32), whole((2, wide)))]
        if made[one] is not None:
            extra += [(4 * one + k, v) for k, v in enumerate(made[one][:3])]
    for out, value in extra:
        aliases[len(ins)] = out
        ins.append(pl.BlockSpec(memory_space=pl.ANY))
        args.append(value)
    got = call(functools.partial(adam_body, count), (steps,), ins, outs, [], 32, tuple(args), "adam", after, aliases)
    return [got[4 * one : 4 * one + 4] for one in range(count)]


def total_body(*refs):
    *parts, out = refs
    for row, group in enumerate(parts_of(parts)):
        for kind in range(2):
            value = sum(jnp.sum(ref[kind : kind + 1, :]) for ref in group)
            out[4 * kind + row : 4 * kind + row + 1, :] = jnp.full((1, out.shape[1]), value, f32)


def parts_of(parts):
    return parts[0:2], parts[2:3], parts[3:5], parts[5:7]


def totals(sums):
    out = jax.ShapeDtypeStruct((8, 128), f32)
    return call(total_body, None, [VM] * len(sums), [(out, VM)], [], 8, tuple(sums), "totals")[0]


def apply_body(one, two, w0, w1, w2, w3, u0, u1, u2, u3, n0, n1, n2, n3, norms):
    total = one[...] + two[...]
    norms[...] = jnp.sqrt(total)
    for row, (w, u, n) in enumerate(((w0, u0, n0), (w1, u1, n1), (w2, u2, n2), (w3, u3, n3))):
        ratio = jnp.sqrt(total[row : row + 1, :1]) * lax.rsqrt(total[4 + row : 5 + row, :1] + adam_eps)
        n[...] = w[...] - (matrix_rate * ratio) * u[...]


def apply(one, two, weights, updates):
    steps = 3
    blocks = [pl.BlockSpec((w.shape[0], w.shape[1] // steps), lambda i: (0, i)) for w in weights]
    norms = jax.ShapeDtypeStruct(one.shape, f32)
    return call(
        apply_body,
        (steps,),
        [whole(one.shape)] * 2 + blocks + blocks,
        [(jax.ShapeDtypeStruct(w.shape, f32), b) for w, b in zip(weights, blocks)] + [(norms, whole(one.shape))],
        [],
        24,
        (one, two, *weights, *updates),
        "apply",
    )


def vector_body(who, one, two, first, second, params, new, first_new, second_new):
    rows, cols = params.shape
    total = one[...] + two[...]
    grad = total[:rows, :cols]
    for block in range(1, 4):
        grad = jnp.where(who[0] == block, total[:rows, block * cols : (block + 1) * cols], grad)
    moved = adam_moments(grad, first[...], second[...])
    first_new[...], second_new[...] = moved[0], moved[1]
    new[...] = params[...] - vector_rate * moved[2]


def vector_step(who, one, two, first, second, params):
    out = jax.ShapeDtypeStruct(params.shape, f32)
    args = (who, one, two, first, second, params)
    return call(vector_body, None, [SM] + [VM] * 5, [(out, VM)] * 3, [], 8, args, "vector_step")


def adam_moments(grad, first, second):
    first_new = beta_one * first + (1.0 - beta_one) * grad
    second_new = beta_two * second + (1.0 - beta_two) * grad * grad
    direction = (
        first_new
        / (1.0 - beta_one**STEP)
        / (jnp.sqrt(second_new / (1.0 - beta_two**STEP)) + adam_eps)
    )
    return (first_new, second_new, direction)


def local(
    block_in,
    out_grad,
    caption_len,
    mask_marks,
    qkv_weight,
    out_weight,
    up_weight,
    down_weight,
    vector_params,
    qkv_first,
    qkv_second,
    out_first,
    out_second,
    up_first,
    up_second,
    down_first,
    down_second,
    vector_first,
    vector_second,
):
    width = block_in.shape[2]
    hidden = up_weight.shape[1]
    groups = width // (GROUP * HEAD)
    shard = lax.axis_index("fsdp")
    replica = lax.axis_index("dp")
    who = jnp.stack([shard, replica & 1, (replica >> 1) & 1]).astype(jnp.int32)
    cols = hidden // PARTS
    core = lambda v: swap(v, "fsdp", 0)
    far = lambda v: swap(v, "fsdp", 1)
    turned = lambda v: v.T

    own_one, own_more = cast_heads(qkv_weight, vector_params)
    far_one, far_more = far(own_one), far(own_more)
    own_out, half_up, half_down, *own_parts = cast_rest(who, out_weight.T, up_weight, down_weight.T, [own_one])
    dm, dmt, grad_bd = prep_grad(who, out_grad, [own_out])
    far_one = tie(far_one, dm)
    far_up, far_down, far_part = (far(v) for v in (half_up, half_down, own_parts[2]))
    core_parts = [core(v) for v in own_parts]
    first_block = lambda *arrays: [(v, 0) for v in arrays]
    one_shards = (own_one, core(own_one), far_one, core(far_one))

    marks = mask_marks.reshape(*mask_marks.shape, 1)
    vecs, xb, a = prep(who, caption_len, block_in, marks, one_shards, [])
    far_more = tie(far_more, xb)
    more_shards = (own_more, core(own_more), far_more, core(far_more))
    heads_full = [first_block(*one_shards)] + [[(v, g) for v in more_shards] for g in range(groups - 1)]
    sides = lambda mine: (mine, swap(mine, "dp", 0))
    heads = [attend(who, caption_len, a, heads_full[0], vecs, 0, [far_more])]
    own_out = tie(own_out, heads[0][0])
    up_far = sides(tie(far_up, heads[0][0]))
    heads.append(attend(who, caption_len, a, heads_full[1], vecs, 1, [heads[0][0], up_far[0]]))
    down_far = sides(tie(far_down, heads[1][0]))
    heads.append(attend(who, caption_len, a, heads_full[2], vecs, 2, [heads[1][0], down_far[0], up_far[1]]))
    far_out = far(own_out)
    out_full = first_block(own_out, core(own_out), far_out, core(far_out))
    outs = [h[1] for h in heads]
    y, c, ct = mix(who, xb, outs, out_full, vecs, [down_far[1]])
    ups = first_block(own_parts[0], core_parts[0], *up_far, *(core(v) for v in up_far))
    downs = first_block(own_parts[1], core_parts[1], *down_far, *(core(v) for v in down_far))
    ffn0 = ffn(who, c, dm, ct, dmt, ups, downs, vecs, 0, [])
    chunk_a = Chunk([ffn0[0], ffn0[2]], [[ffn0[1]], [ffn0[3]]])
    at = turn_rows(who, a, [ffn0[5]])
    done = slot([chunk_a.first()], at)
    far_part = tie(far_part, ffn0[5])
    shards1 = (own_parts[2], core_parts[2], far_part, core(far_part))
    ups1 = first_block(*shards1)
    downs1 = [(v, cols // BLOCK) for v in shards1]
    ffn1 = ffn(who, c, dm, ct, dmt, ups1, downs1, vecs, 1, done)
    chunk_b = Chunk([ffn1[0], ffn1[2]], [[ffn1[1]], [ffn1[3]]])
    done = slot([chunk_a.second()], ffn1[5])
    done = slot([chunk_b.first()], *done)
    dy, out_keep, out_send, *dos, grad_mid = turn(who, [ffn0[6], ffn1[6]], y, dm, outs, out_full, vecs, done)
    done = slot([chunk_a.third()], grad_mid)
    back0 = attend_back(caption_len, heads[0][0], dos[0], heads[0][2], at, 1, done)
    chunk_c = Chunk([out_keep, back0[1]], [[out_send], back0[3:]])
    done = slot([chunk_b.second(), chunk_a.rest()], back0[2])
    back1 = attend_back(caption_len, heads[1][0], dos[1], heads[1][2], at, 1, done)
    done = slot([chunk_b.third(), chunk_c.first()], back1[2])
    back2 = attend_back(caption_len, heads[2][0], dos[2], heads[2][2], at, 3, done)
    backs = [back0, back1, back2]
    chunk_d = Chunk([back1[1], back2[1]], [back1[3:], back2[3:]])
    done = slot([chunk_b.rest(), chunk_a.part(), chunk_c.second()], back2[2])
    done = slot([chunk_d.first()], *done)
    sums = [b[2] for b in backs] + [grad_mid, grad_bd, ffn0[5], ffn1[5]]
    input_grad, vector_grads = start_back(
        who, caption_len, [b[0] for b in backs], heads_full, xb, dy, marks, vecs, sums, done
    )
    rows = Rows(vector_grads)
    done = slot([chunk_b.part(), chunk_a.half(), chunk_c.third(), chunk_d.second()], vector_grads)
    block_out, token = finish(who, y, [ffn0[4], ffn1[4]], [downs, downs1], vecs, done)

    qkv = (qkv_first, qkv_second, qkv_weight)
    out = tuple(turned(v) for v in (out_first, out_second, out_weight))
    up = (up_first, up_second, up_weight)
    down = tuple(turned(v) for v in (down_first, down_second, down_weight))
    wide = 2 * TILE
    per = cols // wide
    done = slot([chunk_b.half(), chunk_c.rest(), chunk_d.third(), rows.step()], token)
    column = lambda first, step: lambda i: first + step * i
    second = lambda i: (1, 0, i)
    halves_a = chunk_a.halves()
    (up0,) = adam(who, halves_a, [up], wide, per, [column(0, 1)], [None], done)
    done = slot([chunk_d.rest(), rows.step()], up0[3])
    (down0,) = adam(who, halves_a, [down], wide, per, [column(0, 1)], [None], done, second)
    done = slot([chunk_c.part(), rows.step()], down0[3])
    done = slot([chunk_c.half(), chunk_d.part()], *done)
    halves_b = chunk_b.halves()
    (up1,) = adam(who, halves_b, [up], wide, per, [column(per, 1)], [up0], done)
    done = slot([chunk_d.half(), rows.step()], up1[3])
    (down1,) = adam(who, halves_b, [down], wide, per, [column(per, 1)], [down0], done, second)
    outer, qkv0 = adam(
        who, chunk_c.halves(), [out, qkv], TILE, 3, [column(0, 1), column(0, groups)], [None] * 2, [down1[3]]
    )
    vector_one, got = rows.last()
    columns = [lambda i: groups * (i % 3) + 1 + i // 3]
    steps = 3 * (groups - 1)
    (qkv1,) = adam(who, chunk_d.halves(), [qkv], TILE, steps, columns, [qkv0], [qkv0[3]], lambda i: (i // 3, 0, i % 3))
    vector_new, vector_first_new, vector_second_new = vector_step(
        who, vector_one, got, vector_first, vector_second, vector_params
    )
    squares = totals([qkv0[3], qkv1[3], outer[3], up0[3], up1[3], down0[3], down1[3]])
    squares = squares + core(squares)
    weights = (qkv_weight, out[2], up_weight, down[2])
    made = (qkv1, outer, up1, down1)
    *new_weights, norms = apply(squares, far(squares), weights, [m[2] for m in made])
    back = (lambda v: v, turned, lambda v: v, turned)
    moments = [f(m[k]) for f, m in zip(back, made) for k in range(2)]
    return (
        block_out,
        input_grad,
        *(f(w) for f, w in zip(back, new_weights)),
        vector_new,
        *moments,
        vector_first_new,
        vector_second_new,
        norms[:, 0].reshape(2, 4),
    )


def solution(mesh):
    placed = (
        P(("dp", "fsdp"), None, None),
        P(("dp", "fsdp"), None, None),
        P(("dp", "fsdp")),
        P(("dp", "fsdp"), None),
        P("fsdp", None),
        P(None, "fsdp"),
        P("fsdp", None),
        P(None, "fsdp"),
        P(None, "fsdp"),
        P("fsdp", None),
        P("fsdp", None),
        P(None, "fsdp"),
        P(None, "fsdp"),
        P("fsdp", None),
        P("fsdp", None),
        P(None, "fsdp"),
        P(None, "fsdp"),
        P(None, "fsdp"),
        P(None, "fsdp"),
    )
    return jax.shard_map(
        local,
        mesh=mesh,
        in_specs=placed,
        out_specs=(
            P(("dp", "fsdp"), None, None),
            P(("dp", "fsdp"), None, None),
            P("fsdp", None),
            P(None, "fsdp"),
            P("fsdp", None),
            P(None, "fsdp"),
            P(None, "fsdp"),
            P("fsdp", None),
            P("fsdp", None),
            P(None, "fsdp"),
            P(None, "fsdp"),
            P("fsdp", None),
            P("fsdp", None),
            P(None, "fsdp"),
            P(None, "fsdp"),
            P(None, "fsdp"),
            P(None, "fsdp"),
            P(),
        ),
        check_vma=False,
    )
```

```python
import functools

import jax
import jax.numpy as jnp
from jax import lax
from jax.experimental import pallas as pl
from jax.experimental.pallas import tpu as pltpu
from jax.sharding import PartitionSpec as P

HEAD = 64
TXT = 40
PATCH = 145
STEP = 7
SEQ = TXT + PATCH
PAD = 192
GROUP = 4
PARTS = 2
EXTRA = 16
LIGHT = 10**4
TILE = 256
BLOCK = 768

ln_eps = 1e-06
beta_one = 0.5
beta_two = 0.55
adam_eps = 1e-06
decay_rate = 0.01
matrix_rate = 0.5
vector_rate = 0.3

f32 = jnp.float32
bf16 = jnp.bfloat16
ORDER = (0, 2, 1, 3)
NT = (((1,), (1,)), ((), ()))
TN = (((0,), (0,)), ((), ()))

VM = pl.BlockSpec(memory_space=pltpu.VMEM)
SM = pl.BlockSpec(memory_space=pltpu.SMEM)


def dot(left, right, dims=None):
    if dims is None:
        return jnp.dot(left, right, preferred_element_type=f32)
    return lax.dot_general(left, right, dims, preferred_element_type=f32)


def call(body, grid, ins, outs, scratch, limit, args, name, after=(), aliases=None, flops=8 * 10**9):
    count = len(ins)
    after = [afar(v) if v.size > 65536 else v for v in after]

    def run(*refs):
        body(*refs[:count], *refs[count + len(after) :])

    return pl.pallas_call(
        run,
        grid=grid or (),
        in_specs=list(ins) + [pl.BlockSpec(memory_space=pl.ANY)] * len(after),
        out_specs=[o[1] for o in outs],
        out_shape=[o[0] for o in outs],
        input_output_aliases=aliases or {},
        scratch_shapes=scratch,
        compiler_params=pltpu.CompilerParams(vmem_limit_bytes=limit << 20),
        cost_estimate=pl.CostEstimate(flops=flops, bytes_accessed=flops // 200, transcendentals=0),
        name=name,
    )(*args, *after)


def far_mem(shape, dtype):
    return pltpu.HBM(tuple(shape), dtype)


def near_mem(shape, dtype):
    return pltpu.VMEM(tuple(shape), dtype)


def near(value):
    return pltpu.with_memory_space_constraint(value, pltpu.VMEM)


def afar(value):
    return pltpu.with_memory_space_constraint(value, pltpu.HBM)


def tie(value, *deps):
    return pl.pallas_call(
        lambda *refs: None,
        in_specs=[pl.BlockSpec(memory_space=pl.ANY)] * (1 + len(deps)),
        out_specs=pl.BlockSpec(memory_space=pl.ANY),
        out_shape=jax.ShapeDtypeStruct(value.shape, value.dtype),
        input_output_aliases={0: 0},
        cost_estimate=pl.CostEstimate(flops=LIGHT, bytes_accessed=LIGHT, transcendentals=0),
        name="tie",
    )(value, *[afar(v) if v.size > 65536 else v for v in deps])


def whole(shape):
    return pl.BlockSpec(shape, lambda i: (0,) * len(shape), pipeline_mode=pl.Buffered(1))


def wholes(*arrays):
    return [whole(v.shape) for v in arrays]


def shard_specs(shards, wide, columns):
    rows = lambda v: v.shape[0] - v.shape[0] % 96
    specs = [pl.BlockSpec((rows(v), wide), lambda i, at=at: (0, at + columns(i))) for v, at in shards]
    return specs, [afar(v) for v, _ in shards]


def unit_rows(rows):
    centred = rows - jnp.mean(rows, axis=-1, keepdims=True)
    factor = lax.rsqrt(jnp.mean(centred * centred, axis=-1, keepdims=True) + ln_eps)
    return centred * factor, factor


def unit_back(grad_normed, unit, factor, gain):
    grad_unit = grad_normed * gain
    return factor * (
        grad_unit
        - jnp.mean(grad_unit, axis=-1, keepdims=True)
        - unit * jnp.mean(grad_unit * unit, axis=-1, keepdims=True)
    )


def put_turned(who_ref, value, scratch, out_ref):
    part = out_ref.shape[0] // 16
    scratch[...] = value.T
    for place in range(16):
        core, one, two, three = (place >> 3) & 1, (place >> 2) & 1, (place >> 1) & 1, place & 1
        odd = (who_ref[0] & 1) ^ core
        pair = jnp.where(odd == 0, one, two)
        low = jnp.where(odd == 0, two, one)
        start = 4 * (who_ref[0] ^ (2 * pair + core)) + 2 * (who_ref[1] ^ low) + (who_ref[2] ^ three)
        out_ref[place * part : (place + 1) * part, :] = scratch[pl.ds(pl.multiple_of(start * part, 16), part), :]


def gather_rows(who_ref, refs, out_ref):
    rows = refs[0].shape[0]
    half = rows // 2
    places = [(0, None), (1, None)]
    places += [(2, None), (3, None)] if len(refs) == 4 else [(2, 0), (2, 1), (3, 0), (3, 1)]
    for (other, part), ref in zip(places, refs):
        start = (who_ref[0] ^ other) * rows
        if part is not None:
            start += (who_ref[1] ^ part) * half
        out_ref[pl.ds(pl.multiple_of(start, 32), ref.shape[0]), :] = ref[...]


def cast_heads_body(q_ref, k_ref, v_ref, vec_ref, one_ref, rest_ref):
    wide = GROUP * HEAD
    rows = q_ref.shape[0]
    step = pl.program_id(0)

    @pl.when(step == 0)
    def _():
        for kind, ref in enumerate((q_ref, k_ref, v_ref)):
            one_ref[:rows, kind * wide : (kind + 1) * wide] = ref[...].astype(bf16)
        count, cols = vec_ref.shape
        one_ref[rows:, :] = jnp.zeros_like(one_ref[rows:, :])
        one_ref[rows : rows + count, :cols] = vec_ref[...].astype(bf16)

    @pl.when(step > 0)
    def _():
        for kind, ref in enumerate((q_ref, k_ref, v_ref)):
            at = pl.multiple_of(((step - 1) * 3 + kind) * wide, wide)
            rest_ref[:, pl.ds(at, wide)] = ref[...].astype(bf16)


def cast_heads(weight, vectors):
    rows, cols = weight.shape
    wide = GROUP * HEAD
    groups = cols // (3 * wide)
    blocks = [pl.BlockSpec((rows, wide), lambda i, kind=kind: (0, kind * groups + i)) for kind in range(3)]
    shapes = [(rows + EXTRA, 3 * wide), (rows, 3 * wide * (groups - 1))]
    outs = [(far_mem(shape, bf16), whole(shape)) for shape in shapes]
    args = (*[afar(weight)] * 3, afar(vectors))
    return call(cast_heads_body, (groups,), blocks + wholes(vectors), outs, [], 12, args, "cast_heads")


def cast_rest_body(who, out_ref, up_ref, down_ref, o_ref, up_half, down_half, *parts):
    half = up_half.shape[0]
    rows = pl.ds(pl.multiple_of(who[1] * half, 32), half)
    step = pl.program_id(0)
    per = pl.num_programs(0) // PARTS

    @pl.when(step == 0)
    def _():
        o_ref[...] = out_ref[...].astype(bf16)

    @pl.when(step < per)
    def _():
        up_half[...] = up_ref[rows, :].astype(bf16)
        down_half[...] = down_ref[rows, :].astype(bf16)

    @pl.when(step < per)
    def _():
        parts[0][...] = up_ref[...].astype(bf16)
        parts[1][...] = down_ref[...].astype(bf16)

    wide = up_ref.shape[1]
    for place in range(per):

        @pl.when(step == per + place)
        def _(place=place):
            parts[2][:, place * wide : (place + 1) * wide] = up_ref[...].astype(bf16)
            parts[2][:, (per + place) * wide : (per + place + 1) * wide] = down_ref[...].astype(bf16)


def cast_rest(who, out_t, up, down_t, after):
    rows, hidden = up.shape
    cols, wide = hidden // PARTS, 768
    per = cols // wide
    block = pl.BlockSpec((rows, wide), lambda i: (0, i))
    at = lambda part: lambda i: (0, jnp.clip(i - part * per, 0, per - 1))
    out = lambda n, part: (far_mem((n, cols), bf16), pl.BlockSpec((n, wide), at(part)))
    outs = [(far_mem(out_t.shape, bf16), whole(out_t.shape)), out(rows // 2, 0), out(rows // 2, 0)]
    both = (rows, 2 * cols)
    outs += [out(rows, 0), out(rows, 0), (far_mem(both, bf16), whole(both))]
    ins = [SM] + wholes(out_t) + [block, block]
    args = (who, out_t, afar(up), afar(down_t))
    return call(cast_rest_body, (hidden // wide,), ins, outs, [], 16, args, "cast_rest", after)


def chosen_rows(marks, length):
    places = lax.broadcasted_iota(jnp.int32, marks.shape, 0)
    return jnp.where((marks == 1) & (places >= 1) & (places < length), 1.0, 0.0)


def spread_rows(chosen, width):
    return jnp.broadcast_to(chosen, (chosen.shape[0], width)) > 0


def prep_grad_body(who, g_ref, dm_ref, dmt_ref, bd_ref, all_ref, scratch):
    step = pl.program_id(0)
    tail = jnp.zeros((PAD - SEQ, g_ref.shape[2]), f32)
    dm = jnp.concatenate([g_ref[0].astype(f32), tail], axis=0)
    dm_ref[...] = dm.astype(bf16)
    all_ref[pl.ds(pl.multiple_of(step * PAD, PAD), PAD), :] = dm.astype(bf16)

    @pl.when(step == 0)
    def _():
        bd_ref[...] = jnp.zeros_like(bd_ref)

    bd_ref[...] += jnp.sum(dm, axis=0, keepdims=True)

    @pl.when(step == pl.num_programs(0) - 1)
    def _():
        put_turned(who, all_ref[...], scratch, dmt_ref)


def prep_grad(who, out_grad, after):
    items, seq, width = out_grad.shape
    rows = items * PAD
    item = pl.BlockSpec((1, seq, width), lambda i: (i, 0, 0))
    return call(
        prep_grad_body,
        (items,),
        [SM, item],
        [
            (far_mem((rows, width), bf16), pl.BlockSpec((PAD, width), lambda i: (i, 0))),
            (far_mem((width, rows), bf16), whole((width, rows))),
            (far_mem((1, width), f32), whole((1, width))),
        ],
        [pltpu.VMEM((rows, width), bf16), pltpu.VMEM((width, rows), bf16)],
        20,
        (who, afar(out_grad)),
        "prep_grad",
        after,
        flops=LIGHT,
    )


def prep_body(who, len_ref, x_ref, mark_ref, v0, v1, v2, v3, vec_ref, xb_ref, a_ref):
    step = pl.program_id(0)
    width = x_ref.shape[2]

    @pl.when(step == 0)
    def _():
        cols = width // 4
        for block in range(4):
            value = v0[:, :cols].astype(f32)
            for other, ref in ((1, v1), (2, v2), (3, v3)):
                value = jnp.where((who[0] ^ other) == block, ref[:, :cols].astype(f32), value)
            vec_ref[:, block * cols : (block + 1) * cols] = value

    gain, shift, embed = vec_ref[0:1, :], vec_ref[1:2, :], vec_ref[12:13, :]
    x = x_ref[0].astype(f32)
    marked = spread_rows(chosen_rows(mark_ref[0], len_ref[step]), width)
    tail = jnp.zeros((PAD - SEQ, width), f32)
    x = jnp.concatenate([jnp.where(marked, embed, x[:TXT]), x[TXT:], tail], axis=0)
    xb_ref[...] = x.astype(bf16)
    unit, _ = unit_rows(x)
    a_ref[...] = (unit * gain + shift).astype(bf16)


def turn_rows_body(who, a_ref, at_ref, scratch):
    put_turned(who, a_ref[...], scratch, at_ref)


def turn_rows(who, a, after):
    rows, width = a.shape
    out = (far_mem((width, rows), bf16), whole((width, rows)))
    scratch = [pltpu.VMEM((width, rows), bf16)]
    return call(turn_rows_body, (1,), [SM] + wholes(a), [out], scratch, 16, (who, afar(a)), "turn_rows", after)[0]


def prep(who, lengths, block_in, marks, vec_shards, after):
    items, seq, width = block_in.shape
    rows = items * PAD
    item = lambda *shape: pl.BlockSpec((1, *shape), lambda i: (i, 0, 0))
    flat = pl.BlockSpec((PAD, width), lambda i: (i, 0))
    extra = pl.BlockSpec((EXTRA, width), lambda i: (vec_shards[0].shape[0] // EXTRA - 1, 0))
    return call(
        prep_body,
        (items,),
        [SM, SM, item(seq, width), item(*marks.shape[1:])] + [extra] * 4,
        [
            (near_mem((16, width), f32), whole((16, width))),
            (far_mem((rows, width), bf16), flat),
            (far_mem((rows, width), bf16), flat),
        ],
        [],
        16,
        (who, lengths, afar(block_in), marks, *[afar(v) for v in vec_shards]),
        "prep",
        after,
        flops=LIGHT,
    )


def key_mask(length):
    places = lax.broadcasted_iota(jnp.int32, (PAD, 1), 0)
    return ((places >= TXT) & (places < SEQ)) | (places < length)


def half_masks():
    lanes = lax.broadcasted_iota(jnp.int32, (1, 2 * HEAD), 1)
    low = jnp.where(lanes < HEAD, 1.0, 0.0)
    return low.astype(bf16), (1.0 - low).astype(bf16)


def scaled_masks():
    return [(mask.astype(f32) * HEAD ** (-0.5)).astype(bf16) for mask in half_masks()]


def attend_body(group, who, len_ref, a_ref, vec_ref, *rest):
    wide = GROUP * HEAD
    shards, (qkv_ref, o_ref, st_ref, w_ref) = rest[:-4], rest[-4:]
    gather_rows(who, shards, w_ref)
    cols = slice(group * wide, (group + 1) * wide)
    bias = jnp.concatenate([vec_ref[2:3, cols], jnp.zeros((1, wide), f32), vec_ref[3:4, cols]], axis=1)
    qkv_ref[...] = (dot(a_ref[...], w_ref[...]) + bias).astype(bf16)
    halves, scaled = half_masks(), scaled_masks()

    @pl.loop(0, len_ref.shape[0])
    def _(item):
        rows = pl.ds(pl.multiple_of(item * PAD, PAD), PAD)
        valid = key_mask(len_ref[item])
        for pair in range(GROUP // 2):
            at = pair * 2 * HEAD
            q = qkv_ref[rows, at : at + 2 * HEAD]
            k = qkv_ref[rows, wide + at : wide + at + 2 * HEAD]
            v = qkv_ref[rows, 2 * wide + at : 2 * wide + at + 2 * HEAD]
            out = None
            for half in range(2):
                s = dot(k * scaled[half], q, NT)
                s = jnp.where(valid, s, -1000000000.0)
                top = jnp.max(s, axis=0, keepdims=True)
                e = jnp.exp(s - top)
                scale = 1.0 / jnp.sum(e, axis=0, keepdims=True)
                p = (e * scale).astype(bf16)
                part = dot(p, v * halves[half], TN)
                out = part if out is None else out + part
                head = 2 * pair + half
                st_ref[item, head : head + 1, :] = top
                st_ref[item, GROUP + head : GROUP + head + 1, :] = scale
            o_ref[rows, at : at + 2 * HEAD] = out.astype(bf16)


def attend(who, lengths, a, weights, vecs, group, after):
    rows, width = a.shape
    wide = GROUP * HEAD
    items = lengths.shape[0]
    specs, arrays = shard_specs(weights, 3 * wide, lambda i: 0)
    return call(
        functools.partial(attend_body, group),
        (1,),
        [SM, SM, whole(a.shape), whole(vecs.shape)] + specs,
        [
            (far_mem((rows, 3 * wide), bf16), whole((rows, 3 * wide))),
            (far_mem((rows, wide), bf16), whole((rows, wide))),
            (far_mem((items, 2 * GROUP, PAD), f32), whole((items, 2 * GROUP, PAD))),
        ],
        [pltpu.VMEM((width, 3 * wide), bf16)],
        16,
        (who, lengths, afar(a), vecs, *arrays),
        "attend",
        after,
    )


def mix_body(who, x_ref, o0, o1, o2, vec_ref, *rest):
    shards, (y_ref, c_ref, ct_ref, w_ref, scratch) = rest[:-5], rest[-5:]
    gather_rows(who, shards, w_ref)
    wide = GROUP * HEAD
    acc = x_ref[...].astype(f32) + vec_ref[4:5, :]
    for group, o in enumerate((o0, o1, o2)):
        acc += dot(o[...], w_ref[:, group * wide : (group + 1) * wide], NT)
    y_ref[...] = acc
    unit, _ = unit_rows(acc)
    c_ref[...] = (unit * vec_ref[5:6, :] + vec_ref[6:7, :]).astype(bf16)
    put_turned(who, c_ref[...], scratch, ct_ref)


def mix(who, xb, outs, weights, vecs, after):
    rows, width = xb.shape
    specs, arrays = shard_specs(weights, width, lambda i: 0)
    return call(
        mix_body,
        (1,),
        [SM, whole(xb.shape)] + [whole(o.shape) for o in outs] + [whole(vecs.shape)] + specs,
        [
            (far_mem((rows, width), f32), whole((rows, width))),
            (near_mem((rows, width), bf16), whole((rows, width))),
            (near_mem((width, rows), bf16), whole((width, rows))),
        ],
        [pltpu.VMEM((width, width), bf16), pltpu.VMEM((width, rows), bf16)],
        18,
        (who, afar(xb), *[afar(o) for o in outs], vecs, *arrays),
        "mix",
        after,
    )


def item_rows(cols):
    return pl.BlockSpec((PAD, cols), lambda i: (i, 0))


def gelu_pair(h):
    bell = jnp.exp(-0.5 * h * h)
    t = 1.0 / (1.0 + (0.3275911 * 0.7071067811865476) * jnp.abs(h))
    poly = t * (0.127414796 + t * (-0.142248368 + t * (0.7107068705 + t * (-0.7265760135 + t * 0.5307027145))))
    tail = poly * bell
    return jnp.where(h < 0, tail, 1.0 - tail), bell


def ffn_body(counts, base, who, c_ref, dm_ref, ct_ref, dmt_ref, *rest):
    ups, downs, rest = rest[: counts[0]], rest[counts[0] : sum(counts)], rest[sum(counts) :]
    bu_ref, uk_ref, us_ref, dk_ref, ds_ref, gelu_ref, gbu_ref, dc_ref, up_w, down_w = rest

    @pl.when(pl.program_id(0) == 0)
    def _():
        dc_ref[...] = jnp.zeros_like(dc_ref)

    gather_rows(who, ups, up_w)
    gather_rows(who, downs, down_w)
    row = (base + pl.program_id(0)) // (c_ref.shape[1] // BLOCK)
    h = dot(c_ref[...], up_w[...]) + bu_ref[pl.ds(row, 1), :]
    phi, bell = gelu_pair(h)
    gelu = (h * phi).astype(bf16)
    gelu_ref[...] = gelu
    slope = phi + h * bell * 0.3989422804014327
    dh = (dot(dm_ref[...], down_w[...]) * slope).astype(bf16)
    gbu_ref[...] = jnp.sum(dh.astype(f32), axis=0, keepdims=True)
    half = uk_ref.shape[0]
    grad = dot(ct_ref[...], dh).astype(bf16)
    uk_ref[...], us_ref[...] = grad[:half], grad[half:]
    grad = dot(dmt_ref[...], gelu).astype(bf16)
    dk_ref[...], ds_ref[...] = grad[:half], grad[half:]
    dc_ref[...] += dot(dh, up_w[...], NT)


def ffn(who, c, dm, ct, dmt, ups, downs, vecs, part, after):
    rows, width = c.shape
    cols = 4 * width // PARTS
    base, across = part * cols // BLOCK, width // BLOCK
    up_specs, up_arrays = shard_specs(ups, BLOCK, lambda i: i)
    down_specs, down_arrays = shard_specs(downs, BLOCK, lambda i: i)
    half = near_mem((width // 2, cols), bf16)
    hspec = pl.BlockSpec((width // 2, BLOCK), lambda i: (0, i))
    return call(
        functools.partial(ffn_body, (len(ups), len(downs)), base),
        (cols // BLOCK,),
        [SM, whole(c.shape), whole(dm.shape), whole(ct.shape), whole(dmt.shape)]
        + up_specs
        + down_specs
        + [pl.BlockSpec((8, BLOCK), lambda i: (1, (base + i) % across))],
        [
            (half, hspec),
            (half, hspec),
            (half, hspec),
            (half, hspec),
            (far_mem((rows, cols), bf16), pl.BlockSpec((rows, BLOCK), lambda i: (0, i))),
            (far_mem((1, cols), f32), pl.BlockSpec((1, BLOCK), lambda i: (0, i))),
            (far_mem((rows, width), f32), whole((rows, width))),
        ],
        [pltpu.VMEM((width, BLOCK), bf16), pltpu.VMEM((width, BLOCK), bf16)],
        36,
        (who, c, dm, ct, dmt, *up_arrays, *down_arrays, vecs),
        "ffn",
        after,
    )


def turn_body(who, dc0_ref, dc1_ref, y_ref, dm_ref, o0, o1, o2, vec_ref, *rest):
    shards, rest = rest[:-11], rest[-11:]
    dy_ref, gk_ref, gs_ref, do0, do1, do2, gv_ref, w_ref, all_ref, scratch, drt_ref = rest
    step = pl.program_id(0)

    @pl.when(step == 0)
    def _():
        gather_rows(who, shards, w_ref)
        gv_ref[...] = jnp.zeros_like(gv_ref)

    wide = GROUP * HEAD
    here = pl.ds(pl.multiple_of(step * PAD, PAD), PAD)
    dc = dc0_ref[...] + dc1_ref[...]
    unit, factor = unit_rows(y_ref[...])
    gv_ref[0:1, :] += jnp.sum(dc * unit, axis=0, keepdims=True)
    gv_ref[1:2, :] += jnp.sum(dc, axis=0, keepdims=True)
    dy = dm_ref[...].astype(f32) + unit_back(dc, unit, factor, vec_ref[5:6, :])
    dy_ref[...] = dy
    dr = dy.astype(bf16)
    gv_ref[2:3, :] += jnp.sum(dr.astype(f32), axis=0, keepdims=True)
    all_ref[here, :] = dr

    @pl.when(step == pl.num_programs(0) - 1)
    def _():
        put_turned(who, all_ref[...], scratch, drt_ref)
        half = gk_ref.shape[0]
        for group, (o, do) in enumerate(((o0, do0), (o1, do1), (o2, do2))):
            cols = slice(group * wide, (group + 1) * wide)
            do[...] = dot(all_ref[...], w_ref[:, cols]).astype(bf16)
            grad = dot(drt_ref[...], o[...]).astype(bf16)
            gk_ref[:, cols] = grad[:half]
            gs_ref[:, cols] = grad[half:]


def turn(who, dcs, y, dm, outs, weights, vecs, after):
    rows, width = y.shape
    half = jax.ShapeDtypeStruct((width // 2, width), bf16)
    do = (jax.ShapeDtypeStruct((rows, GROUP * HEAD), bf16), whole((rows, GROUP * HEAD)))
    small = jax.ShapeDtypeStruct((3, width), f32)
    specs, arrays = shard_specs(weights, width, lambda i: 0)
    flat, across = pltpu.VMEM((rows, width), bf16), pltpu.VMEM((width, rows), bf16)
    return call(
        turn_body,
        (rows // PAD,),
        [SM] + [item_rows(width)] * 4 + wholes(*outs, vecs) + specs,
        [(far_mem((rows, width), f32), item_rows(width))]
        + [(half, whole(half.shape))] * 2
        + [do] * 3
        + [(small, whole(small.shape))],
        [pltpu.VMEM((width, width), bf16), flat, across, across],
        32,
        (who, *[afar(v) for v in dcs], afar(y), afar(dm), *[afar(o) for o in outs], vecs, *arrays),
        "turn",
        after,
    )


def attend_back_body(len_ref, qkv_ref, do_ref, st_ref, at_ref, d_ref, gk_ref, gb_ref, *gs_refs):
    wide = GROUP * HEAD
    halves, scaled = half_masks(), scaled_masks()

    @pl.loop(0, len_ref.shape[0])
    def _(item):
        rows = pl.ds(pl.multiple_of(item * PAD, PAD), PAD)
        valid = key_mask(len_ref[item])
        for pair in range(GROUP // 2):
            at = pair * 2 * HEAD
            q = qkv_ref[rows, at : at + 2 * HEAD]
            k = qkv_ref[rows, wide + at : wide + at + 2 * HEAD]
            v = qkv_ref[rows, 2 * wide + at : 2 * wide + at + 2 * HEAD]
            do = do_ref[rows, at : at + 2 * HEAD]
            dq = dk = dv = jnp.zeros((PAD, 2 * HEAD), f32)
            for half in range(2):
                head = 2 * pair + half
                km = k * scaled[half]
                s = dot(km, q, NT)
                s = jnp.where(valid, s, -1000000000.0)
                p = jnp.exp(s - st_ref[item, head : head + 1, :]) * st_ref[item, GROUP + head : GROUP + head + 1, :]
                dv += dot(p.astype(bf16), do * halves[half])
                dp = dot(v * halves[half], do, NT)
                delta = jnp.sum(dp * p, axis=0, keepdims=True)
                ds = (p * (dp - delta)).astype(bf16)
                dk += dot(ds, q * scaled[half])
                dq += dot(ds, km, TN)
            d_ref[rows, at : at + 2 * HEAD] = dq.astype(bf16)
            d_ref[rows, wide + at : wide + at + 2 * HEAD] = dk.astype(bf16)
            d_ref[rows, 2 * wide + at : 2 * wide + at + 2 * HEAD] = dv.astype(bf16)

    half = gk_ref.shape[0]
    grad = dot(at_ref[...], d_ref[...]).astype(bf16)
    gk_ref[...] = grad[:half]
    for ref in gs_refs:
        ref[...] = grad[half : half + ref.shape[0]]
        half += ref.shape[0]
    gb_ref[...] = jnp.sum(d_ref[...].astype(f32), axis=0, keepdims=True)


def attend_back(lengths, qkv, do, stats, at, pieces, after):
    rows, wide3 = qkv.shape
    width = at.shape[0]
    half = jax.ShapeDtypeStruct((width // 2, wide3), bf16)
    piece = jax.ShapeDtypeStruct((width // 2 // pieces, wide3), bf16)
    return call(
        attend_back_body,
        None,
        [SM, VM, VM, VM, VM],
        [
            (jax.ShapeDtypeStruct((rows, wide3), bf16), VM),
            (half, VM),
            (jax.ShapeDtypeStruct((1, wide3), f32), VM),
        ]
        + [(piece, VM)] * pieces,
        [],
        16,
        (lengths, qkv, do, stats, at),
        "attend_back",
        after,
    )


def start_back_body(counts, who, len_ref, d0, d1, d2, xb_ref, dy_ref, mark_ref, vec_ref, gb0, gb1, gb2, mid_ref, bd_ref, bu0, bu1, *rest):
    shards, (out_ref, gv_ref, w_ref, da_ref) = rest[:-4], rest[-4:]
    at = 0
    wide3 = d0.shape[1]
    acc = None
    for group, d in enumerate((d0, d1, d2)):
        gather_rows(who, shards[at : at + counts[group]], w_ref.at[group])
        at += counts[group]
        part = dot(d[...], w_ref[group], NT)
        acc = part if acc is None else acc + part
    da_ref[...] = acc
    gain_grad = shift_grad = embed_grad = jnp.zeros((1, xb_ref.shape[1]), f32)
    for item in range(out_ref.shape[0]):
        rows = slice(item * PAD, (item + 1) * PAD)
        da = da_ref[rows, :]
        unit, factor = unit_rows(xb_ref[rows, :].astype(f32))
        gain_grad += jnp.sum(da * unit, axis=0, keepdims=True)
        shift_grad += jnp.sum(da, axis=0, keepdims=True)
        dx = dy_ref[rows, :] + unit_back(da, unit, factor, vec_ref[0:1, :])
        marked = spread_rows(chosen_rows(mark_ref[item], len_ref[item]), dx.shape[1])
        text = dx[:TXT]
        embed_grad += jnp.sum(jnp.where(marked, text, 0.0), axis=0, keepdims=True)
        out_ref[item] = jnp.concatenate([jnp.where(marked, 0.0, text), dx[TXT:SEQ]], axis=0)
    wide, width = GROUP * HEAD, gv_ref.shape[1]
    gv_ref[...] = jnp.zeros_like(gv_ref)
    gv_ref[0:1, :] = gain_grad
    gv_ref[1:2, :] = shift_grad
    for group, gb in enumerate((gb0, gb1, gb2)):
        gv_ref[2:3, group * wide : (group + 1) * wide] = gb[:, :wide]
        gv_ref[3:4, group * wide : (group + 1) * wide] = gb[:, 2 * wide :]
    gv_ref[4:5, :] = mid_ref[2:3, :]
    gv_ref[5:7, :] = mid_ref[0:2, :]
    gv_ref[7:8, :] = bd_ref[...]
    for row, (ref, place) in enumerate(((bu0, 0), (bu0, 1), (bu1, 0), (bu1, 1))):
        gv_ref[8 + row : 9 + row, :] = ref[:, place * width : (place + 1) * width]
    gv_ref[12:13, :] = embed_grad


def start_back(who, lengths, grads, weights, xb, dy, marks, vecs, sums, after):
    rows, width = xb.shape
    wide3 = grads[0].shape[1]
    specs, arrays = shard_specs([w for ws in weights for w in ws], wide3, lambda i: 0)
    out = far_mem((rows // PAD, SEQ, width), f32)
    small = jax.ShapeDtypeStruct((16, width), f32)
    return call(
        functools.partial(start_back_body, [len(ws) for ws in weights]),
        (1,),
        [SM, SM] + [whole(v.shape) for v in (*grads, xb, dy, marks, vecs, *sums)] + specs,
        [(out, whole(out.shape)), (small, whole(small.shape))],
        [pltpu.VMEM((len(weights), width, wide3), bf16), pltpu.VMEM((rows, width), f32)],
        28,
        (who, lengths, *grads, afar(xb), afar(dy), marks, vecs, *sums, *arrays),
        "start_back",
        after,
    )


def finish_body(counts, who, y_ref, vec_ref, *rest):
    parts = len(counts)
    gelus, rest = rest[:parts], rest[parts:]
    shards, (out_ref, token, acc_ref, *w_refs) = rest[: sum(counts)], rest[sum(counts) :]
    token[...] = jnp.zeros(TOKEN, f32)
    step = pl.program_id(0)

    @pl.when(step == 0)
    def _():
        acc_ref[...] = y_ref[...] + vec_ref[7:8, :]

    at = 0
    total = acc_ref[...]
    for gelu, count, w_ref in zip(gelus, counts, w_refs):
        gather_rows(who, shards[at : at + count], w_ref)
        total += dot(gelu[...], w_ref[...], NT)
        at += count
    acc_ref[...] = total

    @pl.when(step == pl.num_programs(0) - 1)
    def _():
        for item in range(out_ref.shape[0]):
            out_ref[item] = acc_ref[item * PAD : (item + 1) * PAD, :].astype(bf16)[:SEQ]


def finish(who, y, gelus, downs, vecs, after):
    rows, width = y.shape
    step = BLOCK
    out = far_mem((rows // PAD, SEQ, width), bf16)
    views = [shard_specs([(v, at * BLOCK // step) for v, at in down], step, lambda i: i) for down in downs]
    return call(
        functools.partial(finish_body, [len(down) for down in downs]),
        (gelus[0].shape[1] // step,),
        [SM] + wholes(y, vecs)
        + [pl.BlockSpec((rows, step), lambda i: (0, i)) for _ in gelus]
        + [spec for specs, _ in views for spec in specs],
        [(out, whole(out.shape)), (jax.ShapeDtypeStruct(TOKEN, f32), whole(TOKEN))],
        [pltpu.VMEM((rows, width), f32)] + [pltpu.VMEM((width, step), bf16)] * len(gelus),
        32,
        (who, afar(y), vecs, *[afar(g) for g in gelus], *[v for _, arrays in views for v in arrays]),
        "finish",
        after,
    )


def swap(value, axis, bit):
    size = lax.axis_size(axis)
    return lax.ppermute(value, axis, [(i, i ^ (1 << bit)) for i in range(size)])


def half_of(value, which, dim):
    size = value.shape[dim] // 2
    return lax.dynamic_slice_in_dim(value, which * size, size, dim)


def plus(*arrays):
    return functools.reduce(lambda a, b: a + b, (v.astype(f32) for v in arrays))


TOKEN = (8, 128)


def step_call(body, ins, shapes, name, after):
    outs = [(near_mem(shape, dtype), VM) for shape, dtype in shapes]
    outs.append((near_mem(TOKEN, f32), VM))
    return call(body, None, [VM] * len(ins), outs, [], 8, [near(v) for v in ins], name, after, flops=10**4)


def paired(counts, refs):
    at = 0
    for count in counts:
        got = [ref[...] for ref in refs[at + 1 : at + 1 + count]]
        yield refs[at], got[0] if count == 1 else jnp.concatenate(got, axis=0)
        at += 1 + count


def first_body(counts, *refs):
    out = refs[-1]
    half = out.shape[1]
    for one, (keep, got) in enumerate(paired(counts, refs[:-1])):
        out[one] = plus(keep[half:], got[half:]).astype(bf16)


def second_body(counts, *refs):
    back, send, mine = refs[-3:]
    half = send.shape[1]
    for one, (keep, got) in enumerate(paired(counts, refs[:-3])):
        mine[one] = plus(keep[:half], got[:half], back[one, :half])
        send[one] = plus(keep[half : 2 * half], got[half : 2 * half], back[one, half:]).astype(bf16)


def third_body(keep, got, send, mine):
    half = send.shape[1]
    mine[...] = plus(keep[:, :half], got[:, :half])
    send[...] = plus(keep[:, half:], got[:, half:]).astype(bf16)


def add_body(one, two, out):
    out[...] = plus(one[...], two[...]).astype(out.dtype)


def join_body(mine, got, out):
    half = mine.shape[1]
    out[:, :half] = mine[...]
    out[:, half:] = got[...]


def cross(value, swapped):
    size, shards = lax.axis_size("dp") * lax.axis_size("fsdp"), lax.axis_size("fsdp")
    flip = lambda i: 2 if (i & 1) == swapped else shards
    return lax.ppermute(value, ("dp", "fsdp"), [(i, i ^ flip(i)) for i in range(size)])


def slot(tasks, *after):
    counts = [(len(ins), len(shapes)) for _, _, ins, shapes in tasks]

    def body(*refs):
        at, to = 0, sum(n for n, _ in counts)
        for (_, step, _, _), (n, m) in zip(tasks, counts):
            step(*refs[at : at + n], *refs[to : to + m])
            at, to = at + n, to + m
        refs[-1][...] = jnp.zeros(TOKEN, f32)

    ins = [v for task in tasks for v in task[2]]
    shapes = [v for task in tasks for v in task[3]]
    *results, token = step_call(body, ins, shapes, "slot", after)
    done = [token]
    for (owner, _, _, _), (_, m) in zip(tasks, counts):
        owner.out, *rest = results[:m]
        owner.mine = rest[0] if rest else owner.out
        results = results[m:]
    return done


class Chunk:
    def __init__(self, keeps, sends):
        self.counts = [len(s) for s in sends]
        self.pairs = [w for k, s in zip(keeps, sends) for w in (k, *[swap(v, "fsdp", 0) for v in s])]
        self.shape = (len(keeps), keeps[0].shape[0], keeps[0].shape[1])

    def task(self, body, ins, outs):
        count, rows, cols = self.shape
        return self, body, ins, [((count, rows // parts, cols), dtype) for parts, dtype in outs]

    def first(self):
        return self.task(functools.partial(first_body, self.counts), self.pairs, [(2, bf16)])

    def second(self):
        return self.task(functools.partial(second_body, self.counts), [*self.pairs, cross(self.out, 0)], [(4, bf16), (4, f32)])

    def third(self):
        return self.task(third_body, [self.mine, cross(self.out, 1)], [(8, bf16), (8, f32)])

    def rest(self):
        return self.task(add_body, [self.mine, swap(self.out, "dp", 1)], [(8, bf16)])

    def part(self):
        last = lax.axis_size("dp").bit_length() - 2
        for bit in range(2, last):
            slot([self.task(add_body, [self.out, swap(self.out, "dp", bit)], [(8, bf16)])])
        return self.task(add_body, [self.out, swap(self.out, "dp", last)], [(8, bf16)])

    def half(self):
        return self.task(join_body, [self.out, swap(self.out, "dp", 1)], [(4, bf16)])

    def halves(self):
        return self.out, swap(self.out, "dp", 0)


class Rows:
    def __init__(self, value):
        self.out = value
        bits = lambda axis: range(lax.axis_size(axis).bit_length() - 1)
        steps = [(axis, bit) for axis in ("fsdp", "dp") for bit in bits(axis)]
        self.left = [("dp", 0)] + [step for step in steps if step != ("dp", 0)]

    def pair(self):
        axis, bit = self.left.pop(0)
        return [self.out, swap(self.out, axis, bit)]

    def step(self):
        return self, add_body, self.pair(), [(self.out.shape, f32)]

    def last(self):
        while len(self.left) > 1:
            slot([self.step()])
        return self.pair()


def adam_body(count, who, mine, got, *rest):
    ins, outs = rest[: 3 * count], rest[-4 * count :]
    half = mine.shape[1] // 2
    low, mid = who[1] == 0, who[2] == 0
    for one in range(count):
        first, second, weight = ins[3 * one : 3 * one + 3]
        first_new, second_new, update, sums = outs[4 * one : 4 * one + 4]
        rows = []
        for ref in (mine, got):
            a, b = ref[one, :half].astype(f32), ref[one, half:].astype(f32)
            rows.append((jnp.where(mid, a, b), jnp.where(mid, b, a)))
        near_rows, other_rows = rows
        grad = [jnp.where(low, a, b) for a, b in zip(near_rows, other_rows)]
        grad += [jnp.where(low, b, a) for a, b in zip(near_rows, other_rows)]
        moved = adam_moments(jnp.concatenate(grad, axis=0), first[...], second[...])
        master = weight[...]
        first_new[...], second_new[...] = moved[0], moved[1]
        change = moved[2] + decay_rate * master
        update[...] = change

        @pl.when(pl.program_id(0) == 0)
        def _(sums=sums):
            sums[...] = jnp.zeros_like(sums)

        sums[0:1, :] += jnp.sum(master * master, axis=0, keepdims=True)
        sums[1:2, :] += jnp.sum(change * change, axis=0, keepdims=True)


def adam(who, halves, matrices, wide, steps, columns, made, after, grad_at=None):
    count, rows = len(matrices), halves[0].shape[1]
    grad = pl.BlockSpec((count, rows, wide), grad_at or (lambda i: (0, 0, i)))
    ins, outs, args, extra, aliases = [SM, grad, grad], [], [who, *halves], [], {}
    for one, matrix in enumerate(matrices):
        block = pl.BlockSpec((matrix[2].shape[0], wide), lambda i, at=columns[one]: (0, at(i)))
        full = (jax.ShapeDtypeStruct(matrix[2].shape, f32), block)
        ins += [block] * 3
        args += matrix
        outs += [full] * 3 + [(jax.ShapeDtypeStruct((2, wide), f32), whole((2, wide)))]
        if made[one] is not None:
            extra += [(4 * one + k, v) for k, v in enumerate(made[one][:3])]
    for out, value in extra:
        aliases[len(ins)] = out
        ins.append(pl.BlockSpec(memory_space=pl.ANY))
        args.append(value)
    got = call(functools.partial(adam_body, count), (steps,), ins, outs, [], 32, tuple(args), "adam", after, aliases)
    return [got[4 * one : 4 * one + 4] for one in range(count)]


def total_body(*refs):
    *parts, out = refs
    for row, group in enumerate(parts_of(parts)):
        for kind in range(2):
            value = sum(jnp.sum(ref[kind : kind + 1, :]) for ref in group)
            out[4 * kind + row : 4 * kind + row + 1, :] = jnp.full((1, out.shape[1]), value, f32)


def parts_of(parts):
    return parts[0:2], parts[2:3], parts[3:5], parts[5:7]


def totals(sums):
    out = jax.ShapeDtypeStruct((8, 128), f32)
    return call(total_body, None, [VM] * len(sums), [(out, VM)], [], 8, tuple(sums), "totals")[0]


def apply_body(one, two, w0, w1, w2, w3, u0, u1, u2, u3, n0, n1, n2, n3, norms):
    total = one[...] + two[...]
    for row in range(4):
        for kind in range(2):
            norms[kind : kind + 1, row : row + 1] = jnp.sqrt(total[4 * kind + row : 4 * kind + row + 1, :1])
    for row, (w, u, n) in enumerate(((w0, u0, n0), (w1, u1, n1), (w2, u2, n2), (w3, u3, n3))):
        ratio = jnp.sqrt(total[row : row + 1, :1]) * lax.rsqrt(total[4 + row : 5 + row, :1] + adam_eps)
        n[...] = w[...] - (matrix_rate * ratio) * u[...]


def apply(one, two, weights, updates):
    steps = 3
    blocks = [pl.BlockSpec((w.shape[0], w.shape[1] // steps), lambda i: (0, i)) for w in weights]
    norms = jax.ShapeDtypeStruct((2, 4), f32)
    return call(
        apply_body,
        (steps,),
        [whole(one.shape)] * 2 + blocks + blocks,
        [(jax.ShapeDtypeStruct(w.shape, f32), b) for w, b in zip(weights, blocks)] + [(norms, whole(norms.shape))],
        [],
        24,
        (one, two, *weights, *updates),
        "apply",
    )


def vector_body(who, one, two, first, second, params, new, first_new, second_new):
    rows, cols = params.shape
    total = one[...] + two[...]
    grad = total[:rows, :cols]
    for block in range(1, 4):
        grad = jnp.where(who[0] == block, total[:rows, block * cols : (block + 1) * cols], grad)
    moved = adam_moments(grad, first[...], second[...])
    first_new[...], second_new[...] = moved[0], moved[1]
    new[...] = params[...] - vector_rate * moved[2]


def vector_step(who, one, two, first, second, params):
    out = jax.ShapeDtypeStruct(params.shape, f32)
    args = (who, one, two, first, second, params)
    return call(vector_body, None, [SM] + [VM] * 5, [(out, VM)] * 3, [], 8, args, "vector_step")


def adam_moments(grad, first, second):
    first_new = beta_one * first + (1.0 - beta_one) * grad
    second_new = beta_two * second + (1.0 - beta_two) * grad * grad
    direction = (
        first_new
        / (1.0 - beta_one**STEP)
        / (jnp.sqrt(second_new / (1.0 - beta_two**STEP)) + adam_eps)
    )
    return (first_new, second_new, direction)


def local(
    block_in,
    out_grad,
    caption_len,
    mask_marks,
    qkv_weight,
    out_weight,
    up_weight,
    down_weight,
    vector_params,
    qkv_first,
    qkv_second,
    out_first,
    out_second,
    up_first,
    up_second,
    down_first,
    down_second,
    vector_first,
    vector_second,
):
    width = block_in.shape[2]
    hidden = up_weight.shape[1]
    groups = width // (GROUP * HEAD)
    shard = lax.axis_index("fsdp")
    replica = lax.axis_index("dp")
    who = jnp.stack([shard, replica & 1, (replica >> 1) & 1]).astype(jnp.int32)
    cols = hidden // PARTS
    core = lambda v: swap(v, "fsdp", 0)
    far = lambda v: swap(v, "fsdp", 1)
    turned = lambda v: v.T

    own_one, own_more = cast_heads(qkv_weight, vector_params)
    far_one, far_more = far(own_one), far(own_more)
    own_out, half_up, half_down, *own_parts = cast_rest(who, out_weight.T, up_weight, down_weight.T, [own_one])
    dm, dmt, grad_bd = prep_grad(who, out_grad, [own_out])
    far_one = tie(far_one, dm)
    far_up, far_down, far_part = (far(v) for v in (half_up, half_down, own_parts[2]))
    core_parts = [core(v) for v in own_parts]
    first_block = lambda *arrays: [(v, 0) for v in arrays]
    one_shards = (own_one, core(own_one), far_one, core(far_one))

    marks = mask_marks.reshape(*mask_marks.shape, 1)
    vecs, xb, a = prep(who, caption_len, block_in, marks, one_shards, [])
    far_more = tie(far_more, xb)
    more_shards = (own_more, core(own_more), far_more, core(far_more))
    heads_full = [first_block(*one_shards)] + [[(v, g) for v in more_shards] for g in range(groups - 1)]
    sides = lambda mine: (mine, swap(mine, "dp", 0))
    heads = [attend(who, caption_len, a, heads_full[0], vecs, 0, [far_more])]
    own_out = tie(own_out, heads[0][0])
    up_far = sides(tie(far_up, heads[0][0]))
    heads.append(attend(who, caption_len, a, heads_full[1], vecs, 1, [heads[0][0], up_far[0]]))
    down_far = sides(tie(far_down, heads[1][0]))
    heads.append(attend(who, caption_len, a, heads_full[2], vecs, 2, [heads[1][0], down_far[0], up_far[1]]))
    far_out = far(own_out)
    out_full = first_block(own_out, core(own_out), far_out, core(far_out))
    outs = [h[1] for h in heads]
    y, c, ct = mix(who, xb, outs, out_full, vecs, [down_far[1]])
    ups = first_block(own_parts[0], core_parts[0], *up_far, *(core(v) for v in up_far))
    downs = first_block(own_parts[1], core_parts[1], *down_far, *(core(v) for v in down_far))
    ffn0 = ffn(who, c, dm, ct, dmt, ups, downs, vecs, 0, [])
    chunk_a = Chunk([ffn0[0], ffn0[2]], [[ffn0[1]], [ffn0[3]]])
    at = turn_rows(who, a, [afar(ffn0[4])])
    done = slot([chunk_a.first()], at)
    far_part = tie(far_part, ffn0[4])
    shards1 = (own_parts[2], core_parts[2], far_part, core(far_part))
    ups1 = first_block(*shards1)
    downs1 = [(v, cols // BLOCK) for v in shards1]
    ffn1 = ffn(who, c, dm, ct, dmt, ups1, downs1, vecs, 1, done)
    chunk_b = Chunk([ffn1[0], ffn1[2]], [[ffn1[1]], [ffn1[3]]])
    done = slot([chunk_a.second()], afar(ffn1[5]))
    done = slot([chunk_b.first()], *done)
    dy, out_keep, out_send, *dos, grad_mid = turn(who, [ffn0[6], ffn1[6]], y, dm, outs, out_full, vecs, done)
    done = slot([chunk_a.third()], grad_mid)
    back0 = attend_back(caption_len, heads[0][0], dos[0], heads[0][2], at, 1, done)
    chunk_c = Chunk([out_keep, back0[1]], [[out_send], back0[3:]])
    done = slot([chunk_b.second(), chunk_a.rest()], back0[2])
    back1 = attend_back(caption_len, heads[1][0], dos[1], heads[1][2], at, 1, done)
    done = slot([chunk_b.third(), chunk_c.first()], back1[2])
    back2 = attend_back(caption_len, heads[2][0], dos[2], heads[2][2], at, 3, done)
    backs = [back0, back1, back2]
    chunk_d = Chunk([back1[1], back2[1]], [back1[3:], back2[3:]])
    done = slot([chunk_b.rest(), chunk_a.part(), chunk_c.second()], back2[2])
    done = slot([chunk_d.first()], *done)
    sums = [b[2] for b in backs] + [grad_mid] + [afar(v) for v in (grad_bd, ffn0[5], ffn1[5])]
    input_grad, vector_grads = start_back(
        who, caption_len, [b[0] for b in backs], heads_full, xb, dy, marks, vecs, sums, done
    )
    rows = Rows(vector_grads)
    done = slot([chunk_b.part(), chunk_a.half(), chunk_c.third(), chunk_d.second()], vector_grads)
    block_out, token = finish(who, y, [ffn0[4], ffn1[4]], [downs, downs1], vecs, done)

    qkv = (qkv_first, qkv_second, qkv_weight)
    out = tuple(turned(v) for v in (out_first, out_second, out_weight))
    up = (up_first, up_second, up_weight)
    down = tuple(turned(v) for v in (down_first, down_second, down_weight))
    wide = 3 * TILE
    per = cols // wide
    done = slot([chunk_b.half(), chunk_c.rest(), chunk_d.third(), rows.step()], token)
    column = lambda first, step: lambda i: first + step * i
    second = lambda i: (1, 0, i)
    halves_a = chunk_a.halves()
    (up0,) = adam(who, halves_a, [up], wide, per, [column(0, 1)], [None], done)
    done = slot([chunk_d.rest(), rows.step()], up0[3])
    (down0,) = adam(who, halves_a, [down], wide, per, [column(0, 1)], [None], done, second)
    done = slot([chunk_c.part(), rows.step()], down0[3])
    halves_b = chunk_b.halves()
    (up1,) = adam(who, halves_b, [up], wide, per, [column(per, 1)], [up0], done)
    done = slot([chunk_c.half(), chunk_d.part()], up1[3])
    (down1,) = adam(who, halves_b, [down], wide, per, [column(per, 1)], [down0], done, second)
    done = slot([chunk_d.half(), rows.step()], down1[3])
    outer, qkv0 = adam(
        who, chunk_c.halves(), [out, qkv], TILE, 3, [column(0, 1), column(0, groups)], [None] * 2, done
    )
    vector_one, got = rows.last()
    columns = [lambda i: groups * (i % 3) + 1 + i // 3]
    steps = 3 * (groups - 1)
    (qkv1,) = adam(who, chunk_d.halves(), [qkv], TILE, steps, columns, [qkv0], [qkv0[3]], lambda i: (i // 3, 0, i % 3))
    vector_new, vector_first_new, vector_second_new = vector_step(
        who, vector_one, got, vector_first, vector_second, vector_params
    )
    squares = totals([qkv0[3], qkv1[3], outer[3], up0[3], up1[3], down0[3], down1[3]])
    squares = squares + core(squares)
    weights = (qkv_weight, out[2], up_weight, down[2])
    made = (qkv1, outer, up1, down1)
    *new_weights, norms = apply(squares, far(squares), weights, [m[2] for m in made])
    back = (lambda v: v, turned, lambda v: v, turned)
    moments = [f(m[k]) for f, m in zip(back, made) for k in range(2)]
    return (
        block_out,
        input_grad,
        *(f(w) for f, w in zip(back, new_weights)),
        vector_new,
        *moments,
        vector_first_new,
        vector_second_new,
        norms,
    )


def solution(mesh):
    placed = (
        P(("dp", "fsdp"), None, None),
        P(("dp", "fsdp"), None, None),
        P(("dp", "fsdp")),
        P(("dp", "fsdp"), None),
        P("fsdp", None),
        P(None, "fsdp"),
        P("fsdp", None),
        P(None, "fsdp"),
        P(None, "fsdp"),
        P("fsdp", None),
        P("fsdp", None),
        P(None, "fsdp"),
        P(None, "fsdp"),
        P("fsdp", None),
        P("fsdp", None),
        P(None, "fsdp"),
        P(None, "fsdp"),
        P(None, "fsdp"),
        P(None, "fsdp"),
    )
    return jax.shard_map(
        local,
        mesh=mesh,
        in_specs=placed,
        out_specs=(
            P(("dp", "fsdp"), None, None),
            P(("dp", "fsdp"), None, None),
            P("fsdp", None),
            P(None, "fsdp"),
            P("fsdp", None),
            P(None, "fsdp"),
            P(None, "fsdp"),
            P("fsdp", None),
            P("fsdp", None),
            P(None, "fsdp"),
            P(None, "fsdp"),
            P("fsdp", None),
            P("fsdp", None),
            P(None, "fsdp"),
            P(None, "fsdp"),
            P(None, "fsdp"),
            P(None, "fsdp"),
            P(),
        ),
        check_vma=False,
    )
```

```python
import functools

import jax
import jax.numpy as jnp
from jax import lax
from jax.experimental import pallas as pl
from jax.experimental.pallas import tpu as pltpu
from jax.sharding import PartitionSpec as P

HEAD = 64
TXT = 40
PATCH = 145
STEP = 7
SEQ = TXT + PATCH
PAD = 192
GROUP = 4
PARTS = 2
EXTRA = 16
LIGHT = 10**4
TILE = 256
BLOCK = 768

ln_eps = 1e-06
beta_one = 0.5
beta_two = 0.55
adam_eps = 1e-06
decay_rate = 0.01
matrix_rate = 0.5
vector_rate = 0.3

f32 = jnp.float32
bf16 = jnp.bfloat16
ORDER = (0, 2, 1, 3)
NT = (((1,), (1,)), ((), ()))
TN = (((0,), (0,)), ((), ()))

VM = pl.BlockSpec(memory_space=pltpu.VMEM)
SM = pl.BlockSpec(memory_space=pltpu.SMEM)


def dot(left, right, dims=None):
    if dims is None:
        return jnp.dot(left, right, preferred_element_type=f32)
    return lax.dot_general(left, right, dims, preferred_element_type=f32)


def call(body, grid, ins, outs, scratch, limit, args, name, after=(), aliases=None, flops=8 * 10**9):
    count = len(ins)
    after = [afar(v) if v.size > 65536 else v for v in after]

    def run(*refs):
        body(*refs[:count], *refs[count + len(after) :])

    return pl.pallas_call(
        run,
        grid=grid or (),
        in_specs=list(ins) + [pl.BlockSpec(memory_space=pl.ANY)] * len(after),
        out_specs=[o[1] for o in outs],
        out_shape=[o[0] for o in outs],
        input_output_aliases=aliases or {},
        scratch_shapes=scratch,
        compiler_params=pltpu.CompilerParams(vmem_limit_bytes=limit << 20),
        cost_estimate=pl.CostEstimate(flops=flops, bytes_accessed=flops // 200, transcendentals=0),
        name=name,
    )(*args, *after)


def far_mem(shape, dtype):
    return pltpu.HBM(tuple(shape), dtype)


def near_mem(shape, dtype):
    return pltpu.VMEM(tuple(shape), dtype)


def near(value):
    return pltpu.with_memory_space_constraint(value, pltpu.VMEM)


def afar(value):
    return pltpu.with_memory_space_constraint(value, pltpu.HBM)


def tie(value, *deps):
    return pl.pallas_call(
        lambda *refs: None,
        in_specs=[pl.BlockSpec(memory_space=pl.ANY)] * (1 + len(deps)),
        out_specs=pl.BlockSpec(memory_space=pl.ANY),
        out_shape=jax.ShapeDtypeStruct(value.shape, value.dtype),
        input_output_aliases={0: 0},
        cost_estimate=pl.CostEstimate(flops=LIGHT, bytes_accessed=LIGHT, transcendentals=0),
        name="tie",
    )(value, *[afar(v) if v.size > 65536 else v for v in deps])


def whole(shape):
    return pl.BlockSpec(shape, lambda i: (0,) * len(shape), pipeline_mode=pl.Buffered(1))


def wholes(*arrays):
    return [whole(v.shape) for v in arrays]


def shard_specs(shards, wide, columns, free=False):
    rows = lambda v: v.shape[0] - v.shape[0] % 96
    specs = [pl.BlockSpec((rows(v), wide), lambda i, at=at: (0, at + columns(i))) for v, at in shards]
    return specs, [v if free and place else afar(v) for place, (v, _) in enumerate(shards)]


def unit_rows(rows):
    centred = rows - jnp.mean(rows, axis=-1, keepdims=True)
    factor = lax.rsqrt(jnp.mean(centred * centred, axis=-1, keepdims=True) + ln_eps)
    return centred * factor, factor


def unit_back(grad_normed, unit, factor, gain):
    grad_unit = grad_normed * gain
    return factor * (
        grad_unit
        - jnp.mean(grad_unit, axis=-1, keepdims=True)
        - unit * jnp.mean(grad_unit * unit, axis=-1, keepdims=True)
    )


def put_turned(who_ref, value, scratch, out_ref):
    part = out_ref.shape[0] // 16
    scratch[...] = value.T
    for place in range(16):
        core, one, two, three = (place >> 3) & 1, (place >> 2) & 1, (place >> 1) & 1, place & 1
        odd = (who_ref[0] & 1) ^ core
        pair = jnp.where(odd == 0, one, two)
        low = jnp.where(odd == 0, two, one)
        start = 4 * (who_ref[0] ^ (2 * pair + core)) + 2 * (who_ref[1] ^ low) + (who_ref[2] ^ three)
        out_ref[place * part : (place + 1) * part, :] = scratch[pl.ds(pl.multiple_of(start * part, 16), part), :]


def gather_rows(who_ref, refs, out_ref):
    rows = refs[0].shape[0]
    half = rows // 2
    places = [(0, None), (1, None)]
    places += [(2, None), (3, None)] if len(refs) == 4 else [(2, 0), (2, 1), (3, 0), (3, 1)]
    for (other, part), ref in zip(places, refs):
        start = (who_ref[0] ^ other) * rows
        if part is not None:
            start += (who_ref[1] ^ part) * half
        out_ref[pl.ds(pl.multiple_of(start, 32), ref.shape[0]), :] = ref[...]


def cast_heads_body(q_ref, k_ref, v_ref, *rest):
    wide = GROUP * HEAD
    rows = q_ref.shape[0]
    out_ref = rest[-1]
    for kind, ref in enumerate((q_ref, k_ref, v_ref)):
        out_ref[:rows, kind * wide : (kind + 1) * wide] = ref[...].astype(bf16)
    if len(rest) > 1:
        count, cols = rest[0].shape
        out_ref[rows:, :] = jnp.zeros_like(out_ref[rows:, :])
        out_ref[rows : rows + count, :cols] = rest[0][...].astype(bf16)


def cast_heads(weight, first, steps, vectors, after):
    rows, cols = weight.shape
    wide = GROUP * HEAD
    groups = cols // (3 * wide)
    blocks = [pl.BlockSpec((rows, wide), lambda i, kind=kind: (0, kind * groups + first + i)) for kind in range(3)]
    high = rows + (EXTRA if vectors else 0)
    out = (far_mem((high, 3 * wide * steps), bf16), pl.BlockSpec((high, 3 * wide), lambda i: (0, i)))
    args = (*[afar(weight)] * 3, *[afar(v) for v in vectors])
    return call(cast_heads_body, (steps,), blocks + wholes(*vectors), [out], [], 12, args, "cast_heads", after)[0]


def cast_rest_body(who, out_ref, up_ref, down_ref, o_ref, up_half, down_half, *parts):
    half = up_half.shape[0]
    rows = pl.ds(pl.multiple_of(who[1] * half, 32), half)
    step = pl.program_id(0)
    per = pl.num_programs(0) // PARTS

    @pl.when(step == 0)
    def _():
        o_ref[...] = out_ref[...].astype(bf16)

    @pl.when(step < per)
    def _():
        up_half[...] = up_ref[rows, :].astype(bf16)
        down_half[...] = down_ref[rows, :].astype(bf16)

    @pl.when(step < per)
    def _():
        parts[0][...] = up_ref[...].astype(bf16)
        parts[1][...] = down_ref[...].astype(bf16)

    wide = up_ref.shape[1]
    for place in range(per):

        @pl.when(step == per + place)
        def _(place=place):
            parts[2][:, place * wide : (place + 1) * wide] = up_ref[...].astype(bf16)
            parts[2][:, (per + place) * wide : (per + place + 1) * wide] = down_ref[...].astype(bf16)


def cast_rest(who, out_t, up, down_t, after):
    rows, hidden = up.shape
    cols = wide = hidden // PARTS
    per = cols // wide
    block = pl.BlockSpec((rows, wide), lambda i: (0, i))
    at = lambda part: lambda i: (0, jnp.clip(i - part * per, 0, per - 1))
    out = lambda n, part: (far_mem((n, cols), bf16), pl.BlockSpec((n, wide), at(part)))
    outs = [(far_mem(out_t.shape, bf16), whole(out_t.shape)), out(rows // 2, 0), out(rows // 2, 0)]
    both = (rows, 2 * cols)
    outs += [out(rows, 0), out(rows, 0), (far_mem(both, bf16), whole(both))]
    ins = [SM] + wholes(out_t) + [block, block]
    args = (who, out_t, afar(up), afar(down_t))
    return call(cast_rest_body, (hidden // wide,), ins, outs, [], 24, args, "cast_rest", after)


def chosen_rows(marks, length):
    places = lax.broadcasted_iota(jnp.int32, marks.shape, 0)
    return jnp.where((marks == 1) & (places >= 1) & (places < length), 1.0, 0.0)


def spread_rows(chosen, width):
    return jnp.broadcast_to(chosen, (chosen.shape[0], width)) > 0


def prep_grad_body(who, g_ref, dm_ref, dmt_ref, bd_ref, all_ref, scratch):
    step = pl.program_id(0)
    tail = jnp.zeros((PAD - SEQ, g_ref.shape[2]), f32)
    dm = jnp.concatenate([g_ref[0].astype(f32), tail], axis=0)
    dm_ref[...] = dm.astype(bf16)
    all_ref[pl.ds(pl.multiple_of(step * PAD, PAD), PAD), :] = dm.astype(bf16)

    @pl.when(step == 0)
    def _():
        bd_ref[...] = jnp.zeros_like(bd_ref)

    bd_ref[...] += jnp.sum(dm, axis=0, keepdims=True)

    @pl.when(step == pl.num_programs(0) - 1)
    def _():
        put_turned(who, all_ref[...], scratch, dmt_ref)


def prep_grad(who, out_grad, after):
    items, seq, width = out_grad.shape
    rows = items * PAD
    item = pl.BlockSpec((1, seq, width), lambda i: (i, 0, 0))
    return call(
        prep_grad_body,
        (items,),
        [SM, item],
        [
            (far_mem((rows, width), bf16), pl.BlockSpec((PAD, width), lambda i: (i, 0))),
            (far_mem((width, rows), bf16), whole((width, rows))),
            (far_mem((1, width), f32), whole((1, width))),
        ],
        [pltpu.VMEM((rows, width), bf16), pltpu.VMEM((width, rows), bf16)],
        20,
        (who, afar(out_grad)),
        "prep_grad",
        after,
        flops=LIGHT,
    )


def prep_body(who, len_ref, x_ref, mark_ref, v0, v1, v2, v3, vec_ref, xb_ref, a_ref):
    step = pl.program_id(0)
    width = x_ref.shape[2]

    @pl.when(step == 0)
    def _():
        cols = width // 4
        for block in range(4):
            value = v0[:, :cols].astype(f32)
            for other, ref in ((1, v1), (2, v2), (3, v3)):
                value = jnp.where((who[0] ^ other) == block, ref[:, :cols].astype(f32), value)
            vec_ref[:, block * cols : (block + 1) * cols] = value

    gain, shift, embed = vec_ref[0:1, :], vec_ref[1:2, :], vec_ref[12:13, :]
    x = x_ref[0].astype(f32)
    marked = spread_rows(chosen_rows(mark_ref[0], len_ref[step]), width)
    tail = jnp.zeros((PAD - SEQ, width), f32)
    x = jnp.concatenate([jnp.where(marked, embed, x[:TXT]), x[TXT:], tail], axis=0)
    xb_ref[...] = x.astype(bf16)
    unit, _ = unit_rows(x)
    a_ref[...] = (unit * gain + shift).astype(bf16)


def turn_rows_body(who, a_ref, at_ref, scratch):
    put_turned(who, a_ref[...], scratch, at_ref)


def turn_rows(who, a, after):
    rows, width = a.shape
    out = (far_mem((width, rows), bf16), whole((width, rows)))
    scratch = [pltpu.VMEM((width, rows), bf16)]
    return call(turn_rows_body, (1,), [SM] + wholes(a), [out], scratch, 16, (who, afar(a)), "turn_rows", after)[0]


def prep(who, lengths, block_in, marks, vec_shards, after):
    items, seq, width = block_in.shape
    rows = items * PAD
    item = lambda *shape: pl.BlockSpec((1, *shape), lambda i: (i, 0, 0))
    flat = pl.BlockSpec((PAD, width), lambda i: (i, 0))
    extra = pl.BlockSpec((EXTRA, width), lambda i: (vec_shards[0].shape[0] // EXTRA - 1, 0))
    return call(
        prep_body,
        (items,),
        [SM, SM, item(seq, width), item(*marks.shape[1:])] + [extra] * 4,
        [
            (near_mem((16, width), f32), whole((16, width))),
            (far_mem((rows, width), bf16), flat),
            (far_mem((rows, width), bf16), flat),
        ],
        [],
        16,
        (who, lengths, afar(block_in), marks, *[afar(v) for v in vec_shards]),
        "prep",
        after,
        flops=LIGHT,
    )


def key_mask(length):
    places = lax.broadcasted_iota(jnp.int32, (PAD, 1), 0)
    return ((places >= TXT) & (places < SEQ)) | (places < length)


def half_masks():
    lanes = lax.broadcasted_iota(jnp.int32, (1, 2 * HEAD), 1)
    low = jnp.where(lanes < HEAD, 1.0, 0.0)
    return low.astype(bf16), (1.0 - low).astype(bf16)


def scaled_masks():
    return [(mask.astype(f32) * HEAD ** (-0.5)).astype(bf16) for mask in half_masks()]


def attend_body(group, who, len_ref, a_ref, vec_ref, *rest):
    wide = GROUP * HEAD
    shards, (qkv_ref, o_ref, st_ref, w_ref) = rest[:-4], rest[-4:]
    gather_rows(who, shards, w_ref)
    cols = slice(group * wide, (group + 1) * wide)
    bias = jnp.concatenate([vec_ref[2:3, cols], jnp.zeros((1, wide), f32), vec_ref[3:4, cols]], axis=1)
    qkv_ref[...] = (dot(a_ref[...], w_ref[...]) + bias).astype(bf16)
    halves, scaled = half_masks(), scaled_masks()

    @pl.loop(0, len_ref.shape[0])
    def _(item):
        rows = pl.ds(pl.multiple_of(item * PAD, PAD), PAD)
        valid = key_mask(len_ref[item])
        for pair in range(GROUP // 2):
            at = pair * 2 * HEAD
            q = qkv_ref[rows, at : at + 2 * HEAD]
            k = qkv_ref[rows, wide + at : wide + at + 2 * HEAD]
            v = qkv_ref[rows, 2 * wide + at : 2 * wide + at + 2 * HEAD]
            out = None
            for half in range(2):
                s = dot(k * scaled[half], q, NT)
                s = jnp.where(valid, s, -1000000000.0)
                top = jnp.max(s, axis=0, keepdims=True)
                e = jnp.exp(s - top)
                scale = 1.0 / jnp.sum(e, axis=0, keepdims=True)
                p = (e * scale).astype(bf16)
                part = dot(p, v * halves[half], TN)
                out = part if out is None else out + part
                head = 2 * pair + half
                st_ref[item, head : head + 1, :] = top
                st_ref[item, GROUP + head : GROUP + head + 1, :] = scale
            o_ref[rows, at : at + 2 * HEAD] = out.astype(bf16)


def attend(who, lengths, a, weights, vecs, group, after):
    rows, width = a.shape
    wide = GROUP * HEAD
    items = lengths.shape[0]
    specs, arrays = shard_specs(weights, 3 * wide, lambda i: 0)
    return call(
        functools.partial(attend_body, group),
        (1,),
        [SM, SM, whole(a.shape), whole(vecs.shape)] + specs,
        [
            (far_mem((rows, 3 * wide), bf16), whole((rows, 3 * wide))),
            (far_mem((rows, wide), bf16), whole((rows, wide))),
            (far_mem((items, 2 * GROUP, PAD), f32), whole((items, 2 * GROUP, PAD))),
        ],
        [pltpu.VMEM((width, 3 * wide), bf16)],
        16,
        (who, lengths, afar(a), vecs, *arrays),
        "attend",
        after,
    )


def mix_body(who, x_ref, o0, o1, o2, vec_ref, *rest):
    shards, (y_ref, c_ref, ct_ref, w_ref, scratch) = rest[:-5], rest[-5:]
    gather_rows(who, shards, w_ref)
    wide = GROUP * HEAD
    acc = x_ref[...].astype(f32) + vec_ref[4:5, :]
    for group, o in enumerate((o0, o1, o2)):
        acc += dot(o[...], w_ref[:, group * wide : (group + 1) * wide], NT)
    y_ref[...] = acc
    unit, _ = unit_rows(acc)
    c_ref[...] = (unit * vec_ref[5:6, :] + vec_ref[6:7, :]).astype(bf16)
    put_turned(who, c_ref[...], scratch, ct_ref)


def mix(who, xb, outs, weights, vecs, after):
    rows, width = xb.shape
    specs, arrays = shard_specs(weights, width, lambda i: 0)
    return call(
        mix_body,
        (1,),
        [SM, whole(xb.shape)] + [whole(o.shape) for o in outs] + [whole(vecs.shape)] + specs,
        [
            (far_mem((rows, width), f32), whole((rows, width))),
            (near_mem((rows, width), bf16), whole((rows, width))),
            (near_mem((width, rows), bf16), whole((width, rows))),
        ],
        [pltpu.VMEM((width, width), bf16), pltpu.VMEM((width, rows), bf16)],
        18,
        (who, afar(xb), *[afar(o) for o in outs], vecs, *arrays),
        "mix",
        after,
    )


def item_rows(cols):
    return pl.BlockSpec((PAD, cols), lambda i: (i, 0))


def gelu_pair(h):
    bell = jnp.exp(-0.5 * h * h)
    t = 1.0 / (1.0 + (0.3275911 * 0.7071067811865476) * jnp.abs(h))
    poly = t * (0.127414796 + t * (-0.142248368 + t * (0.7107068705 + t * (-0.7265760135 + t * 0.5307027145))))
    tail = poly * bell
    return jnp.where(h < 0, tail, 1.0 - tail), bell


def ffn_body(counts, base, who, c_ref, dm_ref, ct_ref, dmt_ref, *rest):
    ups, downs, rest = rest[: counts[0]], rest[counts[0] : sum(counts)], rest[sum(counts) :]
    bu_ref, uk_ref, us_ref, dk_ref, ds_ref, gelu_ref, gbu_ref, dc_ref, up_w, down_w = rest

    @pl.when(pl.program_id(0) == 0)
    def _():
        dc_ref[...] = jnp.zeros_like(dc_ref)

    gather_rows(who, ups, up_w)
    gather_rows(who, downs, down_w)
    row = (base + pl.program_id(0)) // (c_ref.shape[1] // BLOCK)
    h = dot(c_ref[...], up_w[...]) + bu_ref[pl.ds(row, 1), :]
    phi, bell = gelu_pair(h)
    gelu = (h * phi).astype(bf16)
    gelu_ref[...] = gelu
    slope = phi + h * bell * 0.3989422804014327
    dh = (dot(dm_ref[...], down_w[...]) * slope).astype(bf16)
    gbu_ref[...] = jnp.sum(dh.astype(f32), axis=0, keepdims=True)
    half = uk_ref.shape[0]
    grad = dot(ct_ref[...], dh).astype(bf16)
    uk_ref[...], us_ref[...] = grad[:half], grad[half:]
    grad = dot(dmt_ref[...], gelu).astype(bf16)
    dk_ref[...], ds_ref[...] = grad[:half], grad[half:]
    dc_ref[...] += dot(dh, up_w[...], NT)


def ffn(who, c, dm, ct, dmt, ups, downs, vecs, part, after):
    rows, width = c.shape
    cols = 4 * width // PARTS
    base, across = part * cols // BLOCK, width // BLOCK
    up_specs, up_arrays = shard_specs(ups, BLOCK, lambda i: i, part > 0)
    down_specs, down_arrays = shard_specs(downs, BLOCK, lambda i: i, part > 0)
    half = near_mem((width // 2, cols), bf16)
    hspec = pl.BlockSpec((width // 2, BLOCK), lambda i: (0, i))
    return call(
        functools.partial(ffn_body, (len(ups), len(downs)), base),
        (cols // BLOCK,),
        [SM, whole(c.shape), whole(dm.shape), whole(ct.shape), whole(dmt.shape)]
        + up_specs
        + down_specs
        + [pl.BlockSpec((8, BLOCK), lambda i: (1, (base + i) % across))],
        [
            (half, hspec),
            (half, hspec),
            (half, hspec),
            (half, hspec),
            (far_mem((rows, cols), bf16), pl.BlockSpec((rows, BLOCK), lambda i: (0, i))),
            (far_mem((1, cols), f32), pl.BlockSpec((1, BLOCK), lambda i: (0, i))),
            (far_mem((rows, width), f32), whole((rows, width))),
        ],
        [pltpu.VMEM((width, BLOCK), bf16), pltpu.VMEM((width, BLOCK), bf16)],
        36,
        (who, c, dm, ct, dmt, *up_arrays, *down_arrays, vecs),
        "ffn",
        after,
    )


def turn_body(who, dc0_ref, dc1_ref, y_ref, dm_ref, o0, o1, o2, vec_ref, *rest):
    shards, rest = rest[:-11], rest[-11:]
    dy_ref, gk_ref, gs_ref, do0, do1, do2, gv_ref, w_ref, all_ref, scratch, drt_ref = rest
    step = pl.program_id(0)

    @pl.when(step == 0)
    def _():
        gather_rows(who, shards, w_ref)
        gv_ref[...] = jnp.zeros_like(gv_ref)

    wide = GROUP * HEAD
    here = pl.ds(pl.multiple_of(step * PAD, PAD), PAD)
    dc = dc0_ref[...] + dc1_ref[...]
    unit, factor = unit_rows(y_ref[...])
    gv_ref[0:1, :] += jnp.sum(dc * unit, axis=0, keepdims=True)
    gv_ref[1:2, :] += jnp.sum(dc, axis=0, keepdims=True)
    dy = dm_ref[...].astype(f32) + unit_back(dc, unit, factor, vec_ref[5:6, :])
    dy_ref[...] = dy
    dr = dy.astype(bf16)
    gv_ref[2:3, :] += jnp.sum(dr.astype(f32), axis=0, keepdims=True)
    all_ref[here, :] = dr

    @pl.when(step == pl.num_programs(0) - 1)
    def _():
        put_turned(who, all_ref[...], scratch, drt_ref)
        half = gk_ref.shape[0]
        for group, (o, do) in enumerate(((o0, do0), (o1, do1), (o2, do2))):
            cols = slice(group * wide, (group + 1) * wide)
            do[...] = dot(all_ref[...], w_ref[:, cols]).astype(bf16)
            grad = dot(drt_ref[...], o[...]).astype(bf16)
            gk_ref[:, cols] = grad[:half]
            gs_ref[:, cols] = grad[half:]


def turn(who, dcs, y, dm, outs, weights, vecs, after):
    rows, width = y.shape
    half = jax.ShapeDtypeStruct((width // 2, width), bf16)
    do = (jax.ShapeDtypeStruct((rows, GROUP * HEAD), bf16), whole((rows, GROUP * HEAD)))
    small = jax.ShapeDtypeStruct((3, width), f32)
    specs, arrays = shard_specs(weights, width, lambda i: 0)
    flat, across = pltpu.VMEM((rows, width), bf16), pltpu.VMEM((width, rows), bf16)
    return call(
        turn_body,
        (rows // PAD,),
        [SM] + [item_rows(width)] * 4 + wholes(*outs, vecs) + specs,
        [(far_mem((rows, width), f32), item_rows(width))]
        + [(half, whole(half.shape))] * 2
        + [do] * 3
        + [(small, whole(small.shape))],
        [pltpu.VMEM((width, width), bf16), flat, across, across],
        32,
        (who, *[afar(v) for v in dcs], afar(y), afar(dm), *[afar(o) for o in outs], vecs, *arrays),
        "turn",
        after,
    )


def attend_back_body(len_ref, qkv_ref, do_ref, st_ref, at_ref, d_ref, gk_ref, gb_ref, *gs_refs):
    wide = GROUP * HEAD
    halves, scaled = half_masks(), scaled_masks()

    @pl.loop(0, len_ref.shape[0])
    def _(item):
        rows = pl.ds(pl.multiple_of(item * PAD, PAD), PAD)
        valid = key_mask(len_ref[item])
        for pair in range(GROUP // 2):
            at = pair * 2 * HEAD
            q = qkv_ref[rows, at : at + 2 * HEAD]
            k = qkv_ref[rows, wide + at : wide + at + 2 * HEAD]
            v = qkv_ref[rows, 2 * wide + at : 2 * wide + at + 2 * HEAD]
            do = do_ref[rows, at : at + 2 * HEAD]
            dq = dk = dv = jnp.zeros((PAD, 2 * HEAD), f32)
            for half in range(2):
                head = 2 * pair + half
                km = k * scaled[half]
                s = dot(km, q, NT)
                s = jnp.where(valid, s, -1000000000.0)
                p = jnp.exp(s - st_ref[item, head : head + 1, :]) * st_ref[item, GROUP + head : GROUP + head + 1, :]
                dv += dot(p.astype(bf16), do * halves[half])
                dp = dot(v * halves[half], do, NT)
                delta = jnp.sum(dp * p, axis=0, keepdims=True)
                ds = (p * (dp - delta)).astype(bf16)
                dk += dot(ds, q * scaled[half])
                dq += dot(ds, km, TN)
            d_ref[rows, at : at + 2 * HEAD] = dq.astype(bf16)
            d_ref[rows, wide + at : wide + at + 2 * HEAD] = dk.astype(bf16)
            d_ref[rows, 2 * wide + at : 2 * wide + at + 2 * HEAD] = dv.astype(bf16)

    half = gk_ref.shape[0]
    grad = dot(at_ref[...], d_ref[...]).astype(bf16)
    gk_ref[...] = grad[:half]
    for ref in gs_refs:
        ref[...] = grad[half : half + ref.shape[0]]
        half += ref.shape[0]
    gb_ref[...] = jnp.sum(d_ref[...].astype(f32), axis=0, keepdims=True)


def attend_back(lengths, qkv, do, stats, at, pieces, after):
    rows, wide3 = qkv.shape
    width = at.shape[0]
    half = jax.ShapeDtypeStruct((width // 2, wide3), bf16)
    piece = jax.ShapeDtypeStruct((width // 2 // pieces, wide3), bf16)
    return call(
        attend_back_body,
        None,
        [SM, VM, VM, VM, VM],
        [
            (jax.ShapeDtypeStruct((rows, wide3), bf16), VM),
            (half, VM),
            (jax.ShapeDtypeStruct((1, wide3), f32), VM),
        ]
        + [(piece, VM)] * pieces,
        [],
        16,
        (lengths, qkv, do, stats, at),
        "attend_back",
        after,
    )


def start_back_body(counts, who, len_ref, d0, d1, d2, xb_ref, dy_ref, mark_ref, vec_ref, gb0, gb1, gb2, mid_ref, bd_ref, bu0, bu1, *rest):
    shards, (out_ref, gv_ref, w_ref, da_ref) = rest[:-4], rest[-4:]
    at = 0
    wide3 = d0.shape[1]
    acc = None
    for group, d in enumerate((d0, d1, d2)):
        gather_rows(who, shards[at : at + counts[group]], w_ref.at[group])
        at += counts[group]
        part = dot(d[...], w_ref[group], NT)
        acc = part if acc is None else acc + part
    da_ref[...] = acc
    gain_grad = shift_grad = embed_grad = jnp.zeros((1, xb_ref.shape[1]), f32)
    for item in range(out_ref.shape[0]):
        rows = slice(item * PAD, (item + 1) * PAD)
        da = da_ref[rows, :]
        unit, factor = unit_rows(xb_ref[rows, :].astype(f32))
        gain_grad += jnp.sum(da * unit, axis=0, keepdims=True)
        shift_grad += jnp.sum(da, axis=0, keepdims=True)
        dx = dy_ref[rows, :] + unit_back(da, unit, factor, vec_ref[0:1, :])
        marked = spread_rows(chosen_rows(mark_ref[item], len_ref[item]), dx.shape[1])
        text = dx[:TXT]
        embed_grad += jnp.sum(jnp.where(marked, text, 0.0), axis=0, keepdims=True)
        out_ref[item] = jnp.concatenate([jnp.where(marked, 0.0, text), dx[TXT:SEQ]], axis=0)
    wide, width = GROUP * HEAD, gv_ref.shape[1]
    gv_ref[...] = jnp.zeros_like(gv_ref)
    gv_ref[0:1, :] = gain_grad
    gv_ref[1:2, :] = shift_grad
    for group, gb in enumerate((gb0, gb1, gb2)):
        gv_ref[2:3, group * wide : (group + 1) * wide] = gb[:, :wide]
        gv_ref[3:4, group * wide : (group + 1) * wide] = gb[:, 2 * wide :]
    gv_ref[4:5, :] = mid_ref[2:3, :]
    gv_ref[5:7, :] = mid_ref[0:2, :]
    gv_ref[7:8, :] = bd_ref[...]
    for row, (ref, place) in enumerate(((bu0, 0), (bu0, 1), (bu1, 0), (bu1, 1))):
        gv_ref[8 + row : 9 + row, :] = ref[:, place * width : (place + 1) * width]
    gv_ref[12:13, :] = embed_grad


def start_back(who, lengths, grads, weights, xb, dy, marks, vecs, sums, after):
    rows, width = xb.shape
    wide3 = grads[0].shape[1]
    specs, arrays = shard_specs([w for ws in weights for w in ws], wide3, lambda i: 0, True)
    out = far_mem((rows // PAD, SEQ, width), f32)
    small = jax.ShapeDtypeStruct((16, width), f32)
    return call(
        functools.partial(start_back_body, [len(ws) for ws in weights]),
        (1,),
        [SM, SM] + [whole(v.shape) for v in (*grads, xb, dy, marks, vecs, *sums)] + specs,
        [(out, whole(out.shape)), (small, whole(small.shape))],
        [pltpu.VMEM((len(weights), width, wide3), bf16), pltpu.VMEM((rows, width), f32)],
        28,
        (who, lengths, *grads, afar(xb), afar(dy), marks, vecs, *sums, *arrays),
        "start_back",
        after,
    )


def finish_body(counts, who, y_ref, vec_ref, *rest):
    parts = len(counts)
    gelus, rest = rest[:parts], rest[parts:]
    shards, (out_ref, token, acc_ref, *w_refs) = rest[: sum(counts)], rest[sum(counts) :]
    token[...] = jnp.zeros(TOKEN, f32)
    step = pl.program_id(0)

    @pl.when(step == 0)
    def _():
        acc_ref[...] = y_ref[...] + vec_ref[7:8, :]

    at = 0
    total = acc_ref[...]
    for gelu, count, w_ref in zip(gelus, counts, w_refs):
        gather_rows(who, shards[at : at + count], w_ref)
        total += dot(gelu[...], w_ref[...], NT)
        at += count
    acc_ref[...] = total

    @pl.when(step == pl.num_programs(0) - 1)
    def _():
        for item in range(out_ref.shape[0]):
            out_ref[item] = acc_ref[item * PAD : (item + 1) * PAD, :].astype(bf16)[:SEQ]


def finish(who, y, gelus, downs, vecs, after):
    rows, width = y.shape
    step = BLOCK
    out = far_mem((rows // PAD, SEQ, width), bf16)
    views = [shard_specs([(v, at * BLOCK // step) for v, at in down], step, lambda i: i) for down in downs]
    return call(
        functools.partial(finish_body, [len(down) for down in downs]),
        (gelus[0].shape[1] // step,),
        [SM] + wholes(y, vecs)
        + [pl.BlockSpec((rows, step), lambda i: (0, i)) for _ in gelus]
        + [spec for specs, _ in views for spec in specs],
        [(out, whole(out.shape)), (jax.ShapeDtypeStruct(TOKEN, f32), whole(TOKEN))],
        [pltpu.VMEM((rows, width), f32)] + [pltpu.VMEM((width, step), bf16)] * len(gelus),
        32,
        (who, afar(y), vecs, *[afar(g) for g in gelus], *[v for _, arrays in views for v in arrays]),
        "finish",
        after,
    )


def swap(value, axis, bit):
    size = lax.axis_size(axis)
    return lax.ppermute(value, axis, [(i, i ^ (1 << bit)) for i in range(size)])


def half_of(value, which, dim):
    size = value.shape[dim] // 2
    return lax.dynamic_slice_in_dim(value, which * size, size, dim)


def plus(*arrays):
    return functools.reduce(lambda a, b: a + b, (v.astype(f32) for v in arrays))


TOKEN = (8, 128)


def step_call(body, ins, shapes, name, after):
    outs = [(near_mem(shape, dtype), VM) for shape, dtype in shapes]
    outs.append((near_mem(TOKEN, f32), VM))
    return call(body, None, [VM] * len(ins), outs, [], 8, [near(v) for v in ins], name, after, flops=10**4)


def paired(counts, refs):
    at = 0
    for count in counts:
        got = [ref[...] for ref in refs[at + 1 : at + 1 + count]]
        yield refs[at], got[0] if count == 1 else jnp.concatenate(got, axis=0)
        at += 1 + count


def first_body(counts, *refs):
    out = refs[-1]
    half = out.shape[1]
    for one, (keep, got) in enumerate(paired(counts, refs[:-1])):
        out[one] = plus(keep[half:], got[half:]).astype(bf16)


def second_body(counts, *refs):
    back, send, mine = refs[-3:]
    half = send.shape[1]
    for one, (keep, got) in enumerate(paired(counts, refs[:-3])):
        mine[one] = plus(keep[:half], got[:half], back[one, :half])
        send[one] = plus(keep[half : 2 * half], got[half : 2 * half], back[one, half:]).astype(bf16)


def third_body(keep, got, send, mine):
    half = send.shape[1]
    mine[...] = plus(keep[:, :half], got[:, :half])
    send[...] = plus(keep[:, half:], got[:, half:]).astype(bf16)


def add_body(one, two, out):
    out[...] = plus(one[...], two[...]).astype(out.dtype)


def join_body(mine, got, out):
    half = mine.shape[1]
    out[:, :half] = mine[...]
    out[:, half:] = got[...]


def cross(value, swapped):
    size, shards = lax.axis_size("dp") * lax.axis_size("fsdp"), lax.axis_size("fsdp")
    flip = lambda i: 2 if (i & 1) == swapped else shards
    return lax.ppermute(value, ("dp", "fsdp"), [(i, i ^ flip(i)) for i in range(size)])


def slot(tasks, *after):
    counts = [(len(ins), len(shapes)) for _, _, ins, shapes in tasks]

    def body(*refs):
        at, to = 0, sum(n for n, _ in counts)
        for (_, step, _, _), (n, m) in zip(tasks, counts):
            step(*refs[at : at + n], *refs[to : to + m])
            at, to = at + n, to + m
        refs[-1][...] = jnp.zeros(TOKEN, f32)

    ins = [v for task in tasks for v in task[2]]
    shapes = [v for task in tasks for v in task[3]]
    *results, token = step_call(body, ins, shapes, "slot", after)
    done = [token]
    for (owner, _, _, _), (_, m) in zip(tasks, counts):
        owner.out, *rest = results[:m]
        owner.mine = rest[0] if rest else owner.out
        results = results[m:]
    return done


class Chunk:
    def __init__(self, keeps, sends):
        self.counts = [len(s) for s in sends]
        self.pairs = [w for k, s in zip(keeps, sends) for w in (k, *[swap(v, "fsdp", 0) for v in s])]
        self.shape = (len(keeps), keeps[0].shape[0], keeps[0].shape[1])

    def task(self, body, ins, outs):
        count, rows, cols = self.shape
        return self, body, ins, [((count, rows // parts, cols), dtype) for parts, dtype in outs]

    def first(self):
        return self.task(functools.partial(first_body, self.counts), self.pairs, [(2, bf16)])

    def second(self):
        return self.task(functools.partial(second_body, self.counts), [*self.pairs, cross(self.out, 0)], [(4, bf16), (4, f32)])

    def third(self):
        return self.task(third_body, [self.mine, cross(self.out, 1)], [(8, bf16), (8, f32)])

    def rest(self):
        return self.task(add_body, [self.mine, swap(self.out, "dp", 1)], [(8, bf16)])

    def part(self):
        last = lax.axis_size("dp").bit_length() - 2
        for bit in range(2, last):
            slot([self.task(add_body, [self.out, swap(self.out, "dp", bit)], [(8, bf16)])])
        return self.task(add_body, [self.out, swap(self.out, "dp", last)], [(8, bf16)])

    def half(self):
        return self.task(join_body, [self.out, swap(self.out, "dp", 1)], [(4, bf16)])

    def halves(self):
        return self.out, swap(self.out, "dp", 0)


class Rows:
    def __init__(self, value):
        self.out = value
        bits = lambda axis: range(lax.axis_size(axis).bit_length() - 1)
        steps = [(axis, bit) for axis in ("fsdp", "dp") for bit in bits(axis)]
        self.left = [("dp", 0)] + [step for step in steps if step != ("dp", 0)]

    def pair(self):
        axis, bit = self.left.pop(0)
        return [self.out, swap(self.out, axis, bit)]

    def step(self):
        return self, add_body, self.pair(), [(self.out.shape, f32)]

    def last(self):
        while len(self.left) > 1:
            slot([self.step()])
        return self.pair()


def adam_body(count, who, mine, got, *rest):
    ins, outs = rest[: 3 * count], rest[-4 * count :]
    half = mine.shape[1] // 2
    low, mid = who[1] == 0, who[2] == 0
    for one in range(count):
        first, second, weight = ins[3 * one : 3 * one + 3]
        first_new, second_new, update, sums = outs[4 * one : 4 * one + 4]
        rows = []
        for ref in (mine, got):
            a, b = ref[one, :half].astype(f32), ref[one, half:].astype(f32)
            rows.append((jnp.where(mid, a, b), jnp.where(mid, b, a)))
        near_rows, other_rows = rows
        grad = [jnp.where(low, a, b) for a, b in zip(near_rows, other_rows)]
        grad += [jnp.where(low, b, a) for a, b in zip(near_rows, other_rows)]
        moved = adam_moments(jnp.concatenate(grad, axis=0), first[...], second[...])
        master = weight[...]
        first_new[...], second_new[...] = moved[0], moved[1]
        change = moved[2] + decay_rate * master
        update[...] = change

        @pl.when(pl.program_id(0) == 0)
        def _(sums=sums):
            sums[...] = jnp.zeros_like(sums)

        sums[0:1, :] += jnp.sum(master * master, axis=0, keepdims=True)
        sums[1:2, :] += jnp.sum(change * change, axis=0, keepdims=True)


def adam(who, halves, matrices, wide, steps, columns, made, after, grad_at=None):
    count, rows = len(matrices), halves[0].shape[1]
    grad = pl.BlockSpec((count, rows, wide), grad_at or (lambda i: (0, 0, i)))
    ins, outs, args, extra, aliases = [SM, grad, grad], [], [who, *halves], [], {}
    for one, matrix in enumerate(matrices):
        block = pl.BlockSpec((matrix[2].shape[0], wide), lambda i, at=columns[one]: (0, at(i)))
        full = (jax.ShapeDtypeStruct(matrix[2].shape, f32), block)
        ins += [block] * 3
        args += matrix
        outs += [full] * 3 + [(jax.ShapeDtypeStruct((2, wide), f32), whole((2, wide)))]
        if made[one] is not None:
            extra += [(4 * one + k, v) for k, v in enumerate(made[one][:3])]
    for out, value in extra:
        aliases[len(ins)] = out
        ins.append(pl.BlockSpec(memory_space=pl.ANY))
        args.append(value)
    got = call(functools.partial(adam_body, count), (steps,), ins, outs, [], 32, tuple(args), "adam", after, aliases)
    return [got[4 * one : 4 * one + 4] for one in range(count)]


def total_body(*refs):
    *parts, out = refs
    for row, group in enumerate(parts_of(parts)):
        for kind in range(2):
            value = sum(jnp.sum(ref[kind : kind + 1, :]) for ref in group)
            out[4 * kind + row : 4 * kind + row + 1, :] = jnp.full((1, out.shape[1]), value, f32)


def parts_of(parts):
    return parts[0:2], parts[2:3], parts[3:5], parts[5:7]


def totals(sums):
    out = jax.ShapeDtypeStruct((8, 128), f32)
    return call(total_body, None, [VM] * len(sums), [(out, VM)], [], 8, tuple(sums), "totals")[0]


def apply_body(one, two, w0, w1, w2, w3, u0, u1, u2, u3, n0, n1, n2, n3, norms):
    total = one[...] + two[...]
    for row in range(4):
        for kind in range(2):
            norms[kind : kind + 1, row : row + 1] = jnp.sqrt(total[4 * kind + row : 4 * kind + row + 1, :1])
    for row, (w, u, n) in enumerate(((w0, u0, n0), (w1, u1, n1), (w2, u2, n2), (w3, u3, n3))):
        ratio = jnp.sqrt(total[row : row + 1, :1]) * lax.rsqrt(total[4 + row : 5 + row, :1] + adam_eps)
        n[...] = w[...] - (matrix_rate * ratio) * u[...]


def apply(one, two, weights, updates):
    steps = 3
    blocks = [pl.BlockSpec((w.shape[0], w.shape[1] // steps), lambda i: (0, i)) for w in weights]
    norms = jax.ShapeDtypeStruct((2, 4), f32)
    return call(
        apply_body,
        (steps,),
        [whole(one.shape)] * 2 + blocks + blocks,
        [(jax.ShapeDtypeStruct(w.shape, f32), b) for w, b in zip(weights, blocks)] + [(norms, whole(norms.shape))],
        [],
        24,
        (one, two, *weights, *updates),
        "apply",
    )


def vector_body(who, one, two, first, second, params, new, first_new, second_new):
    rows, cols = params.shape
    total = one[...] + two[...]
    grad = total[:rows, :cols]
    for block in range(1, 4):
        grad = jnp.where(who[0] == block, total[:rows, block * cols : (block + 1) * cols], grad)
    moved = adam_moments(grad, first[...], second[...])
    first_new[...], second_new[...] = moved[0], moved[1]
    new[...] = params[...] - vector_rate * moved[2]


def vector_step(who, one, two, first, second, params):
    out = jax.ShapeDtypeStruct(params.shape, f32)
    args = (who, one, two, first, second, params)
    return call(vector_body, None, [SM] + [VM] * 5, [(out, VM)] * 3, [], 8, args, "vector_step")


def adam_moments(grad, first, second):
    first_new = beta_one * first + (1.0 - beta_one) * grad
    second_new = beta_two * second + (1.0 - beta_two) * grad * grad
    direction = (
        first_new
        / (1.0 - beta_one**STEP)
        / (jnp.sqrt(second_new / (1.0 - beta_two**STEP)) + adam_eps)
    )
    return (first_new, second_new, direction)


def local(
    block_in,
    out_grad,
    caption_len,
    mask_marks,
    qkv_weight,
    out_weight,
    up_weight,
    down_weight,
    vector_params,
    qkv_first,
    qkv_second,
    out_first,
    out_second,
    up_first,
    up_second,
    down_first,
    down_second,
    vector_first,
    vector_second,
):
    width = block_in.shape[2]
    hidden = up_weight.shape[1]
    groups = width // (GROUP * HEAD)
    shard = lax.axis_index("fsdp")
    replica = lax.axis_index("dp")
    who = jnp.stack([shard, replica & 1, (replica >> 1) & 1]).astype(jnp.int32)
    cols = hidden // PARTS
    core = lambda v: swap(v, "fsdp", 0)
    far = lambda v: swap(v, "fsdp", 1)
    turned = lambda v: v.T

    own_one = cast_heads(qkv_weight, 0, 1, [vector_params], [])
    own_more = cast_heads(qkv_weight, 1, groups - 1, [], [own_one])
    far_one, far_more = far(own_one), far(own_more)
    own_out, half_up, half_down, *own_parts = cast_rest(who, out_weight.T, up_weight, down_weight.T, [own_more])
    dm, dmt, grad_bd = prep_grad(who, out_grad, [own_out])
    far_one = tie(far_one, dm)
    far_up, far_down, far_part = (far(v) for v in (half_up, half_down, own_parts[2]))
    core_parts = [core(v) for v in own_parts]
    first_block = lambda *arrays: [(v, 0) for v in arrays]
    one_shards = (own_one, core(own_one), far_one, core(far_one))

    marks = mask_marks.reshape(*mask_marks.shape, 1)
    vecs, xb, a = prep(who, caption_len, block_in, marks, one_shards, [])
    far_more = tie(far_more, xb)
    more_shards = (own_more, core(own_more), far_more, core(far_more))
    heads_full = [first_block(*one_shards)] + [[(v, g) for v in more_shards] for g in range(groups - 1)]
    sides = lambda mine: (mine, swap(mine, "dp", 0))
    heads = [attend(who, caption_len, a, heads_full[0], vecs, 0, [far_more])]
    own_out = tie(own_out, heads[0][0])
    up_far = sides(tie(far_up, heads[0][0]))
    heads.append(attend(who, caption_len, a, heads_full[1], vecs, 1, [heads[0][0], up_far[0]]))
    down_far = sides(tie(far_down, heads[1][0]))
    heads.append(attend(who, caption_len, a, heads_full[2], vecs, 2, [heads[1][0], down_far[0], up_far[1]]))
    far_out = far(own_out)
    out_full = first_block(own_out, core(own_out), far_out, core(far_out))
    outs = [h[1] for h in heads]
    y, c, ct = mix(who, xb, outs, out_full, vecs, [down_far[1]])
    ups = first_block(own_parts[0], core_parts[0], *up_far, *(core(v) for v in up_far))
    downs = first_block(own_parts[1], core_parts[1], *down_far, *(core(v) for v in down_far))
    ffn0 = ffn(who, c, dm, ct, dmt, ups, downs, vecs, 0, [])
    chunk_a = Chunk([ffn0[0], ffn0[2]], [[ffn0[1]], [ffn0[3]]])
    at = turn_rows(who, a, [afar(ffn0[4])])
    done = slot([chunk_a.first()], at)
    far_part = tie(far_part, ffn0[4])
    shards1 = (own_parts[2], core_parts[2], far_part, core(far_part))
    ups1 = first_block(*shards1)
    downs1 = [(v, cols // BLOCK) for v in shards1]
    ffn1 = ffn(who, c, dm, ct, dmt, ups1, downs1, vecs, 1, done)
    chunk_b = Chunk([ffn1[0], ffn1[2]], [[ffn1[1]], [ffn1[3]]])
    done = slot([chunk_a.second()], afar(ffn1[5]))
    done = slot([chunk_b.first()], *done)
    dy, out_keep, out_send, *dos, grad_mid = turn(who, [ffn0[6], ffn1[6]], y, dm, outs, out_full, vecs, done)
    done = slot([chunk_a.third()], grad_mid)
    back0 = attend_back(caption_len, heads[0][0], dos[0], heads[0][2], at, 1, done)
    chunk_c = Chunk([out_keep, back0[1]], [[out_send], back0[3:]])
    done = slot([chunk_b.second(), chunk_a.rest()], back0[2])
    back1 = attend_back(caption_len, heads[1][0], dos[1], heads[1][2], at, 1, done)
    done = slot([chunk_b.third(), chunk_c.first()], back1[2])
    back2 = attend_back(caption_len, heads[2][0], dos[2], heads[2][2], at, 3, done)
    backs = [back0, back1, back2]
    chunk_d = Chunk([back1[1], back2[1]], [back1[3:], back2[3:]])
    done = slot([chunk_b.rest(), chunk_a.part(), chunk_c.second()], back2[2])
    done = slot([chunk_d.first()], *done)
    sums = [b[2] for b in backs] + [grad_mid] + [afar(v) for v in (grad_bd, ffn0[5], ffn1[5])]
    input_grad, vector_grads = start_back(
        who, caption_len, [b[0] for b in backs], heads_full, xb, dy, marks, vecs, sums, done
    )
    rows = Rows(vector_grads)
    done = slot([chunk_b.part(), chunk_a.half(), chunk_c.third(), chunk_d.second()], vector_grads)
    block_out, token = finish(who, y, [ffn0[4], ffn1[4]], [downs, downs1], vecs, done)

    qkv = (qkv_first, qkv_second, qkv_weight)
    out = tuple(turned(v) for v in (out_first, out_second, out_weight))
    up = (up_first, up_second, up_weight)
    down = tuple(turned(v) for v in (down_first, down_second, down_weight))
    wide = 3 * TILE
    per = cols // wide
    done = slot([chunk_b.half(), chunk_c.rest(), chunk_d.third(), rows.step()], token)
    column = lambda first, step: lambda i: first + step * i
    second = lambda i: (1, 0, i)
    halves_a = chunk_a.halves()
    (up0,) = adam(who, halves_a, [up], wide, per, [column(0, 1)], [None], done)
    done = slot([chunk_d.rest(), rows.step()], up0[3])
    (down0,) = adam(who, halves_a, [down], wide, per, [column(0, 1)], [None], done, second)
    done = slot([chunk_c.part(), rows.step()], down0[3])
    halves_b = chunk_b.halves()
    (up1,) = adam(who, halves_b, [up], wide, per, [column(per, 1)], [up0], done)
    done = slot([chunk_c.half(), chunk_d.part()], up1[3])
    (down1,) = adam(who, halves_b, [down], wide, per, [column(per, 1)], [down0], done, second)
    done = slot([chunk_d.half(), rows.step()], down1[3])
    outer, qkv0 = adam(
        who, chunk_c.halves(), [out, qkv], TILE, 3, [column(0, 1), column(0, groups)], [None] * 2, done
    )
    vector_one, got = rows.last()
    columns = [lambda i: groups * (i % 3) + 1 + i // 3]
    steps = 3 * (groups - 1)
    (qkv1,) = adam(who, chunk_d.halves(), [qkv], TILE, steps, columns, [qkv0], [qkv0[3]], lambda i: (i // 3, 0, i % 3))
    vector_new, vector_first_new, vector_second_new = vector_step(
        who, vector_one, got, vector_first, vector_second, vector_params
    )
    squares = totals([qkv0[3], qkv1[3], outer[3], up0[3], up1[3], down0[3], down1[3]])
    squares = squares + core(squares)
    weights = (qkv_weight, out[2], up_weight, down[2])
    made = (qkv1, outer, up1, down1)
    *new_weights, norms = apply(squares, far(squares), weights, [m[2] for m in made])
    back = (lambda v: v, turned, lambda v: v, turned)
    moments = [f(m[k]) for f, m in zip(back, made) for k in range(2)]
    return (
        block_out,
        input_grad,
        *(f(w) for f, w in zip(back, new_weights)),
        vector_new,
        *moments,
        vector_first_new,
        vector_second_new,
        norms,
    )


def solution(mesh):
    placed = (
        P(("dp", "fsdp"), None, None),
        P(("dp", "fsdp"), None, None),
        P(("dp", "fsdp")),
        P(("dp", "fsdp"), None),
        P("fsdp", None),
        P(None, "fsdp"),
        P("fsdp", None),
        P(None, "fsdp"),
        P(None, "fsdp"),
        P("fsdp", None),
        P("fsdp", None),
        P(None, "fsdp"),
        P(None, "fsdp"),
        P("fsdp", None),
        P("fsdp", None),
        P(None, "fsdp"),
        P(None, "fsdp"),
        P(None, "fsdp"),
        P(None, "fsdp"),
    )
    return jax.shard_map(
        local,
        mesh=mesh,
        in_specs=placed,
        out_specs=(
            P(("dp", "fsdp"), None, None),
            P(("dp", "fsdp"), None, None),
            P("fsdp", None),
            P(None, "fsdp"),
            P("fsdp", None),
            P(None, "fsdp"),
            P(None, "fsdp"),
            P("fsdp", None),
            P("fsdp", None),
            P(None, "fsdp"),
            P(None, "fsdp"),
            P("fsdp", None),
            P("fsdp", None),
            P(None, "fsdp"),
            P(None, "fsdp"),
            P(None, "fsdp"),
            P(None, "fsdp"),
            P(),
        ),
        check_vma=False,
    )
```
